512 devices in a mesh: slab: 4 (over x_lo, core), mapx: 16 (over z), mapy: 8 (over y, x_hi).
Axes of the slice: x: 4 (x_hi: 2, x_lo: 2; x = x_hi * 2 + x_lo), y: 4, z: 16, core: 2. Of those that a mesh axis runs over, the one named last changes fastest.
Arguments:
- pressure: float32 [32, 1536, 2048], P('slab', 'mapx', 'mapy'), may hold values from -2 to 2
- porosity: float32 [32, 1536, 2048], P('slab', 'mapx', 'mapy'), may hold values from 0.1 to 0.5
- lithology: int32 [32, 1536, 2048], P('slab', 'mapx', 'mapy'), may hold values from 0 to 3
- layer_solid: float32 [32], P('slab'), may hold values from 0.05 to 0.15
Outputs:
- pressure_new: float32 [32, 1536, 2048], P('slab', 'mapx', 'mapy')
- porosity_new: float32 [32, 1536, 2048], P('slab', 'mapx', 'mapy')
- thickness_new: float32 [32, 1536, 2048], P('slab', 'mapx', 'mapy')
The draws below stay inside these ranges and needn't reach their ends.
All inputs are finite; a program needn't handle non-finite values.
Results may differ from the reference program's by a relative error of at most 0.00015.
Values sent between devices are 32-bit elements; how exact they have to be, the bound alone decides.
No kernel may reach another device: no remote copies, remote signals or barrier semaphores. Data moves between devices by JAX's collectives and lax.ppermute only.
A program may use at most 64 MiB of HBM per device.

```python
import jax
import jax.numpy as jnp

NCLASS = 4
NZ = 32
NX = 1536
NY = 2048


def plant(entries, stream_key, least, top_value):
    extent = entries.shape
    index_at = [jax.random.randint(jax.random.fold_in(stream_key, axis), (), 0, extent[axis]) for axis in range(len(extent))]
    entries = entries.at[tuple(index_at)].set(least)
    longest = extent.index(max(extent))
    index_at[longest] = (index_at[longest] + 1) % extent[longest]
    return entries.at[tuple(index_at)].set(top_value)


def block_scale(key, dims, cuts, least, top_value):
    loudness = 1.0
    for dim, blocks in cuts:
        heights = jax.random.uniform(jax.random.fold_in(jax.random.fold_in(key, 6), dim), (blocks,), jnp.float32, least / len(cuts), top_value / len(cuts))
        loudness = loudness * jnp.repeat(jnp.exp(heights), dims[dim] // blocks).reshape((-1,) + (1,) * (len(dims) - 1 - dim))
    return loudness


def gaussian(key, shape, width, reach, cuts=(), kind=jnp.bfloat16):
    loudness = block_scale(key, shape, cuts, -0.22, 0.18) if cuts else 1.0
    array = jax.random.normal(key, shape, jnp.float32) * width * loudness
    return jnp.minimum(jnp.maximum(array, -reach), reach).astype(kind)


def setup_inputs(seed: int = 0) -> dict:
    streams_of = jax.random.split(jax.random.key(seed), 5)
    pressure = gaussian(streams_of[0], (NZ, NX, NY), 0.4, 2.0, ((0, 4), (1, 16), (2, 8)), jnp.float32)
    porosity = jnp.clip(0.1 + 0.4 * jax.random.uniform(streams_of[1], (NZ, NX, NY), jnp.float32) ** block_scale(streams_of[1], (NZ, NX, NY), ((0, 4), (1, 16), (2, 8)), -0.2, 0.2), 0.1, 0.5)
    lithology = plant(jax.random.randint(streams_of[2], (NZ, NX, NY), 0, NCLASS), jax.random.fold_in(streams_of[2], 1), 0, NCLASS - 1).astype(jnp.int32)
    layer_solid = jnp.clip(0.05 + 0.10000001 * jax.random.uniform(streams_of[3], (NZ,), jnp.float32) ** block_scale(streams_of[3], (NZ,), ((0, 4),), -0.2, 0.2), 0.05, 0.15)
    return {"pressure": pressure, "porosity": porosity, "lithology": lithology, "layer_solid": layer_solid}


PHI_SURFACE = (0.45, 0.55, 0.65, 0.40)
ATHY_RATE = (0.25, 0.45, 0.8, 0.35)
MOB_BASE = (1.0, 0.0, -1.5, -0.5)
MOB_SLOPE = (6.0, 5.0, 8.0, 4.0)
GRAIN_DENSITY = (2.65, 2.68, 2.72, 2.71)
WATER_DENSITY = 1.03
SPECTRUM_MID = 1.0
SPECTRUM_HALF = 0.95
SIGMA_RATIO = SPECTRUM_MID / SPECTRUM_HALF
RHO_FIRST = 1.0 / SIGMA_RATIO
RHO_SECOND = 1.0 / (2.0 * SIGMA_RATIO - RHO_FIRST)


def lookup(lithology, table):
    result = jnp.zeros(lithology.shape, jnp.float32)
    for index, entry in enumerate(table):
        result = result + jnp.where(lithology == index, jnp.float32(entry), jnp.float32(0.0))
    return result


def neighbours(padded):
    return [padded[2:, 1:-1, 1:-1], padded[:-2, 1:-1, 1:-1],
            padded[1:-1, 2:, 1:-1], padded[1:-1, :-2, 1:-1],
            padded[1:-1, 1:-1, 2:], padded[1:-1, 1:-1, :-2]]


def apply_operator(trans, field):
    result = field
    for weight, beside in zip(trans, neighbours(jnp.pad(field, 1))):
        result = result + weight * (field - beside)
    return result


def reference(pressure, porosity, lithology, layer_solid):
    mobility = jnp.exp(lookup(lithology, MOB_BASE) + lookup(lithology, MOB_SLOPE) * (porosity - 0.35))
    trans = [2.0 * mobility * other / (mobility + other) for other in neighbours(jnp.pad(mobility, 1))]
    diag = 1.0 + trans[0] + trans[1] + trans[2] + trans[3] + trans[4] + trans[5]
    first_res = pressure - apply_operator(trans, pressure)
    first_step = first_res / (SPECTRUM_MID * diag)
    middle = pressure + first_step
    second_res = pressure - apply_operator(trans, middle)
    second_step = RHO_SECOND * RHO_FIRST * first_step + (2.0 * RHO_SECOND / SPECTRUM_HALF) * second_res / diag
    pressure_new = middle + second_step
    solid = layer_solid[:, None, None]
    load = (lookup(lithology, GRAIN_DENSITY) + WATER_DENSITY * porosity / (1.0 - porosity)) * solid
    overburden = jnp.cumsum(load, axis=0) - 0.5 * load
    stress = jnp.maximum(overburden - pressure_new, 0.0)
    porosity_new = lookup(lithology, PHI_SURFACE) * jnp.exp(-lookup(lithology, ATHY_RATE) * stress)
    thickness_new = solid / (1.0 - porosity_new)
    return pressure_new, porosity_new, thickness_new
```

```python
import math

import jax
import jax.numpy as jnp
from jax import lax
from jax.experimental import pallas as pl
from jax.experimental.pallas import tpu as pltpu
from jax.sharding import PartitionSpec as P

PHI_SURFACE = (0.45, 0.55, 0.65, 0.4)
ATHY_RATE = (0.25, 0.45, 0.8, 0.35)
MOB_BASE = (1.0, 0.0, -1.5, -0.5)
MOB_SLOPE = (6.0, 5.0, 8.0, 4.0)
GRAIN_DENSITY = (2.65, 2.68, 2.72, 2.71)
WATER_DENSITY = 1.03
SPECTRUM_MID = 1.0
SPECTRUM_HALF = 0.95
SIGMA_RATIO = SPECTRUM_MID / SPECTRUM_HALF
RHO_FIRST = 1.0 / SIGMA_RATIO
RHO_SECOND = 1.0 / (2.0 * SIGMA_RATIO - RHO_FIRST)

H_BASE = tuple(math.log(0.5) - b + 0.35 * s for b, s in zip(MOB_BASE, MOB_SLOPE))
H_SLOPE = tuple(-s for s in MOB_SLOPE)
ABSENT = 1e38

F32 = jnp.float32
L, R, C = 8, 96, 256
GR = 32
VMEM_LIMIT = 40 * 1024 * 1024


def recip(x):
    r = pl.reciprocal(x, approx=True)
    return r * (2.0 - x * r)


def present(h):
    return jnp.where(h == 0.0, ABSENT, h)


def classes(lith):
    return (lith & 1) == 1, lith >= 2


def pick(odd, upper, t):
    return jnp.where(upper, jnp.where(odd, t[3], t[2]), jnp.where(odd, t[1], t[0]))


def iota(shape, dim):
    return lax.broadcasted_iota(jnp.int32, shape, dim)


def roll(x, shift, axis):
    return pltpu.roll(x, shift % x.shape[axis], axis)


def start_kernel(par, solid, p, poro, lith, h, over, first, second):
    def chunk(i, carry):
        rows = pl.ds(pl.multiple_of(i * 32, 32), 32)
        total = jnp.zeros((32, C), F32)
        for z in range(L):
            odd, upper = classes(lith[z, rows, :])
            phi = poro[z, rows, :]
            h[z, rows, :] = jnp.exp(pick(odd, upper, H_BASE) + pick(odd, upper, H_SLOPE) * phi)
            load = (pick(odd, upper, GRAIN_DENSITY) + WATER_DENSITY * phi * recip(1.0 - phi)) * solid[z]
            over[z, rows, :] = total + 0.5 * load
            total = total + load
        first[pl.ds(pl.multiple_of(4 * R + i * 32, 32), 32), :] = total
        return carry

    lax.fori_loop(0, R // 32, chunk, 0)
    is_odd = par[0] == 1
    for ref, o, i in (
        (first, jnp.where(is_odd, 0, L - 1), jnp.where(is_odd, 1, L - 2)),
        (second, jnp.where(is_odd, L - 1, 0), jnp.where(is_odd, L - 2, 1)),
    ):
        ref[0:R, :] = h[o]
        ref[R : 2 * R, :] = p[o]
        ref[2 * R : 3 * R, :] = h[i]
        ref[3 * R : 4 * R, :] = p[i]


def pack_y_kernel(par, h, p, first, second, lo, hi):
    is_odd = par[0] == 1
    lane = iota((GR, 128), 1)

    def plane(arr, z, g, cols):
        rows = slice(GR * g, GR * g + GR)
        if 0 <= z < L:
            return (h, p)[arr][z, rows, cols]
        at = slice(R * arr + GR * g, R * arr + GR * g + GR)
        a, b = first[at, cols], second[at, cols]
        return jnp.where(is_odd, a, b) if z < 0 else jnp.where(is_odd, b, a)

    acc_lo = jnp.zeros((GR, 128), F32)
    acc_hi = jnp.zeros((GR, 128), F32)
    for g in range(3):
        for z in range(-1, L + 1):
            for arr in range(2):
                base = 40 * g + 4 * (z + 1) + 2 * arr
                here = (lane >= base) & (lane < base + 2)
                acc_lo = jnp.where(here, roll(plane(arr, z, g, slice(0, 128)), base, 1), acc_lo)
                acc_hi = jnp.where(here, roll(plane(arr, z, g, slice(C - 128, C)), base + 2, 1), acc_hi)
    lo[...] = acc_lo
    hi[...] = acc_hi


def pack_x_kernel(par, h, p, first, second, ylo, yhi, lo, hi):
    is_odd = par[0] == 1
    for ref, o, i, yrow in ((lo, 0, 1, 0), (hi, R - 1, R - 2, GR - 1)):
        for arr, own in ((0, h), (1, p)):
            at = slice(R * arr + o, R * arr + o + 1)
            a, b = first[at, :], second[at, :]
            top = 10 * arr
            ref[top : top + 1, :] = jnp.where(is_odd, a, b)
            for z in range(L):
                ref[top + 1 + z : top + 2 + z, :] = own[z, o : o + 1, :]
                ref[20 + L * arr + z : 21 + L * arr + z, :] = own[z, i : i + 1, :]
            ref[top + 9 : top + 10, :] = jnp.where(is_odd, b, a)
        ref[36:37, 0:128] = ylo[yrow : yrow + 1, :]
        ref[36:37, 128:256] = yhi[yrow : yrow + 1, :]
        ref[37:40, :] = jnp.zeros((3, C), F32)


def step(h, p, beside):
    total, flow = None, None
    weights = []
    for hn, pn in beside:
        t = recip(h + hn)
        weights.append(t)
        total = 1.0 + t if total is None else total + t
        flow = t * (pn - p) if flow is None else flow + t * (pn - p)
    inv = recip(total)
    return p + flow * inv, weights, inv


def main_kernel(
    par, solid, h, p, over, lith, first, second, above,
    ylo, yhi, wlo, whi, xlo, xhi, vlo, vhi,
    p_out, poro_out, thick_out,
    hs, ps, p1s, txl, txh, tyl, tyh, tz, inv,
    xh, xp, xq, yh, yp, yq,
):
    is_odd = par[0] == 1
    for z in range(L):
        hs[z + 2] = h[z]
        ps[z + 2] = p[z]
    for k, zl, zh in ((0, 1, 10), (1, 0, 11)):
        ha, hb = first[2 * k * R : (2 * k + 1) * R, :], second[2 * k * R : (2 * k + 1) * R, :]
        pa, pb = first[(2 * k + 1) * R : (2 * k + 2) * R, :], second[(2 * k + 1) * R : (2 * k + 2) * R, :]
        hs[zl] = present(jnp.where(is_odd, ha, hb))
        hs[zh] = present(jnp.where(is_odd, hb, ha))
        ps[zl] = jnp.where(is_odd, pa, pb)
        ps[zh] = jnp.where(is_odd, pb, pa)

    sub = iota((16, C), 0)
    lane = iota((16, C), 1)
    lane_x = iota((16, 128), 1)
    sub_x = iota((16, 128), 0)
    for s, msg, own, row_lane in ((0, xlo, vlo, 80), (1, xhi, vhi, 0)):
        def rows10(ref, at):
            return jnp.concatenate([ref[at : at + 10, :], jnp.zeros((6, C), F32)], axis=0)

        def rows8(ref, at):
            return jnp.concatenate([jnp.zeros((1, C), F32), ref[at : at + 8, :], jnp.zeros((7, C), F32)], axis=0)

        ho, po = present(rows10(msg, 0)), rows10(msg, 10)
        hi_, pi_ = present(rows8(msg, 20)), rows8(msg, 28)
        hw, pw = present(rows10(own, 0)), rows10(own, 10)

        def corner(cols, k):
            row = jnp.broadcast_to(msg[36:37, cols], (16, 128))
            return jnp.sum(jnp.where(lane_x == row_lane + 4 * sub_x + k, row, 0.0), axis=1, keepdims=True)

        left, right = slice(0, 128), slice(128, 256)
        hl = jnp.where(lane == 0, present(corner(left, 1)), roll(ho, 1, 1))
        pl_ = jnp.where(lane == 0, corner(left, 3), roll(po, 1, 1))
        hr = jnp.where(lane == C - 1, present(corner(right, 0)), roll(ho, -1, 1))
        pr = jnp.where(lane == C - 1, corner(right, 2), roll(po, -1, 1))
        beside = (
            (hi_, pi_), (hw, pw), (hl, pl_), (hr, pr),
            (roll(ho, 1, 0), roll(po, 1, 0)), (roll(ho, -1, 0), roll(po, -1, 0)),
        )
        q, _, _ = step(ho, po, beside)
        xh[s] = ho
        xp[s] = po
        xq[s] = q

    lane = iota((GR, 128), 1)
    sub = iota((GR, 128), 0)
    for s, msg, own, o, i, w, cols in (
        (0, ylo, wlo, 1, 0, 0, slice(0, 128)),
        (1, yhi, whi, 0, 1, 1, slice(128, 256)),
    ):
        m, v = msg[...], own[...]
        ho, po = present(roll(m, -o, 1)), roll(m, -o - 2, 1)
        hi_, pi_ = present(roll(m, -i, 1)), roll(m, -i - 2, 1)
        hw, pw = present(roll(v, -w, 1)), roll(v, -w - 2, 1)

        def along_x(f, k, fix):
            low = jnp.broadcast_to(fix(xlo[36:37, cols]), (GR, 128))
            high = jnp.broadcast_to(fix(xhi[36:37, cols]), (GR, 128))
            u = roll(f, 1, 0)
            u = jnp.where(sub == 0, jnp.where(lane < 40, roll(low, -80 - k, 1), roll(u, 40, 1)), u)
            d = roll(f, -1, 0)
            d = jnp.where(sub == GR - 1, jnp.where(lane >= 80, roll(high, 80 - k, 1), roll(d, -40, 1)), d)
            return u, d

        hu, hd = along_x(ho, o, present)
        pu, pd = along_x(po, o + 2, lambda t: t)
        beside = (
            (hi_, pi_), (hw, pw), (hu, pu), (hd, pd),
            (roll(ho, 4, 1), roll(po, 4, 1)), (roll(ho, -4, 1), roll(po, -4, 1)),
        )
        q, _, _ = step(ho, po, beside)
        yh[s] = ho
        yp[s] = po
        yq[s] = q

    row = iota((R, C), 0)
    col = iota((R, C), 1)

    def column(ref, s, z):
        f = ref[s]
        pieces = [roll(f, 128 - 40 * g - 4 * z, 1)[:, 0:1] for g in range(3)]
        return jnp.concatenate(pieces, axis=0)

    def lateral(f, z, rows_ref, cols_ref):
        up = jnp.where(row == 0, rows_ref[0, pl.ds(z, 1), :], roll(f, 1, 0))
        down = jnp.where(row == R - 1, rows_ref[1, pl.ds(z, 1), :], roll(f, -1, 0))
        left = jnp.where(col == 0, column(cols_ref, 0, z), roll(f, 1, 1))
        right = jnp.where(col == C - 1, column(cols_ref, 1, z), roll(f, -1, 1))
        return up, down, left, right

    def first_step(z, carry):
        hc, pc = hs[z + 1], ps[z + 1]
        hn = lateral(hc, z, xh, yh) + (hs[z], hs[z + 2])
        pn = lateral(pc, z, xp, yp) + (ps[z], ps[z + 2])
        q, weights, d = step(hc, pc, tuple(zip(hn, pn)))
        p1s[z] = q
        for ref, t in zip((txl, txh, tyl, tyh, tz), weights):
            ref[z] = t
        inv[z] = d
        return carry

    lax.fori_loop(0, L + 2, first_step, 0)

    base = above[...] + jnp.where(is_odd, first[4 * R : 5 * R, :], 0.0)

    def second_step(z, carry):
        k = z + 1
        q = p1s[k]
        pc = ps[k + 1]
        up, down, left, right = lateral(q, k, xq, yq)
        flow = txl[k] * (up - q) + txh[k] * (down - q)
        flow = flow + tyl[k] * (left - q) + tyh[k] * (right - q)
        flow = flow + tz[k] * (p1s[k - 1] - q) + tz[k + 1] * (p1s[k + 1] - q)
        d0 = q - pc
        pn = q + RHO_SECOND * RHO_FIRST * d0 + (2.0 * RHO_SECOND / SPECTRUM_HALF) * (flow - d0) * inv[k]
        p_out[z] = pn
        stress = jnp.maximum(base + over[z] - pn, 0.0)
        odd, upper = classes(lith[z])
        new = pick(odd, upper, PHI_SURFACE) * jnp.exp(-pick(odd, upper, ATHY_RATE) * stress)
        poro_out[z] = new
        thick_out[z] = solid[z] * recip(1.0 - new)
        return carry

    lax.fori_loop(0, L, second_step, 0)


def call(kernel, outs, n_smem, n_in, scratch=(), name=None):
    smem = pl.BlockSpec(memory_space=pltpu.SMEM)
    vmem = pl.BlockSpec(memory_space=pltpu.VMEM)
    return pl.pallas_call(
        kernel,
        out_shape=[jax.ShapeDtypeStruct(s, F32) for s in outs],
        in_specs=[smem] * n_smem + [vmem] * n_in,
        out_specs=[vmem] * len(outs),
        scratch_shapes=[pltpu.VMEM(s, F32) for s in scratch],
        compiler_params=pltpu.CompilerParams(vmem_limit_bytes=VMEM_LIMIT),
        name=name,
    )


def pair(axis, lo, hi):
    n = lax.axis_size(axis)
    up = [(i, i + 1) for i in range(n - 1)]
    down = [(j, i) for i, j in up]
    return lax.ppermute(hi, axis, up), lax.ppermute(lo, axis, down)


def body(p, poro, lith, solid):
    par = (lax.axis_index("slab") % 2).astype(jnp.int32).reshape(1)
    block = (L, R, C)
    h, over, first, second = call(
        start_kernel, [block, block, (5 * R, C), (4 * R, C)], 2, 3, name="start"
    )(par, solid, p, poro, lith)
    from_second = lax.ppermute(second, "slab", [(1, 2), (2, 1)])
    from_first = lax.ppermute(first, "slab", [(0, 1), (1, 0), (2, 3), (3, 2)])
    both = first[4 * R :] + from_first[4 * R :]
    above = lax.ppermute(both, "slab", [(1, 2), (0, 3)])
    wlo, whi = call(pack_y_kernel, [(GR, 128)] * 2, 1, 4, name="pack_y")(
        par, h, p, from_first, from_second
    )
    ylo, yhi = pair("mapy", wlo, whi)
    vlo, vhi = call(pack_x_kernel, [(40, C)] * 2, 1, 6, name="pack_x")(
        par, h, p, from_first, from_second, ylo, yhi
    )
    xlo, xhi = pair("mapx", vlo, vhi)
    plane = (10, R, C)
    scratch = [(12, R, C)] * 2 + [plane] * 7 + [(2, 16, C)] * 3 + [(2, GR, 128)] * 3
    return tuple(
        call(main_kernel, [block] * 3, 2, 15, scratch, name="main")(
            par, solid, h, p, over, lith, from_first, from_second, above,
            ylo, yhi, wlo, whi, xlo, xhi, vlo, vhi,
        )
    )


def solution(mesh):
    spec = P("slab", "mapx", "mapy")
    return jax.shard_map(
        body, mesh=mesh, in_specs=(spec, spec, spec, P("slab")), out_specs=(spec,) * 3, check_vma=False
    )
```

```python
import math

import jax
import jax.numpy as jnp
from jax import lax
from jax.experimental import pallas as pl
from jax.experimental.pallas import tpu as pltpu
from jax.sharding import PartitionSpec as P

PHI_SURFACE = (0.45, 0.55, 0.65, 0.4)
ATHY_RATE = (0.25, 0.45, 0.8, 0.35)
MOB_BASE = (1.0, 0.0, -1.5, -0.5)
MOB_SLOPE = (6.0, 5.0, 8.0, 4.0)
GRAIN_DENSITY = (2.65, 2.68, 2.72, 2.71)
WATER_DENSITY = 1.03
SPECTRUM_MID = 1.0
SPECTRUM_HALF = 0.95
SIGMA_RATIO = SPECTRUM_MID / SPECTRUM_HALF
RHO_FIRST = 1.0 / SIGMA_RATIO
RHO_SECOND = 1.0 / (2.0 * SIGMA_RATIO - RHO_FIRST)

H_BASE = tuple(math.log(0.5) - b + 0.35 * s for b, s in zip(MOB_BASE, MOB_SLOPE))
H_SLOPE = tuple(-s for s in MOB_SLOPE)
ABSENT = 1e38

F32 = jnp.float32
L, R, C = 8, 96, 256
GR = 32
VMEM_LIMIT = 40 * 1024 * 1024


def recip(x):
    r = pl.reciprocal(x, approx=True)
    return r * (2.0 - x * r)


def present(h):
    return jnp.where(h == 0.0, ABSENT, h)


def classes(lith):
    return (lith & 1) == 1, lith >= 2


def pick(odd, upper, t):
    return jnp.where(upper, jnp.where(odd, t[3], t[2]), jnp.where(odd, t[1], t[0]))


def iota(shape, dim):
    return lax.broadcasted_iota(jnp.int32, shape, dim)


def roll(x, shift, axis):
    return pltpu.roll(x, shift % x.shape[axis], axis)


def start_kernel(slab, p_in, poro_in, lith_in, solid_in, p, lith, h, over, first, second, poro, solid, sems, solid_sem):
    copies = []
    solid_copy = pltpu.make_async_copy(solid_in, solid, solid_sem)
    solid_copy.start()
    for z in range(L):
        row = []
        for k, (src, dst) in enumerate(((poro_in, poro), (lith_in, lith), (p_in, p))):
            copy = pltpu.make_async_copy(src.at[z], dst.at[z], sems.at[k, z])
            copy.start()
            row.append(copy)
        copies.append(row)
    solid_copy.wait()
    for z in range(L):
        copies[z][0].wait()
        copies[z][1].wait()

        def chunk(i, carry, z=z):
            rows = pl.ds(pl.multiple_of(i * 32, 32), 32)
            at = pl.ds(pl.multiple_of(4 * R + i * 32, 32), 32)
            odd, upper = classes(lith[z, rows, :])
            phi = poro[z, rows, :]
            h[z, rows, :] = jnp.exp(pick(odd, upper, H_BASE) + pick(odd, upper, H_SLOPE) * phi)
            load = (pick(odd, upper, GRAIN_DENSITY) + WATER_DENSITY * phi * recip(1.0 - phi)) * solid[z]
            if z == 0:
                over[z, rows, :] = 0.5 * load
                first[at, :] = load
            else:
                total = first[at, :]
                over[z, rows, :] = total + 0.5 * load
                first[at, :] = total + load
            return carry

        lax.fori_loop(0, R // 32, chunk, 0)
    for z in range(L):
        copies[z][2].wait()
    is_odd = (slab[0] & 1) == 1
    o, i = jnp.where(is_odd, 0, L - 1), jnp.where(is_odd, 1, L - 2)
    first[0:R, :] = h[o]
    first[R : 2 * R, :] = p[o]
    first[2 * R : 3 * R, :] = h[i]
    first[3 * R : 4 * R, :] = p[i]
    o = jnp.where(is_odd, L - 1, 0)
    second[0:R, :] = h[o]
    second[R : 2 * R, :] = p[o]


def pack_y_kernel(slab, h, p, mine, first, second, lo, hi, third):
    is_odd = (slab[0] & 1) == 1
    lane = iota((GR, 128), 1)

    def plane(arr, z, g, cols):
        rows = slice(GR * g, GR * g + GR)
        if 0 <= z < L:
            return (h, p)[arr][z, rows, cols]
        at = slice(R * arr + GR * g, R * arr + GR * g + GR)
        a, b = first[at, cols], second[at, cols]
        return jnp.where(is_odd, a, b) if z < 0 else jnp.where(is_odd, b, a)

    acc_lo = jnp.zeros((GR, 128), F32)
    acc_hi = jnp.zeros((GR, 128), F32)
    for g in range(3):
        for z in range(-1, L + 1):
            for arr in range(2):
                base = 40 * g + 4 * (z + 1) + 2 * arr
                here = (lane >= base) & (lane < base + 2)
                acc_lo = jnp.where(here, roll(plane(arr, z, g, slice(0, 128)), base, 1), acc_lo)
                acc_hi = jnp.where(here, roll(plane(arr, z, g, slice(C - 128, C)), base + 2, 1), acc_hi)
    lo[...] = acc_lo
    hi[...] = acc_hi
    i = jnp.where(is_odd, L - 2, 1)
    third[0:R, :] = h[i]
    third[R : 2 * R, :] = p[i]
    third[2 * R : 3 * R, :] = mine[4 * R : 5 * R, :] + first[4 * R : 5 * R, :]


def pack_x_kernel(slab, h, p, first, second, ylo, yhi, lo, hi):
    is_odd = (slab[0] & 1) == 1
    for ref, o, i, yrow in ((lo, 0, 1, 0), (hi, R - 1, R - 2, GR - 1)):
        for arr, own in ((0, h), (1, p)):
            at = slice(R * arr + o, R * arr + o + 1)
            a, b = first[at, :], second[at, :]
            top = 10 * arr
            ref[top : top + 1, :] = jnp.where(is_odd, a, b)
            for z in range(L):
                ref[top + 1 + z : top + 2 + z, :] = own[z, o : o + 1, :]
                ref[20 + L * arr + z : 21 + L * arr + z, :] = own[z, i : i + 1, :]
            ref[top + 9 : top + 10, :] = jnp.where(is_odd, b, a)
        ref[36:37, 0:128] = ylo[yrow : yrow + 1, :]
        ref[36:37, 128:256] = yhi[yrow : yrow + 1, :]
        ref[37:40, :] = jnp.zeros((3, C), F32)


def step(h, p, beside):
    total, flow = None, None
    for hn, pn in beside:
        t = recip(h + hn)
        total = 1.0 + t if total is None else total + t
        flow = t * (pn - p) if flow is None else flow + t * (pn - p)
    return p + flow * recip(total)


def beside_y(msgs, owns, corners):
    lane = iota((GR, 128), 1)
    sub = iota((GR, 128), 0)
    result = []
    for msg, own, o, i, w, cols in (
        (msgs[0], owns[0], 1, 0, 0, slice(0, 128)),
        (msgs[1], owns[1], 0, 1, 1, slice(128, 256)),
    ):
        m, v = msg[...], own[...]
        ho, po = present(roll(m, -o, 1)), roll(m, -o - 2, 1)
        hi_, pi_ = present(roll(m, -i, 1)), roll(m, -i - 2, 1)
        hw, pw = present(roll(v, -w, 1)), roll(v, -w - 2, 1)

        def along_x(f, k, fix):
            u = roll(f, 1, 0)
            u = jnp.where(sub == 0, roll(u, 40, 1), u)
            d = roll(f, -1, 0)
            d = jnp.where(sub == GR - 1, roll(d, -40, 1), d)
            if corners is not None:
                low = jnp.broadcast_to(fix(corners[0][36:37, cols]), (GR, 128))
                high = jnp.broadcast_to(fix(corners[1][36:37, cols]), (GR, 128))
                u = jnp.where((sub == 0) & (lane < 40), roll(low, -80 - k, 1), u)
                d = jnp.where((sub == GR - 1) & (lane >= 80), roll(high, 80 - k, 1), d)
            return u, d

        hu, hd = along_x(ho, o, present)
        pu, pd = along_x(po, o + 2, lambda t: t)
        q = step(ho, po, (
            (hi_, pi_), (hw, pw), (hu, pu), (hd, pd),
            (roll(ho, 4, 1), roll(po, 4, 1)), (roll(ho, -4, 1), roll(po, -4, 1)),
        ))
        result.append((ho, po, q))
    return result


def beside_x(msgs, owns, xh, xp, xq):
    lane = iota((16, C), 1)
    lane_x = iota((16, 128), 1)
    sub_x = iota((16, 128), 0)
    for s, row_lane in ((0, 80), (1, 0)):
        msg, own = msgs[s], owns[s]

        def rows10(ref, at):
            return jnp.concatenate([ref[at : at + 10, :], jnp.zeros((6, C), F32)], axis=0)

        def rows8(ref, at):
            return jnp.concatenate([jnp.zeros((1, C), F32), ref[at : at + 8, :], jnp.zeros((7, C), F32)], axis=0)

        ho, po = present(rows10(msg, 0)), rows10(msg, 10)
        hi_, pi_ = present(rows8(msg, 20)), rows8(msg, 28)
        hw, pw = present(rows10(own, 0)), rows10(own, 10)

        def corner(cols, k):
            row = jnp.broadcast_to(msg[36:37, cols], (16, 128))
            return jnp.sum(jnp.where(lane_x == row_lane + 4 * sub_x + k, row, 0.0), axis=1, keepdims=True)

        left, right = slice(0, 128), slice(128, 256)
        hl = jnp.where(lane == 0, present(corner(left, 1)), roll(ho, 1, 1))
        pl_ = jnp.where(lane == 0, corner(left, 3), roll(po, 1, 1))
        hr = jnp.where(lane == C - 1, present(corner(right, 0)), roll(ho, -1, 1))
        pr = jnp.where(lane == C - 1, corner(right, 2), roll(po, -1, 1))
        xh[s] = ho
        xp[s] = po
        xq[s] = step(ho, po, (
            (hi_, pi_), (hw, pw), (hl, pl_), (hr, pr),
            (roll(ho, 1, 0), roll(po, 1, 0)), (roll(ho, -1, 0), roll(po, -1, 0)),
        ))


def edge_columns(lo, hi, z, g):
    lane = iota((GR, 128), 1)
    at = 40 * g + 4 * (z + 1)
    return jnp.where(lane == 0, roll(lo, -at, 1), roll(hi, 127 - at, 1))


def around(before, here, after, edge):
    sub = iota((8, C), 0)
    lane = iota((8, 128), 1)
    up = roll(jnp.where(sub == 7, before, here), 1, 0)
    down = roll(jnp.where(sub == 0, after, here), -1, 0)
    a, b = here[:, :128], here[:, 128:]
    ra, rb = roll(a, 1, 1), roll(b, 1, 1)
    left = jnp.concatenate([jnp.where(lane == 0, edge, ra), jnp.where(lane == 0, ra, rb)], axis=1)
    ra, rb = roll(a, -1, 1), roll(b, -1, 1)
    right = jnp.concatenate([jnp.where(lane == 127, rb, ra), jnp.where(lane == 127, edge, rb)], axis=1)
    return up, down, left, right


def first_chunk(hval, pval, hedge, pedge, put):
    hc, pc = hval(-1), pval(-1)
    t = recip(hc[1] + hval(-2)[1])
    flow = t * (pc[1] - pval(-2)[1])
    for z in range(-1, L + 1):
        hn, pn = hval(z + 1), pval(z + 1)
        t2 = recip(hc[1] + hn[1])
        flow2 = t2 * (pn[1] - pc[1])
        h, p = hc[1], pc[1]
        total, change = 1.0 + (t + t2), flow2 - flow
        weights = []
        for hb, pb in zip(around(*hc, hedge(z)), around(*pc, pedge(z))):
            w = recip(h + hb)
            weights.append(w)
            total = total + w
            change = change + w * (pb - p)
        inv = recip(total)
        put(z, p + change * inv, weights, t, inv)
        hc, pc, t, flow = hn, pn, t2, flow2


def second_chunk(qval, qedge, weight, pval, base, over, lith, solid, put):
    low = qval(-1)[1]
    qc = qval(0)
    flow = weight(0, 4) * (qc[1] - low)
    for z in range(L):
        qn = qval(z + 1)
        flow2 = weight(z + 1, 4) * (qn[1] - qc[1])
        q = qc[1]
        change = flow2 - flow
        for k, qb in enumerate(around(*qc, qedge(z))):
            change = change + weight(z, k) * (qb - q)
        d0 = q - pval(z)
        pn = q + RHO_SECOND * RHO_FIRST * d0 + (2.0 * RHO_SECOND / SPECTRUM_HALF) * (change - d0) * weight(z, 5)
        stress = jnp.maximum(base + over(z) - pn, 0.0)
        odd, upper = classes(lith(z))
        new = pick(odd, upper, PHI_SURFACE) * jnp.exp(-pick(odd, upper, ATHY_RATE) * stress)
        put(z, pn, new, solid[z] * recip(1.0 - new))
        qc, flow = qn, flow2


def above_rows(slab, first, third, rows):
    base = jnp.where((slab[0] & 1) == 1, first[rows(4 * R), :], 0.0)
    return base + jnp.where(slab[0] >= 2, third[rows(2 * R), :], 0.0)


def inner_kernel(
    slab, solid, h, p, over, lith, first, second, third, ylo, yhi, wlo, whi,
    hz, pz, eh, ep, p1, out0, out1, out2,
    eq, wt, o0, o1, o2, sems,
):
    is_odd = (slab[0] & 1) == 1
    for k, (a, b) in enumerate(((first, second), (first, third))):
        at = 2 * R * k
        ha, hb = a[at : at + R, :], b[0:R, :]
        pa, pb = a[at + R : at + 2 * R, :], b[R : 2 * R, :]
        hz[2 * k] = present(jnp.where(is_odd, ha, hb))
        hz[2 * k + 1] = present(jnp.where(is_odd, hb, ha))
        pz[2 * k] = jnp.where(is_odd, pa, pb)
        pz[2 * k + 1] = jnp.where(is_odd, pb, pa)
    lo, hi = beside_y((ylo, yhi), (wlo, whi), None)
    for z in range(-1, L + 1):
        for g in range(3):
            rows = slice(GR * g, GR * g + GR)
            eh[z + 1, rows, :] = edge_columns(lo[0], hi[0], z, g)
            ep[z + 1, rows, :] = edge_columns(lo[1], hi[1], z, g)
            if 0 <= z < L:
                eq[z, rows, :] = edge_columns(lo[2], hi[2], z, g)

    def at8(i):
        return pl.ds(pl.multiple_of(8 * i, 8), 8)

    def triple(own, halo, i):
        here = (at8(jnp.maximum(i - 1, 0)), at8(i), at8(jnp.minimum(i + 1, R // 8 - 1)))

        def value(z):
            ref, k = (own, z) if 0 <= z < L else (halo, {-1: 0, L: 1, -2: 2, L + 1: 3}[z])
            return tuple(ref[k, rows, :] for rows in here)

        return value

    def chunk1(i, carry):
        rows = at8(i)

        def put(z, q, weights, t, inv):
            p1[z + 1, rows, :] = q
            if 0 <= z <= L:
                wt[4, z, rows, :] = t
            if 0 <= z < L:
                for k, w in enumerate(weights):
                    wt[k, z, rows, :] = w
                wt[5, z, rows, :] = inv

        first_chunk(
            triple(h, hz, i), triple(p, pz, i),
            lambda z: eh[z + 1, rows, :], lambda z: ep[z + 1, rows, :], put,
        )
        return carry

    lax.fori_loop(0, R // 8, chunk1, 0)

    def chunk2(i, carry):
        rows = at8(i)
        here = (at8(i - 1), rows, at8(i + 1))

        def put(z, a, b, c):
            o0[z, rows, :] = a
            o1[z, rows, :] = b
            o2[z, rows, :] = c

        second_chunk(
            lambda z: tuple(p1[z + 1, r, :] for r in here),
            lambda z: eq[z, rows, :],
            lambda z, k: wt[k, z, rows, :],
            lambda z: p[z, rows, :],
            above_rows(slab, first, third, lambda top: pl.ds(pl.multiple_of(top + 8 * i, 8), 8)),
            lambda z: over[z, rows, :],
            lambda z: lith[z, rows, :],
            solid, put,
        )
        return carry

    lax.fori_loop(1, R // 8 - 1, chunk2, 0)
    rows = pl.ds(8, R - 16)
    copies = [
        pltpu.make_async_copy(src.at[:, rows, :], dst.at[:, rows, :], sems.at[k])
        for k, (src, dst) in enumerate(((o0, out0), (o1, out1), (o2, out2)))
    ]
    for copy in copies:
        copy.start()
    for copy in copies:
        copy.wait()


def outer_kernel(
    slab, solid, h, p, over, lith, first, third, ylo, yhi, wlo, whi, xlo, xhi, vlo, vhi,
    hz, pz, eh, ep, p1, in0, in1, in2,
    out0, out1, out2,
    xh, xp, xq, q1, wt, o0, o1, o2, sems,
):
    beside_x((xlo, xhi), (vlo, vhi), xh, xp, xq)
    lo, hi = beside_y((ylo, yhi), (wlo, whi), (xlo, xhi))
    copies = []
    for s, top, g, part in ((0, 0, 0, slice(0, 8)), (1, R - 8, 2, slice(GR - 8, GR))):
        rows = slice(top, top + 8)
        near = slice(8, 16) if s == 0 else slice(R - 16, R - 8)

        def triple(own, halo, strip, s=s, rows=rows, near=near):
            def value(z):
                ref, k = (own, z) if 0 <= z < L else (halo, {-1: 0, L: 1, -2: 2, L + 1: 3}[z])
                here, inside = ref[k, rows, :], ref[k, near, :]
                if z < -1 or z > L:
                    return here, here, here
                row = jnp.broadcast_to(strip[s, z + 1 : z + 2, :], (8, C))
                return (row, here, inside) if s == 0 else (inside, here, row)

            return value

        def put(z, q, weights, t, inv, s=s):
            q1[s, z + 1] = q
            if 0 <= z <= L:
                wt[s, 4, z] = t
            if 0 <= z < L:
                for k, w in enumerate(weights):
                    wt[s, k, z] = w
                wt[s, 5, z] = inv

        first_chunk(
            triple(h, hz, xh), triple(p, pz, xp),
            lambda z: eh[z + 1, rows, :], lambda z: ep[z + 1, rows, :], put,
        )

        def q_triple(z, s=s, near=near):
            here = q1[s, z + 1]
            if z < 0 or z >= L:
                return here, here, here
            row = jnp.broadcast_to(xq[s, z + 1 : z + 2, :], (8, C))
            inside = p1[z + 1, near, :]
            return (row, here, inside) if s == 0 else (inside, here, row)

        def put2(z, a, b, c, s=s):
            o0[s, z] = a
            o1[s, z] = b
            o2[s, z] = c

        second_chunk(
            q_triple,
            lambda z: edge_columns(lo[2], hi[2], z, g)[part],
            lambda z, k: wt[s, k, z],
            lambda z: p[z, rows, :],
            above_rows(slab, first, third, lambda t: slice(t + top, t + top + 8)),
            lambda z: over[z, rows, :],
            lambda z: lith[z, rows, :],
            solid, put2,
        )
        for k, (src, dst) in enumerate(((o0, out0), (o1, out1), (o2, out2))):
            copy = pltpu.make_async_copy(src.at[s], dst.at[:, rows, :], sems.at[s, k])
            copy.start()
            copies.append(copy)
    for copy in copies:
        copy.wait()


SMEM, VMEM, HBM = pltpu.SMEM, pltpu.VMEM, pltpu.HBM


def call(kernel, name, ins, outs, scratch=(), aliases=None):
    return pl.pallas_call(
        kernel,
        out_shape=[jax.ShapeDtypeStruct(s, t) for s, t, _ in outs],
        in_specs=[pl.BlockSpec(memory_space=m) for m in ins],
        out_specs=[pl.BlockSpec(memory_space=m) for _, _, m in outs],
        scratch_shapes=list(scratch),
        input_output_aliases=aliases or {},
        compiler_params=pltpu.CompilerParams(vmem_limit_bytes=VMEM_LIMIT),
        name=name,
    )


def pair(axis, lo, hi):
    n = lax.axis_size(axis)
    up = [(i, i + 1) for i in range(n - 1)]
    down = [(j, i) for i, j in up]
    return lax.ppermute(hi, axis, up), lax.ppermute(lo, axis, down)


def vm(*shape):
    return (shape, F32, VMEM)


def body(p_in, poro, lith_in, solid):
    p_in, poro, lith_in, solid_in = (pltpu.with_memory_space_constraint(a, HBM) for a in (p_in, poro, lith_in, solid))
    slab = lax.axis_index("slab").astype(jnp.int32).reshape(1)
    block = (L, R, C)
    dma = pltpu.SemaphoreType.DMA
    p, lith, h, over, first, second = call(
        start_kernel, "start", [SMEM] + [HBM] * 4,
        [vm(*block), (block, jnp.int32, VMEM), vm(*block), vm(*block), vm(5 * R, C), vm(2 * R, C)],
        [VMEM(block, F32), SMEM((L,), F32), dma((3, L)), dma(())],
    )(slab, p_in, poro, lith_in, solid_in)
    second_in = lax.ppermute(second, "slab", [(1, 2), (2, 1)])
    first_in = lax.ppermute(first, "slab", [(0, 1), (1, 0), (2, 3), (3, 2)])
    wlo, whi, third = call(
        pack_y_kernel, "pack_y", [SMEM] + [VMEM] * 5, [vm(GR, 128), vm(GR, 128), vm(3 * R, C)]
    )(slab, h, p, first, first_in, second_in)
    ylo, yhi = pair("mapy", wlo, whi)
    third_in = lax.ppermute(third, "slab", [(1, 2), (2, 1), (0, 3)])
    vlo, vhi = call(pack_x_kernel, "pack_x", [SMEM] + [VMEM] * 6, [vm(40, C)] * 2)(
        slab, h, p, first_in, second_in, ylo, yhi
    )
    xlo, xhi = pair("mapx", vlo, vhi)
    hbm = (block, F32, HBM)
    hz, pz, eh, ep, p1, *outs = call(
        inner_kernel, "inner", [SMEM] * 2 + [VMEM] * 11,
        [vm(4, R, C)] * 2 + [vm(L + 2, R, 128)] * 2 + [vm(L + 2, R, C)] + [hbm] * 3,
        [VMEM((L, R, 128), F32), VMEM((6, L + 1, R, C), F32)] + [VMEM(block, F32)] * 3 + [dma((3,))],
    )(slab, solid, h, p, over, lith, first_in, second_in, third_in, ylo, yhi, wlo, whi)
    return tuple(
        call(
            outer_kernel, "outer", [SMEM] * 2 + [VMEM] * 19 + [HBM] * 3, [hbm] * 3,
            [VMEM((2, 16, C), F32)] * 3
            + [VMEM((2, L + 2, 8, C), F32), VMEM((2, 6, L + 1, 8, C), F32)]
            + [VMEM((2, L, 8, C), F32)] * 3 + [dma((2, 3))],
            {21: 0, 22: 1, 23: 2},
        )(
            slab, solid, h, p, over, lith, first_in, third_in, ylo, yhi, wlo, whi, xlo, xhi, vlo, vhi,
            hz, pz, eh, ep, p1, *outs,
        )
    )


def solution(mesh):
    spec = P("slab", "mapx", "mapy")
    return jax.shard_map(
        body, mesh=mesh, in_specs=(spec, spec, spec, P("slab")), out_specs=(spec,) * 3, check_vma=False
    )
```

```python
import math

import jax
import jax.numpy as jnp
from jax import lax
from jax.experimental import pallas as pl
from jax.experimental.pallas import tpu as pltpu
from jax.sharding import PartitionSpec as P

PHI_SURFACE = (0.45, 0.55, 0.65, 0.4)
ATHY_RATE = (0.25, 0.45, 0.8, 0.35)
MOB_BASE = (1.0, 0.0, -1.5, -0.5)
MOB_SLOPE = (6.0, 5.0, 8.0, 4.0)
GRAIN_DENSITY = (2.65, 2.68, 2.72, 2.71)
WATER_DENSITY = 1.03
SPECTRUM_MID = 1.0
SPECTRUM_HALF = 0.95
SIGMA_RATIO = SPECTRUM_MID / SPECTRUM_HALF
RHO_FIRST = 1.0 / SIGMA_RATIO
RHO_SECOND = 1.0 / (2.0 * SIGMA_RATIO - RHO_FIRST)

H_BASE = tuple(math.log(0.5) - b + 0.35 * s for b, s in zip(MOB_BASE, MOB_SLOPE))
H_SLOPE = tuple(-s for s in MOB_SLOPE)
ABSENT = 1e38

F32 = jnp.float32
L, R, C = 8, 96, 256
GR = 32
VMEM_LIMIT = 40 * 1024 * 1024


def recip(x):
    r = pl.reciprocal(x, approx=True)
    return r * (2.0 - x * r)


def present(h):
    return jnp.where(h == 0.0, ABSENT, h)


def classes(lith):
    return (lith & 1) == 1, lith >= 2


def pick(odd, upper, t):
    return jnp.where(upper, jnp.where(odd, t[3], t[2]), jnp.where(odd, t[1], t[0]))


def iota(shape, dim):
    return lax.broadcasted_iota(jnp.int32, shape, dim)


def roll(x, shift, axis):
    return pltpu.roll(x, shift % x.shape[axis], axis)


def start_kernel(slab, p_in, poro_in, lith_in, solid_in, p, lith, h, over, first, second, shade, poro, solid, sems, solid_sem):
    copies = []
    solid_copy = pltpu.make_async_copy(solid_in, solid, solid_sem)
    solid_copy.start()
    for z in range(L):
        row = []
        for k, (src, dst) in enumerate(((poro_in, poro), (lith_in, lith), (p_in, p))):
            copy = pltpu.make_async_copy(src.at[z], dst.at[z], sems.at[k, z])
            copy.start()
            row.append(copy)
        copies.append(row)
    solid_copy.wait()
    for z in range(L):
        shade[z : z + 1, :] = jnp.full((1, C), solid[z], F32)
    for z in range(L):
        copies[z][0].wait()
        copies[z][1].wait()

        def chunk(i, carry, z=z):
            rows = pl.ds(pl.multiple_of(i * 32, 32), 32)
            at = pl.ds(pl.multiple_of(4 * R + i * 32, 32), 32)
            odd, upper = classes(lith[z, rows, :])
            phi = poro[z, rows, :]
            h[z, rows, :] = jnp.exp(pick(odd, upper, H_BASE) + pick(odd, upper, H_SLOPE) * phi)
            load = (pick(odd, upper, GRAIN_DENSITY) + WATER_DENSITY * phi * recip(1.0 - phi)) * solid[z]
            if z == 0:
                over[z, rows, :] = 0.5 * load
                first[at, :] = load
            else:
                total = first[at, :]
                over[z, rows, :] = total + 0.5 * load
                first[at, :] = total + load
            return carry

        lax.fori_loop(0, R // 32, chunk, 0)
    for z in range(L):
        copies[z][2].wait()
    is_odd = (slab[0] & 1) == 1
    o, i = jnp.where(is_odd, 0, L - 1), jnp.where(is_odd, 1, L - 2)
    first[0:R, :] = h[o]
    first[R : 2 * R, :] = p[o]
    first[2 * R : 3 * R, :] = h[i]
    first[3 * R : 4 * R, :] = p[i]
    o, i = jnp.where(is_odd, L - 1, 0), jnp.where(is_odd, L - 2, 1)
    second[0:R, :] = h[o]
    second[R : 2 * R, :] = p[o]
    second[2 * R : 3 * R, :] = h[i]


def packed(plane, layers, acc_lo, acc_hi):
    lane = iota((GR, 128), 1)
    for g in range(3):
        for z in layers:
            for arr in range(2):
                base = 40 * g + 4 * (z + 1) + 2 * arr
                here = (lane >= base) & (lane < base + 2)
                acc_lo = jnp.where(here, roll(plane(arr, z, g, slice(0, 128)), base, 1), acc_lo)
                acc_hi = jnp.where(here, roll(plane(arr, z, g, slice(C - 128, C)), base + 2, 1), acc_hi)
    return acc_lo, acc_hi


def pack_y_kernel(slab, first, second, own_lo, own_hi, lo, hi):
    is_odd = (slab[0] & 1) == 1

    def plane(arr, z, g, cols):
        at = slice(R * arr + GR * g, R * arr + GR * g + GR)
        a, b = first[at, cols], second[at, cols]
        return jnp.where(is_odd, a, b) if z < 0 else jnp.where(is_odd, b, a)

    lo[...], hi[...] = packed(plane, (-1, L), own_lo[...], own_hi[...])


def pack_x_kernel(slab, h, p, first, second, ylo, yhi, lo, hi):
    is_odd = (slab[0] & 1) == 1
    for ref, o, i, yrow in ((lo, 0, 1, 0), (hi, R - 1, R - 2, GR - 1)):
        for arr, own in ((0, h), (1, p)):
            at = slice(R * arr + o, R * arr + o + 1)
            a, b = first[at, :], second[at, :]
            top = 10 * arr
            ref[top : top + 1, :] = jnp.where(is_odd, a, b)
            for z in range(L):
                ref[top + 1 + z : top + 2 + z, :] = own[z, o : o + 1, :]
                ref[20 + L * arr + z : 21 + L * arr + z, :] = own[z, i : i + 1, :]
            ref[top + 9 : top + 10, :] = jnp.where(is_odd, b, a)
        ref[36:37, 0:128] = ylo[yrow : yrow + 1, :]
        ref[36:37, 128:256] = yhi[yrow : yrow + 1, :]
        ref[37:40, :] = jnp.zeros((3, C), F32)


def sums(h, p, beside):
    total, flow = None, None
    for hn, pn in beside:
        t = recip(h + hn)
        total = 1.0 + t if total is None else total + t
        flow = t * (pn - p) if flow is None else flow + t * (pn - p)
    return total, flow


def beside_y(msgs, owns):
    lane = iota((GR, 128), 1)
    sub = iota((GR, 128), 0)
    result = []
    for msg, own, o, i, w in ((msgs[0], owns[0], 1, 0, 0), (msgs[1], owns[1], 0, 1, 1)):
        m, v = msg[...], own[...]
        ho, po = present(roll(m, -o, 1)), roll(m, -o - 2, 1)
        hi_, pi_ = present(roll(m, -i, 1)), roll(m, -i - 2, 1)
        hw, pw = present(roll(v, -w, 1)), roll(v, -w - 2, 1)

        def along_x(f):
            u = roll(f, 1, 0)
            u = jnp.where(sub == 0, roll(u, 40, 1), u)
            d = roll(f, -1, 0)
            d = jnp.where(sub == GR - 1, roll(d, -40, 1), d)
            return u, d

        hu, hd = along_x(ho)
        pu, pd = along_x(po)
        hu = jnp.where((sub == 0) & (lane < 40), ABSENT, hu)
        hd = jnp.where((sub == GR - 1) & (lane >= 80), ABSENT, hd)
        total, flow = sums(ho, po, (
            (hi_, pi_), (hw, pw), (hu, pu), (hd, pd),
            (roll(ho, 4, 1), roll(po, 4, 1)), (roll(ho, -4, 1), roll(po, -4, 1)),
        ))
        result.append((ho, po, total, flow))
    return result


def beside_y_corners(msgs, yst):
    lane = iota((GR, 128), 1)
    sub = iota((GR, 128), 0)
    at_low = (sub == 0) & (lane < 40)
    at_high = (sub == GR - 1) & (lane >= 80)
    result = []
    for s, o, cols in ((0, 1, slice(0, 128)), (1, 0, slice(128, 256))):
        ho, po, total, flow = (yst[s, k] for k in range(4))

        def corner(k):
            low = jnp.broadcast_to(msgs[0][36:37, cols], (GR, 128))
            high = jnp.broadcast_to(msgs[1][36:37, cols], (GR, 128))
            return jnp.where(sub == 0, roll(low, -80 - k, 1), roll(high, 80 - k, 1))

        t = jnp.where(at_low | at_high, recip(ho + present(corner(o))), 0.0)
        result.append(po + (flow + t * (corner(o + 2) - po)) * recip(total + t))
    return result


def beside_x(msgs, owns, xh, xp, xq):
    lane = iota((16, C), 1)
    lane_x = iota((16, 128), 1)
    sub_x = iota((16, 128), 0)
    for s, row_lane in ((0, 80), (1, 0)):
        msg, own = msgs[s], owns[s]

        def rows10(ref, at):
            return jnp.concatenate([ref[at : at + 10, :], jnp.zeros((6, C), F32)], axis=0)

        def rows8(ref, at):
            return jnp.concatenate([jnp.zeros((1, C), F32), ref[at : at + 8, :], jnp.zeros((7, C), F32)], axis=0)

        ho, po = present(rows10(msg, 0)), rows10(msg, 10)
        hi_, pi_ = present(rows8(msg, 20)), rows8(msg, 28)
        hw, pw = present(rows10(own, 0)), rows10(own, 10)

        def corner(cols, k):
            row = jnp.broadcast_to(msg[36:37, cols], (16, 128))
            return jnp.sum(jnp.where(lane_x == row_lane + 4 * sub_x + k, row, 0.0), axis=1, keepdims=True)

        left, right = slice(0, 128), slice(128, 256)
        hl = jnp.where(lane == 0, present(corner(left, 1)), roll(ho, 1, 1))
        pl_ = jnp.where(lane == 0, corner(left, 3), roll(po, 1, 1))
        hr = jnp.where(lane == C - 1, present(corner(right, 0)), roll(ho, -1, 1))
        pr = jnp.where(lane == C - 1, corner(right, 2), roll(po, -1, 1))
        xh[s] = ho
        xp[s] = po
        total, flow = sums(ho, po, (
            (hi_, pi_), (hw, pw), (hl, pl_), (hr, pr),
            (roll(ho, 1, 0), roll(po, 1, 0)), (roll(ho, -1, 0), roll(po, -1, 0)),
        ))
        xq[s] = po + flow * recip(total)


def edge_columns(lo, hi, z, g):
    lane = iota((GR, 128), 1)
    at = 40 * g + 4 * (z + 1)
    return jnp.where(lane == 0, roll(lo, -at, 1), roll(hi, 127 - at, 1))


def around_x(before, here, after):
    sub = iota((8, C), 0)
    return roll(jnp.where(sub == 7, before, here), 1, 0), roll(jnp.where(sub == 0, after, here), -1, 0)


def around_y(here, edge):
    lane = iota((8, 128), 1)
    a, b = here[:, :128], here[:, 128:]
    ra, rb = roll(a, 1, 1), roll(b, 1, 1)
    left = jnp.concatenate([jnp.where(lane == 0, edge, ra), jnp.where(lane == 0, ra, rb)], axis=1)
    ra, rb = roll(a, -1, 1), roll(b, -1, 1)
    right = jnp.concatenate([jnp.where(lane == 127, rb, ra), jnp.where(lane == 127, edge, rb)], axis=1)
    return left, right


def second_chunk(qval, qedge, weight, pval, base, over, lith, shade, put):
    low = qval(-1)[1]
    qc = qval(0)
    flow = weight(0, 4) * (qc[1] - low)
    for z in range(L):
        qn = qval(z + 1)
        flow2 = weight(z + 1, 4) * (qn[1] - qc[1])
        q = qc[1]
        change = flow2 - flow
        for k, qb in enumerate(around_x(*qc) + around_y(q, qedge(z))):
            change = change + weight(z, k) * (qb - q)
        d0 = q - pval(z)
        pn = q + RHO_SECOND * RHO_FIRST * d0 + (2.0 * RHO_SECOND / SPECTRUM_HALF) * (change - d0) * weight(z, 5)
        stress = jnp.maximum(base + over(z) - pn, 0.0)
        odd, upper = classes(lith(z))
        new = pick(odd, upper, PHI_SURFACE) * jnp.exp(-pick(odd, upper, ATHY_RATE) * stress)
        put(z, pn, new, jnp.broadcast_to(shade[z : z + 1, :], (8, C)) * recip(1.0 - new))
        qc, flow = qn, flow2


def above_rows(slab, first, third, rows):
    base = jnp.where((slab[0] & 1) == 1, first[rows(4 * R), :], 0.0)
    return base + jnp.where(slab[0] >= 2, third[rows(R), :], 0.0)


def at8(i):
    return pl.ds(pl.multiple_of(8 * i, 8), 8)


LAST = R // 8 - 1


def triples(h, p, hz, pz, i):
    here = (at8(jnp.maximum(i - 1, 0)), at8(i), at8(jnp.minimum(i + 1, LAST)))

    def at(z):
        return (h, p, z) if 0 <= z < L else (hz, pz, {-1: 0, L: 1, -2: 2, L + 1: 3}[z])

    def hval(z):
        ref, _, k = at(z)
        a, b, c = (ref[k, rows, :] for rows in here)
        return jnp.where(i == 0, ABSENT, a), b, jnp.where(i == LAST, ABSENT, c)

    def pval(z):
        _, ref, k = at(z)
        return tuple(ref[k, rows, :] for rows in here)

    return hval, pval


def pack_own_kernel(slab, h, p, mine, first, third, lo, hi):
    zero = jnp.zeros((GR, 128), F32)
    lo[...], hi[...] = packed(
        lambda arr, z, g, cols: (h, p)[arr][z, GR * g : GR * g + GR, cols], range(L), zero, zero
    )
    i = jnp.where((slab[0] & 1) == 1, L - 2, 1)
    third[0:R, :] = p[i]
    third[R : 2 * R, :] = mine[4 * R : 5 * R, :] + first[4 * R : 5 * R, :]


def pre_kernel(slab, h, p, first, second, w, hz, pz):
    is_odd = (slab[0] & 1) == 1
    for ref, at, fix in ((hz, 0, present), (pz, R, lambda t: t)):
        a, b = first[at : at + R, :], second[at : at + R, :]
        ref[0] = fix(jnp.where(is_odd, a, b))
        ref[1] = fix(jnp.where(is_odd, b, a))

    def chunk(i, carry):
        rows = at8(i)
        hval, pval = triples(h, p, hz, pz, i)
        hc, pc = hval(0), pval(0)
        t = recip(hc[1] + hz[0, rows, :])
        flow = t * (pc[1] - pz[0, rows, :])
        w[2, 0, rows, :] = t
        for z in range(L):
            hn, pn = hval(z + 1), pval(z + 1)
            t2 = recip(hc[1] + hn[1])
            flow2 = t2 * (pn[1] - pc[1])
            w[2, z + 1, rows, :] = t2
            total, change = (1.0 + t) + t2, flow2 - flow
            for k, (hb, pb) in enumerate(zip(around_x(*hc), around_x(*pc))):
                u = recip(hc[1] + hb)
                w[k, z, rows, :] = u
                total = total + u
                change = change + u * (pb - pc[1])
            w[3, z, rows, :] = total
            w[4, z, rows, :] = change
            hc, pc, t, flow = hn, pn, t2, flow2
        return carry

    lax.fori_loop(0, R // 8, chunk, 0)


def inner_kernel(
    slab, shade, h, p, over, lith, first, second, third, w, hz1, pz1, ylo, yhi, wlo, whi,
    yst, wy, p1, dd, rr, out0, out1, out2,
    hz, pz, eh, ep, eq, o0, o1, o2, sems,
):
    is_odd = (slab[0] & 1) == 1
    for k in range(2):
        hz[k] = hz1[k]
        pz[k] = pz1[k]
    for ref, a, b, fix in (
        (hz, first[2 * R : 3 * R, :], second[2 * R : 3 * R, :], present),
        (pz, first[3 * R : 4 * R, :], third[0:R, :], lambda t: t),
    ):
        ref[2] = fix(jnp.where(is_odd, a, b))
        ref[3] = fix(jnp.where(is_odd, b, a))
    lo, hi = beside_y((ylo, yhi), (wlo, whi))
    for s, values in enumerate((lo, hi)):
        for k in range(4):
            yst[s, k] = values[k]
    qlo, qhi = (v[1] + v[3] * recip(v[2]) for v in (lo, hi))
    for z in range(-1, L + 1):
        for g in range(3):
            rows = slice(GR * g, GR * g + GR)
            eh[z + 1, rows, :] = edge_columns(lo[0], hi[0], z, g)
            ep[z + 1, rows, :] = edge_columns(lo[1], hi[1], z, g)
            if 0 <= z < L:
                eq[z, rows, :] = edge_columns(qlo, qhi, z, g)

    def chunk1(i, carry):
        rows = at8(i)
        hval, pval = triples(h, p, hz, pz, i)

        def finish(z, hc, pc, total, change):
            for k, (hb, pb) in enumerate(zip(around_y(hc, eh[z + 1, rows, :]), around_y(pc, ep[z + 1, rows, :]))):
                u = recip(hc + hb)
                if 0 <= z < L:
                    wy[k, z, rows, :] = u
                total = total + u
                change = change + u * (pb - pc)
            inv = recip(total)
            if 0 <= z < L:
                wy[2, z, rows, :] = inv
            p1[z + 1, rows, :] = pc + change * inv
            at = pl.ds(pl.multiple_of(jnp.where(i == LAST, 8, jnp.where(i == 0, 0, 16)), 8), 8)
            dd[z + 1, at, :] = total
            rr[z + 1, at, :] = change

        for z, out, own in ((-1, -2, 0), (L, L + 1, L - 1)):
            hc, pc = hval(z), pval(z)
            beside = [(hval(out)[1], pval(out)[1]), (hval(own)[1], pval(own)[1])]
            beside += list(zip(around_x(*hc), around_x(*pc)))
            finish(z, hc[1], pc[1], *sums(hc[1], pc[1], beside))
        for z in range(L):
            finish(z, h[z, rows, :], p[z, rows, :], w[3, z, rows, :], w[4, z, rows, :])
        return carry

    lax.fori_loop(0, R // 8, chunk1, 0)

    def moved(i):
        return [
            pltpu.make_async_copy(src.at[:, at8(i), :], dst.at[:, at8(i), :], sems.at[k, i])
            for k, (src, dst) in enumerate(((o0, out0), (o1, out1), (o2, out2)))
        ]

    def chunk2(i, carry):
        rows = at8(i)
        here = (at8(i - 1), rows, at8(i + 1))

        def put(z, a, b, c):
            o0[z, rows, :] = a
            o1[z, rows, :] = b
            o2[z, rows, :] = c

        second_chunk(
            lambda z: tuple(p1[z + 1, r, :] for r in here),
            lambda z: eq[z, rows, :],
            lambda z, k: (w, w, wy, wy, w, wy)[k][(0, 1, 0, 1, 2, 2)[k], z, rows, :],
            lambda z: p[z, rows, :],
            above_rows(slab, first, third, lambda top: pl.ds(pl.multiple_of(top + 8 * i, 8), 8)),
            lambda z: over[z, rows, :],
            lambda z: lith[z, rows, :],
            shade, put,
        )
        for copy in moved(i):
            copy.start()
        return carry

    lax.fori_loop(1, LAST, chunk2, 0)

    def arrive(i, carry):
        for copy in moved(i):
            copy.wait()
        return carry

    lax.fori_loop(1, LAST, arrive, 0)


def outer_kernel(
    slab, shade, h, p, over, lith, first, third, xlo, xhi, vlo, vhi,
    hz, pz, w, yst, wy, p1, dd, rr, in0, in1, in2,
    out0, out1, out2,
    xh, xp, xq, q1, wt, o0, o1, o2, sems,
):
    beside_x((xlo, xhi), (vlo, vhi), xh, xp, xq)
    lo, hi = beside_y_corners((xlo, xhi), yst)
    sub = iota((8, C), 0)
    copies = []
    for s, top, g, part in ((0, 0, 0, slice(0, 8)), (1, R - 8, 2, slice(GR - 8, GR))):
        rows = slice(top, top + 8)
        near = slice(8, 16) if s == 0 else slice(R - 16, R - 8)
        edge = sub == (0 if s == 0 else 7)

        def strip(ref, z, s=s):
            return jnp.broadcast_to(ref[s, z + 1 : z + 2, :], (8, C))

        for z in range(-1, L + 1):
            if 0 <= z < L:
                hc, pc = h[z, rows, :], p[z, rows, :]
            else:
                k = 0 if z < 0 else 1
                hc, pc = hz[k, rows, :], pz[k, rows, :]
            total, change = dd[z + 1, 8 * s : 8 * s + 8, :], rr[z + 1, 8 * s : 8 * s + 8, :]
            t = jnp.where(edge, recip(hc + strip(xh, z)), 0.0)
            inv = recip(total + t)
            q1[s, z + 1] = pc + (change + t * (strip(xp, z) - pc)) * inv
            if 0 <= z < L:
                wt[s, 0, z] = w[s, z, rows, :] + t
                wt[s, 1, z] = inv

        def q_triple(z, s=s, near=near):
            here = q1[s, z + 1]
            if z < 0 or z >= L:
                return here, here, here
            inside = p1[z + 1, near, :]
            return (strip(xq, z), here, inside) if s == 0 else (inside, here, strip(xq, z))

        def weight(z, k, s=s, rows=rows):
            if k == s:
                return wt[s, 0, z]
            if k == 5:
                return wt[s, 1, z]
            return (w, w, wy, wy, w)[k][(0, 1, 0, 1, 2)[k], z, rows, :]

        def put(z, a, b, c, s=s):
            o0[s, z] = a
            o1[s, z] = b
            o2[s, z] = c

        second_chunk(
            q_triple,
            lambda z: edge_columns(lo, hi, z, g)[part],
            weight,
            lambda z: p[z, rows, :],
            above_rows(slab, first, third, lambda t: slice(t + top, t + top + 8)),
            lambda z: over[z, rows, :],
            lambda z: lith[z, rows, :],
            shade, put,
        )
        for k, (src, dst) in enumerate(((o0, out0), (o1, out1), (o2, out2))):
            copy = pltpu.make_async_copy(src.at[s], dst.at[:, rows, :], sems.at[s, k])
            copy.start()
            copies.append(copy)
    for copy in copies:
        copy.wait()


SMEM, VMEM, HBM = pltpu.SMEM, pltpu.VMEM, pltpu.HBM


def call(kernel, name, ins, outs, scratch=(), aliases=None):
    return pl.pallas_call(
        kernel,
        out_shape=[jax.ShapeDtypeStruct(s, t) for s, t, _ in outs],
        in_specs=[pl.BlockSpec(memory_space=m) for m in ins],
        out_specs=[pl.BlockSpec(memory_space=m) for _, _, m in outs],
        scratch_shapes=list(scratch),
        input_output_aliases=aliases or {},
        compiler_params=pltpu.CompilerParams(vmem_limit_bytes=VMEM_LIMIT),
        name=name,
    )


def pair(axis, lo, hi):
    n = lax.axis_size(axis)
    up = [(i, i + 1) for i in range(n - 1)]
    down = [(j, i) for i, j in up]
    return lax.ppermute(hi, axis, up), lax.ppermute(lo, axis, down)


def vm(*shape):
    return (shape, F32, VMEM)


def body(p_in, poro, lith_in, solid):
    p_in, poro, lith_in, solid = (
        pltpu.with_memory_space_constraint(a, HBM) for a in (p_in, poro, lith_in, solid)
    )
    slab = lax.axis_index("slab").astype(jnp.int32).reshape(1)
    block = (L, R, C)
    dma = pltpu.SemaphoreType.DMA
    p, lith, h, over, first, second, shade = call(
        start_kernel, "start", [SMEM] + [HBM] * 4,
        [vm(*block), (block, jnp.int32, VMEM), vm(*block), vm(*block), vm(5 * R, C), vm(3 * R, C), vm(L, C)],
        [VMEM(block, F32), SMEM((L,), F32), dma((3, L)), dma(())],
    )(slab, p_in, poro, lith_in, solid)
    second_in = lax.ppermute(second, "slab", [(1, 2), (2, 1)])
    first_in = lax.ppermute(first, "slab", [(0, 1), (1, 0), (2, 3), (3, 2)])
    third, *own_y = call(
        pack_own_kernel, "pack_own", [SMEM] + [VMEM] * 4, [vm(2 * R, C), vm(GR, 128), vm(GR, 128)]
    )(slab, h, p, first, first_in)
    third_in = lax.ppermute(third, "slab", [(1, 2), (2, 1), (0, 3)])
    wlo, whi = call(pack_y_kernel, "pack_y", [SMEM] + [VMEM] * 4, [vm(GR, 128)] * 2)(
        slab, first_in, second_in, *own_y
    )
    ylo, yhi = pair("mapy", wlo, whi)
    h2, wlo2 = lax.optimization_barrier((h, wlo))
    w, hz, pz = call(
        pre_kernel, "pre", [SMEM] + [VMEM] * 4, [vm(5, L + 1, R, C), vm(2, R, C), vm(2, R, C)]
    )(slab, h2, p, first_in, second_in)
    ylo, yhi, hz = lax.optimization_barrier((ylo, yhi, hz))
    vlo, vhi = call(pack_x_kernel, "pack_x", [SMEM] + [VMEM] * 6, [vm(40, C)] * 2)(
        slab, h, p, first_in, second_in, ylo, yhi
    )
    xlo, xhi = pair("mapx", vlo, vhi)
    hbm = (block, F32, HBM)
    plane = VMEM((4, R, C), F32)
    edges = VMEM((L + 2, R, 128), F32)
    yst, wy, p1, dd, rr, *outs = call(
        inner_kernel, "inner", [SMEM] + [VMEM] * 15,
        [vm(2, 4, GR, 128), vm(3, L, R, C), vm(L + 2, R, C)] + [vm(L + 2, 24, C)] * 2 + [hbm] * 3,
        [plane, plane, edges, edges, VMEM((L, R, 128), F32)] + [VMEM(block, F32)] * 3 + [dma((3, R // 8))],
    )(slab, shade, h, p, over, lith, first_in, second_in, third_in, w, hz, pz, ylo, yhi, wlo, whi)
    return tuple(
        call(
            outer_kernel, "outer", [SMEM] + [VMEM] * 19 + [HBM] * 3, [hbm] * 3,
            [VMEM((2, 16, C), F32)] * 3
            + [VMEM((2, L + 2, 8, C), F32), VMEM((2, 2, L, 8, C), F32)]
            + [VMEM((2, L, 8, C), F32)] * 3 + [dma((2, 3))],
            {20: 0, 21: 1, 22: 2},
        )(
            slab, shade, h, p, over, lith, first_in, third_in, xlo, xhi, vlo, vhi,
            hz, pz, w, yst, wy, p1, dd, rr, *outs,
        )
    )


def solution(mesh):
    spec = P("slab", "mapx", "mapy")
    return jax.shard_map(
        body, mesh=mesh, in_specs=(spec, spec, spec, P("slab")), out_specs=(spec,) * 3, check_vma=False
    )
```

```python
import math

import jax
import jax.numpy as jnp
from jax import lax
from jax.experimental import pallas as pl
from jax.experimental.pallas import tpu as pltpu
from jax.sharding import PartitionSpec as P

PHI_SURFACE = (0.45, 0.55, 0.65, 0.4)
ATHY_RATE = (0.25, 0.45, 0.8, 0.35)
MOB_BASE = (1.0, 0.0, -1.5, -0.5)
MOB_SLOPE = (6.0, 5.0, 8.0, 4.0)
GRAIN_DENSITY = (2.65, 2.68, 2.72, 2.71)
WATER_DENSITY = 1.03
SPECTRUM_MID = 1.0
SPECTRUM_HALF = 0.95
SIGMA_RATIO = SPECTRUM_MID / SPECTRUM_HALF
RHO_FIRST = 1.0 / SIGMA_RATIO
RHO_SECOND = 1.0 / (2.0 * SIGMA_RATIO - RHO_FIRST)

H_BASE = tuple(math.log(0.5) - b + 0.35 * s for b, s in zip(MOB_BASE, MOB_SLOPE))
H_SLOPE = tuple(-s for s in MOB_SLOPE)
ABSENT = 1e38

F32 = jnp.float32
L, R, C = 8, 96, 256
GR = 32
STEPS = 3
VMEM_LIMIT = 40 * 1024 * 1024


def recip(x):
    r = pl.reciprocal(x, approx=True)
    return r * (2.0 - x * r)


def present(h):
    return jnp.where(h == 0.0, ABSENT, h)


def classes(lith):
    return (lith & 1) == 1, lith >= 2


def pick(odd, upper, t):
    return jnp.where(upper, jnp.where(odd, t[3], t[2]), jnp.where(odd, t[1], t[0]))


def iota(shape, dim):
    return lax.broadcasted_iota(jnp.int32, shape, dim)


def roll(x, shift, axis):
    return pltpu.roll(x, shift % x.shape[axis], axis)


class Later:
    def __init__(self, every):
        self.every, self.count, self.kept = every, 0, []

    def put(self, *stores):
        self.kept.extend(stores)
        self.count += 1
        if self.count % self.every == 0:
            self.flush()

    def flush(self):
        for ref, at, value in self.kept:
            ref[at] = value
        self.kept = []


def start_kernel(slab, p_in, poro_in, lith_in, solid_in, p, lith, h, over, first, second, shade, poro, solid, sems, solid_sem):
    step = R // STEPS
    copies = []
    solid_copy = pltpu.make_async_copy(solid_in, solid, solid_sem)
    solid_copy.start()
    for k in range(STEPS):
        rows = slice(k * step, (k + 1) * step)
        group = [
            pltpu.make_async_copy(src.at[:, rows, :], dst.at[:, rows, :], sems.at[j, k])
            for j, (src, dst) in enumerate(((poro_in, poro), (lith_in, lith), (p_in, p)))
        ]
        for copy in group:
            copy.start()
        copies.append(group)
    solid_copy.wait()
    for z in range(L):
        shade[z : z + 1, :] = jnp.full((1, C), solid[z], F32)
    for k in range(STEPS):
        copies[k][0].wait()
        copies[k][1].wait()

        def chunk(i, carry, k=k):
            rows = pl.ds(pl.multiple_of(k * step + i * 16, 16), 16)
            total = jnp.zeros((16, C), F32)
            later = Later(4)
            for z in range(L):
                odd, upper = classes(lith[z, rows, :])
                phi = poro[z, rows, :]
                hz = jnp.exp(pick(odd, upper, H_BASE) + pick(odd, upper, H_SLOPE) * phi)
                load = (pick(odd, upper, GRAIN_DENSITY) + WATER_DENSITY * phi * recip(1.0 - phi)) * solid[z]
                later.put((h, (z, rows), hz), (over, (z, rows), total + 0.5 * load))
                total = total + load
            first[pl.ds(pl.multiple_of(4 * R + k * step + i * 16, 16), 16), :] = total
            return carry

        lax.fori_loop(0, step // 16, chunk, 0, unroll=True)
    for k in range(STEPS):
        copies[k][2].wait()
    is_odd = (slab[0] & 1) == 1
    o, i = jnp.where(is_odd, 0, L - 1), jnp.where(is_odd, 1, L - 2)
    first[0:R, :] = h[o]
    first[R : 2 * R, :] = p[o]
    first[2 * R : 3 * R, :] = h[i]
    first[3 * R : 4 * R, :] = p[i]
    o, i = jnp.where(is_odd, L - 1, 0), jnp.where(is_odd, L - 2, 1)
    second[0:R, :] = h[o]
    second[R : 2 * R, :] = p[o]
    second[2 * R : 3 * R, :] = h[i]


def packed(plane, layers, acc_lo, acc_hi):
    lane = iota((GR, 128), 1)
    for g in range(3):
        for z in layers:
            for arr in range(2):
                base = 40 * g + 4 * (z + 1) + 2 * arr
                here = (lane >= base) & (lane < base + 2)
                acc_lo = jnp.where(here, roll(plane(arr, z, g, slice(0, 128)), base, 1), acc_lo)
                acc_hi = jnp.where(here, roll(plane(arr, z, g, slice(C - 128, C)), base + 2, 1), acc_hi)
    return acc_lo, acc_hi


def pack_y_kernel(slab, first, second, own_lo, own_hi, lo, hi):
    is_odd = (slab[0] & 1) == 1

    def plane(arr, z, g, cols):
        at = slice(R * arr + GR * g, R * arr + GR * g + GR)
        a, b = first[at, cols], second[at, cols]
        return jnp.where(is_odd, a, b) if z < 0 else jnp.where(is_odd, b, a)

    lo[...], hi[...] = packed(plane, (-1, L), own_lo[...], own_hi[...])


def pack_x_kernel(slab, h, p, first, second, ylo, yhi, lo, hi):
    is_odd = (slab[0] & 1) == 1
    for ref, o, i, yrow in ((lo, 0, 1, 0), (hi, R - 1, R - 2, GR - 1)):
        for arr, own in ((0, h), (1, p)):
            at = slice(R * arr + o, R * arr + o + 1)
            a, b = first[at, :], second[at, :]
            top = 10 * arr
            ref[top : top + 1, :] = jnp.where(is_odd, a, b)
            for z in range(L):
                ref[top + 1 + z : top + 2 + z, :] = own[z, o : o + 1, :]
                ref[20 + L * arr + z : 21 + L * arr + z, :] = own[z, i : i + 1, :]
            ref[top + 9 : top + 10, :] = jnp.where(is_odd, b, a)
        ref[36:37, 0:128] = ylo[yrow : yrow + 1, :]
        ref[36:37, 128:256] = yhi[yrow : yrow + 1, :]
        ref[37:40, :] = jnp.zeros((3, C), F32)


def sums(h, p, beside):
    total, flow = None, None
    for hn, pn in beside:
        t = recip(h + hn)
        total = 1.0 + t if total is None else total + t
        flow = t * (pn - p) if flow is None else flow + t * (pn - p)
    return total, flow


def beside_y(msgs, owns):
    lane = iota((GR, 128), 1)
    sub = iota((GR, 128), 0)
    result = []
    for msg, own, o, i, w in ((msgs[0], owns[0], 1, 0, 0), (msgs[1], owns[1], 0, 1, 1)):
        m, v = msg[...], own[...]
        ho, po = present(roll(m, -o, 1)), roll(m, -o - 2, 1)
        hi_, pi_ = present(roll(m, -i, 1)), roll(m, -i - 2, 1)
        hw, pw = present(roll(v, -w, 1)), roll(v, -w - 2, 1)

        def along_x(f):
            u = roll(f, 1, 0)
            u = jnp.where(sub == 0, roll(u, 40, 1), u)
            d = roll(f, -1, 0)
            d = jnp.where(sub == GR - 1, roll(d, -40, 1), d)
            return u, d

        hu, hd = along_x(ho)
        pu, pd = along_x(po)
        hu = jnp.where((sub == 0) & (lane < 40), ABSENT, hu)
        hd = jnp.where((sub == GR - 1) & (lane >= 80), ABSENT, hd)
        total, flow = sums(ho, po, (
            (hi_, pi_), (hw, pw), (hu, pu), (hd, pd),
            (roll(ho, 4, 1), roll(po, 4, 1)), (roll(ho, -4, 1), roll(po, -4, 1)),
        ))
        result.append((ho, po, total, flow))
    return result


def beside_y_corners(msgs, yst):
    lane = iota((GR, 128), 1)
    sub = iota((GR, 128), 0)
    at_low = (sub == 0) & (lane < 40)
    at_high = (sub == GR - 1) & (lane >= 80)
    result = []
    for s, o, cols in ((0, 1, slice(0, 128)), (1, 0, slice(128, 256))):
        ho, po, total, flow = (yst[s, k] for k in range(4))

        def corner(k):
            low = jnp.broadcast_to(msgs[0][36:37, cols], (GR, 128))
            high = jnp.broadcast_to(msgs[1][36:37, cols], (GR, 128))
            return jnp.where(sub == 0, roll(low, -80 - k, 1), roll(high, 80 - k, 1))

        t = jnp.where(at_low | at_high, recip(ho + present(corner(o))), 0.0)
        result.append(po + (flow + t * (corner(o + 2) - po)) * recip(total + t))
    return result


def beside_x(msgs, owns, xh, xp, xq):
    lane = iota((16, C), 1)
    lane_x = iota((16, 128), 1)
    sub_x = iota((16, 128), 0)
    for s, row_lane in ((0, 80), (1, 0)):
        msg, own = msgs[s], owns[s]

        def rows10(ref, at):
            return jnp.concatenate([ref[at : at + 10, :], jnp.zeros((6, C), F32)], axis=0)

        def rows8(ref, at):
            return jnp.concatenate([jnp.zeros((1, C), F32), ref[at : at + 8, :], jnp.zeros((7, C), F32)], axis=0)

        ho, po = present(rows10(msg, 0)), rows10(msg, 10)
        hi_, pi_ = present(rows8(msg, 20)), rows8(msg, 28)
        hw, pw = present(rows10(own, 0)), rows10(own, 10)

        def corner(cols, k):
            row = jnp.broadcast_to(msg[36:37, cols], (16, 128))
            return jnp.sum(jnp.where(lane_x == row_lane + 4 * sub_x + k, row, 0.0), axis=1, keepdims=True)

        left, right = slice(0, 128), slice(128, 256)
        hl = jnp.where(lane == 0, present(corner(left, 1)), roll(ho, 1, 1))
        pl_ = jnp.where(lane == 0, corner(left, 3), roll(po, 1, 1))
        hr = jnp.where(lane == C - 1, present(corner(right, 0)), roll(ho, -1, 1))
        pr = jnp.where(lane == C - 1, corner(right, 2), roll(po, -1, 1))
        xh[s] = ho
        xp[s] = po
        total, flow = sums(ho, po, (
            (hi_, pi_), (hw, pw), (hl, pl_), (hr, pr),
            (roll(ho, 1, 0), roll(po, 1, 0)), (roll(ho, -1, 0), roll(po, -1, 0)),
        ))
        xq[s] = po + flow * recip(total)


def both_edges(lo, hi):
    lane = iota((GR, 128), 1)
    return jnp.where((lane & 3) == 0, lo, roll(hi, -1, 1))


def edge_columns(both, z, g):
    return roll(both, -40 * g - 4 * (z + 1), 1)


def around_x(before, here, after):
    sub = iota((8, C), 0)
    return roll(jnp.where(sub == 7, before, here), 1, 0), roll(jnp.where(sub == 0, after, here), -1, 0)


def around_y(here, edge):
    lane = iota((8, 128), 1)
    a, b = here[:, :128], here[:, 128:]
    ra, rb = roll(a, 1, 1), roll(b, 1, 1)
    left = jnp.concatenate([jnp.where(lane == 0, edge, ra), jnp.where(lane == 0, ra, rb)], axis=1)
    ra, rb = roll(a, -1, 1), roll(b, -1, 1)
    right = jnp.concatenate([jnp.where(lane == 127, rb, ra), jnp.where(lane == 127, edge, rb)], axis=1)
    return left, right


def second_chunk(qval, qedge, weight, pval, base, over, lith, shade, put):
    low = qval(-1)[1]
    qc = qval(0)
    flow = weight(0, 4) * (qc[1] - low)
    for z in range(L):
        qn = qval(z + 1)
        flow2 = weight(z + 1, 4) * (qn[1] - qc[1])
        q = qc[1]
        change = flow2 - flow
        for k, qb in enumerate(around_x(*qc) + around_y(q, qedge(z))):
            change = change + weight(z, k) * (qb - q)
        d0 = q - pval(z)
        pn = q + RHO_SECOND * RHO_FIRST * d0 + (2.0 * RHO_SECOND / SPECTRUM_HALF) * (change - d0) * weight(z, 5)
        stress = jnp.maximum(base + over(z) - pn, 0.0)
        odd, upper = classes(lith(z))
        new = pick(odd, upper, PHI_SURFACE) * jnp.exp(-pick(odd, upper, ATHY_RATE) * stress)
        put(z, pn, new, jnp.broadcast_to(shade[z : z + 1, :], (8, C)) * recip(1.0 - new))
        qc, flow = qn, flow2


def above_rows(slab, first, third, rows):
    base = jnp.where((slab[0] & 1) == 1, first[rows(4 * R), :], 0.0)
    return base + jnp.where(slab[0] >= 2, third[rows(R), :], 0.0)


def at8(i):
    return pl.ds(pl.multiple_of(8 * i, 8), 8)


LAST = R // 8 - 1


def triples(h, p, hz, pz, i):
    here = (at8(jnp.maximum(i - 1, 0)), at8(i), at8(jnp.minimum(i + 1, LAST)))

    def at(z):
        return (h, p, z) if 0 <= z < L else (hz, pz, {-1: 0, L: 1, -2: 2, L + 1: 3}[z])

    def hval(z):
        ref, _, k = at(z)
        a, b, c = (ref[k, rows, :] for rows in here)
        return jnp.where(i == 0, ABSENT, a), b, jnp.where(i == LAST, ABSENT, c)

    def pval(z):
        _, ref, k = at(z)
        return tuple(ref[k, rows, :] for rows in here)

    return hval, pval


def pack_own_kernel(slab, h, p, mine, first, third, lo, hi):
    zero = jnp.zeros((GR, 128), F32)
    lo[...], hi[...] = packed(
        lambda arr, z, g, cols: (h, p)[arr][z, GR * g : GR * g + GR, cols], range(L), zero, zero
    )
    i = jnp.where((slab[0] & 1) == 1, L - 2, 1)
    third[0:R, :] = p[i]
    third[R : 2 * R, :] = mine[4 * R : 5 * R, :] + first[4 * R : 5 * R, :]


def pre_kernel(slab, h, p, first, second, w, hz, pz):
    is_odd = (slab[0] & 1) == 1
    for ref, at, fix in ((hz, 0, present), (pz, R, lambda t: t)):
        a, b = first[at : at + R, :], second[at : at + R, :]
        ref[0] = fix(jnp.where(is_odd, a, b))
        ref[1] = fix(jnp.where(is_odd, b, a))

    def chunk(i, carry):
        rows = at8(i)
        hval, pval = triples(h, p, hz, pz, i)
        hc, pc = hval(0), pval(0)
        t = recip(hc[1] + hz[0, rows, :])
        flow = t * (pc[1] - pz[0, rows, :])
        w[2, 0, rows, :] = t
        later = Later(4)
        for z in range(L):
            hn, pn = hval(z + 1), pval(z + 1)
            t2 = recip(hc[1] + hn[1])
            flow2 = t2 * (pn[1] - pc[1])
            total, change = (1.0 + t) + t2, flow2 - flow
            stores = [(w, (2, z + 1, rows), t2)]
            for k, (hb, pb) in enumerate(zip(around_x(*hc), around_x(*pc))):
                u = recip(hc[1] + hb)
                stores.append((w, (k, z, rows), u))
                total = total + u
                change = change + u * (pb - pc[1])
            later.put(*stores, (w, (3, z, rows), total), (w, (4, z, rows), change))
            hc, pc, t, flow = hn, pn, t2, flow2
        later.flush()
        return carry

    lax.fori_loop(0, R // 8, chunk, 0, unroll=True)


def inner_kernel(
    slab, shade, h, p, over, lith, first, second, third, w, hz1, pz1, ylo, yhi, wlo, whi,
    yst, wy, p1, iv, out0, out1, out2,
    hz, pz, eh, ep, eq, o0, o1, o2, sems,
):
    is_odd = (slab[0] & 1) == 1
    for k in range(2):
        hz[k] = hz1[k]
        pz[k] = pz1[k]
    for ref, a, b, fix in (
        (hz, first[2 * R : 3 * R, :], second[2 * R : 3 * R, :], present),
        (pz, first[3 * R : 4 * R, :], third[0:R, :], lambda t: t),
    ):
        ref[2] = fix(jnp.where(is_odd, a, b))
        ref[3] = fix(jnp.where(is_odd, b, a))
    lo, hi = beside_y((ylo, yhi), (wlo, whi))
    for s, values in enumerate((lo, hi)):
        for k in range(4):
            yst[s, k] = values[k]
    qlo, qhi = (v[1] + v[3] * recip(v[2]) for v in (lo, hi))
    hb, pb, qb = both_edges(lo[0], hi[0]), both_edges(lo[1], hi[1]), both_edges(qlo, qhi)
    for z in range(-1, L + 1):
        for g in range(3):
            rows = slice(GR * g, GR * g + GR)
            eh[z + 1, rows, :] = edge_columns(hb, z, g)
            ep[z + 1, rows, :] = edge_columns(pb, z, g)
            if 0 <= z < L:
                eq[z, rows, :] = edge_columns(qb, z, g)

    def chunk1(i, carry):
        rows = at8(i)
        hval, pval = triples(h, p, hz, pz, i)

        later = Later(4)

        def finish(z, hc, pc, total, change):
            stores = []
            for k, (hb, pb) in enumerate(zip(around_y(hc, eh[z + 1, rows, :]), around_y(pc, ep[z + 1, rows, :]))):
                u = recip(hc + hb)
                if 0 <= z < L:
                    stores.append((wy, (k, z, rows), u))
                total = total + u
                change = change + u * (pb - pc)
            inv = recip(total)
            later.put(*stores, (iv, (z + 1, rows), inv), (p1, (z + 1, rows), pc + change * inv))

        for z, out, own in ((-1, -2, 0), (L, L + 1, L - 1)):
            hc, pc = hval(z), pval(z)
            beside = [(hval(out)[1], pval(out)[1]), (hval(own)[1], pval(own)[1])]
            beside += list(zip(around_x(*hc), around_x(*pc)))
            finish(z, hc[1], pc[1], *sums(hc[1], pc[1], beside))
        for z in range(L):
            finish(z, h[z, rows, :], p[z, rows, :], w[3, z, rows, :], w[4, z, rows, :])
        later.flush()
        return carry

    lax.fori_loop(0, R // 8, chunk1, 0, unroll=True)

    def moved(i):
        return [
            pltpu.make_async_copy(src.at[:, at8(i), :], dst.at[:, at8(i), :], sems.at[k, i])
            for k, (src, dst) in enumerate(((o0, out0), (o1, out1), (o2, out2)))
        ]

    def chunk2(i, carry):
        rows = at8(i)
        here = (at8(i - 1), rows, at8(i + 1))

        later = Later(4)

        def put(z, a, b, c):
            later.put((o0, (z, rows), a), (o1, (z, rows), b), (o2, (z, rows), c))

        second_chunk(
            lambda z: tuple(p1[z + 1, r, :] for r in here),
            lambda z: eq[z, rows, :],
            lambda z, k: iv[z + 1, rows, :] if k == 5 else (w, w, wy, wy, w)[k][(0, 1, 0, 1, 2)[k], z, rows, :],
            lambda z: p[z, rows, :],
            above_rows(slab, first, third, lambda top: pl.ds(pl.multiple_of(top + 8 * i, 8), 8)),
            lambda z: over[z, rows, :],
            lambda z: lith[z, rows, :],
            shade, put,
        )
        later.flush()
        for copy in moved(i):
            copy.start()
        return carry

    lax.fori_loop(1, LAST, chunk2, 0, unroll=True)

    def arrive(i, carry):
        for copy in moved(i):
            copy.wait()
        return carry

    lax.fori_loop(1, LAST, arrive, 0)


def outer_kernel(
    slab, shade, h, p, over, lith, first, third, xlo, xhi, vlo, vhi,
    hz, pz, w, yst, wy, p1, iv, in0, in1, in2,
    out0, out1, out2,
    xh, xp, xq, q1, wt, o0, o1, o2, sems,
):
    beside_x((xlo, xhi), (vlo, vhi), xh, xp, xq)
    columns = both_edges(*beside_y_corners((xlo, xhi), yst))
    sub = iota((8, C), 0)
    copies = []
    for s, top, g, part in ((0, 0, 0, slice(0, 8)), (1, R - 8, 2, slice(GR - 8, GR))):
        rows = slice(top, top + 8)
        near = slice(8, 16) if s == 0 else slice(R - 16, R - 8)
        edge = sub == (0 if s == 0 else 7)

        def strip(ref, z, s=s):
            return jnp.broadcast_to(ref[s, z + 1 : z + 2, :], (8, C))

        later = Later(5)
        for z in range(-1, L + 1):
            if 0 <= z < L:
                hc, pc = h[z, rows, :], p[z, rows, :]
            else:
                k = 0 if z < 0 else 1
                hc, pc = hz[k, rows, :], pz[k, rows, :]
            total = recip(iv[z + 1, rows, :])
            change = (p1[z + 1, rows, :] - pc) * total
            t = jnp.where(edge, recip(hc + strip(xh, z)), 0.0)
            inv = recip(total + t)
            stores = [(q1, (s, z + 1), pc + (change + t * (strip(xp, z) - pc)) * inv)]
            if 0 <= z < L:
                stores += [(wt, (s, 0, z), w[s, z, rows, :] + t), (wt, (s, 1, z), inv)]
            later.put(*stores)
        later.flush()

        def q_triple(z, s=s, near=near):
            here = q1[s, z + 1]
            if z < 0 or z >= L:
                return here, here, here
            inside = p1[z + 1, near, :]
            return (strip(xq, z), here, inside) if s == 0 else (inside, here, strip(xq, z))

        def weight(z, k, s=s, rows=rows):
            if k == s:
                return wt[s, 0, z]
            if k == 5:
                return wt[s, 1, z]
            return (w, w, wy, wy, w)[k][(0, 1, 0, 1, 2)[k], z, rows, :]

        later = Later(4)

        def put(z, a, b, c, s=s, later=later):
            later.put((o0, (s, z), a), (o1, (s, z), b), (o2, (s, z), c))

        second_chunk(
            q_triple,
            lambda z: edge_columns(columns[part], z, g),
            weight,
            lambda z: p[z, rows, :],
            above_rows(slab, first, third, lambda t: slice(t + top, t + top + 8)),
            lambda z: over[z, rows, :],
            lambda z: lith[z, rows, :],
            shade, put,
        )
        for k, (src, dst) in enumerate(((o0, out0), (o1, out1), (o2, out2))):
            copy = pltpu.make_async_copy(src.at[s], dst.at[:, rows, :], sems.at[s, k])
            copy.start()
            copies.append(copy)
    for copy in copies:
        copy.wait()


SMEM, VMEM, HBM = pltpu.SMEM, pltpu.VMEM, pltpu.HBM


def call(kernel, name, ins, outs, scratch=(), aliases=None):
    return pl.pallas_call(
        kernel,
        out_shape=[jax.ShapeDtypeStruct(s, t) for s, t, _ in outs],
        in_specs=[pl.BlockSpec(memory_space=m) for m in ins],
        out_specs=[pl.BlockSpec(memory_space=m) for _, _, m in outs],
        scratch_shapes=list(scratch),
        input_output_aliases=aliases or {},
        compiler_params=pltpu.CompilerParams(vmem_limit_bytes=VMEM_LIMIT),
        name=name,
    )


def pair(axis, lo, hi):
    n = lax.axis_size(axis)
    up = [(i, i + 1) for i in range(n - 1)]
    down = [(j, i) for i, j in up]
    return lax.ppermute(hi, axis, up), lax.ppermute(lo, axis, down)


def vm(*shape):
    return (shape, F32, VMEM)


def body(p_in, poro, lith_in, solid):
    p_in, poro, lith_in, solid = (
        pltpu.with_memory_space_constraint(a, HBM) for a in (p_in, poro, lith_in, solid)
    )
    slab = lax.axis_index("slab").astype(jnp.int32).reshape(1)
    block = (L, R, C)
    dma = pltpu.SemaphoreType.DMA
    p, lith, h, over, first, second, shade = call(
        start_kernel, "start", [SMEM] + [HBM] * 4,
        [vm(*block), (block, jnp.int32, VMEM), vm(*block), vm(*block), vm(5 * R, C), vm(3 * R, C), vm(L, C)],
        [VMEM(block, F32), SMEM((L,), F32), dma((3, STEPS)), dma(())],
    )(slab, p_in, poro, lith_in, solid)
    second_in = lax.ppermute(second, "slab", [(1, 2), (2, 1)])
    first_in = lax.ppermute(first, "slab", [(0, 1), (1, 0), (2, 3), (3, 2)])
    third, *own_y = call(
        pack_own_kernel, "pack_own", [SMEM] + [VMEM] * 4, [vm(2 * R, C), vm(GR, 128), vm(GR, 128)]
    )(slab, h, p, first, first_in)
    third_in = lax.ppermute(third, "slab", [(1, 2), (2, 1), (0, 3)])
    wlo, whi = call(pack_y_kernel, "pack_y", [SMEM] + [VMEM] * 4, [vm(GR, 128)] * 2)(
        slab, first_in, second_in, *own_y
    )
    ylo, yhi = pair("mapy", wlo, whi)
    h2, wlo2 = lax.optimization_barrier((h, wlo))
    w, hz, pz = call(
        pre_kernel, "pre", [SMEM] + [VMEM] * 4, [vm(5, L + 1, R, C), vm(2, R, C), vm(2, R, C)]
    )(slab, h2, p, first_in, second_in)
    ylo, yhi, hz = lax.optimization_barrier((ylo, yhi, hz))
    vlo, vhi = call(pack_x_kernel, "pack_x", [SMEM] + [VMEM] * 6, [vm(40, C)] * 2)(
        slab, h, p, first_in, second_in, ylo, yhi
    )
    xlo, xhi = pair("mapx", vlo, vhi)
    hbm = (block, F32, HBM)
    plane = VMEM((4, R, C), F32)
    edges = VMEM((L + 2, R, 128), F32)
    yst, wy, p1, iv, *outs = call(
        inner_kernel, "inner", [SMEM] + [VMEM] * 15,
        [vm(2, 4, GR, 128), vm(2, L, R, C), vm(L + 2, R, C), vm(L + 2, R, C)] + [hbm] * 3,
        [plane, plane, edges, edges, VMEM((L, R, 128), F32)] + [VMEM(block, F32)] * 3 + [dma((3, R // 8))],
    )(slab, shade, h, p, over, lith, first_in, second_in, third_in, w, hz, pz, ylo, yhi, wlo, whi)
    return tuple(
        call(
            outer_kernel, "outer", [SMEM] + [VMEM] * 18 + [HBM] * 3, [hbm] * 3,
            [VMEM((2, 16, C), F32)] * 3
            + [VMEM((2, L + 2, 8, C), F32), VMEM((2, 2, L, 8, C), F32)]
            + [VMEM((2, L, 8, C), F32)] * 3 + [dma((2, 3))],
            {19: 0, 20: 1, 21: 2},
        )(
            slab, shade, h, p, over, lith, first_in, third_in, xlo, xhi, vlo, vhi,
            hz, pz, w, yst, wy, p1, iv, *outs,
        )
    )


def solution(mesh):
    spec = P("slab", "mapx", "mapy")
    return jax.shard_map(
        body, mesh=mesh, in_specs=(spec, spec, spec, P("slab")), out_specs=(spec,) * 3, check_vma=False
    )
```

```python
import math

import jax
import jax.numpy as jnp
from jax import lax
from jax.experimental import pallas as pl
from jax.experimental.pallas import tpu as pltpu
from jax.sharding import PartitionSpec as P

PHI_SURFACE = (0.45, 0.55, 0.65, 0.4)
ATHY_RATE = (0.25, 0.45, 0.8, 0.35)
MOB_BASE = (1.0, 0.0, -1.5, -0.5)
MOB_SLOPE = (6.0, 5.0, 8.0, 4.0)
GRAIN_DENSITY = (2.65, 2.68, 2.72, 2.71)
WATER_DENSITY = 1.03
SPECTRUM_MID = 1.0
SPECTRUM_HALF = 0.95
SIGMA_RATIO = SPECTRUM_MID / SPECTRUM_HALF
RHO_FIRST = 1.0 / SIGMA_RATIO
RHO_SECOND = 1.0 / (2.0 * SIGMA_RATIO - RHO_FIRST)

H_BASE = tuple(math.log(0.5) - b + 0.35 * s for b, s in zip(MOB_BASE, MOB_SLOPE))
H_SLOPE = tuple(-s for s in MOB_SLOPE)
ABSENT = 1e38

F32 = jnp.float32
L, R, C = 8, 96, 256
GR = 32
STEPS = 3
VMEM_LIMIT = 40 * 1024 * 1024


def recip(x):
    r = pl.reciprocal(x, approx=True)
    return r * (2.0 - x * r)


def present(h):
    return jnp.where(h == 0.0, ABSENT, h)


def classes(lith):
    return (lith & 1) == 1, lith >= 2


def pick(odd, upper, t):
    return jnp.where(upper, jnp.where(odd, t[3], t[2]), jnp.where(odd, t[1], t[0]))


def iota(shape, dim):
    return lax.broadcasted_iota(jnp.int32, shape, dim)


def roll(x, shift, axis):
    return pltpu.roll(x, shift % x.shape[axis], axis)


class Later:
    def __init__(self, every):
        self.every, self.count, self.kept = every, 0, []

    def put(self, *stores):
        self.kept.extend(stores)
        self.count += 1
        if self.count % self.every == 0:
            self.flush()

    def flush(self):
        for ref, at, value in self.kept:
            ref[at] = value
        self.kept = []


def packed(plane, layers, acc_lo, acc_hi):
    lane = iota((GR, 128), 1)
    for g in range(3):
        for z in layers:
            for arr in range(2):
                base = 40 * g + 4 * (z + 1) + 2 * arr
                here = (lane >= base) & (lane < base + 2)
                acc_lo = jnp.where(here, roll(plane(arr, z, g, slice(0, 128)), base, 1), acc_lo)
                acc_hi = jnp.where(here, roll(plane(arr, z, g, slice(C - 128, C)), base + 2, 1), acc_hi)
    return acc_lo, acc_hi


def start_kernel(slab, p_in, poro_in, lith_in, solid_in, p, lith, h, over, first, second, shade, poro, solid, sems, solid_sem):
    step = R // STEPS
    copies = []
    solid_copy = pltpu.make_async_copy(solid_in, solid, solid_sem)
    solid_copy.start()
    for k in range(STEPS):
        rows = slice(k * step, (k + 1) * step)
        group = [
            pltpu.make_async_copy(src.at[:, rows, :], dst.at[:, rows, :], sems.at[j, k])
            for j, (src, dst) in enumerate(((poro_in, poro), (lith_in, lith), (p_in, p)))
        ]
        for copy in group:
            copy.start()
        copies.append(group)
    solid_copy.wait()
    for z in range(L):
        shade[z : z + 1, :] = jnp.full((1, C), solid[z], F32)
    for k in range(STEPS):
        copies[k][0].wait()
        copies[k][1].wait()

        def chunk(i, carry, k=k):
            rows = pl.ds(pl.multiple_of(k * step + i * 16, 16), 16)
            total = jnp.zeros((16, C), F32)
            later = Later(4)
            for z in range(L):
                odd, upper = classes(lith[z, rows, :])
                phi = poro[z, rows, :]
                hz = jnp.exp(pick(odd, upper, H_BASE) + pick(odd, upper, H_SLOPE) * phi)
                load = (pick(odd, upper, GRAIN_DENSITY) + WATER_DENSITY * phi * recip(1.0 - phi)) * solid[z]
                later.put((h, (z, rows), hz), (over, (z, rows), total + 0.5 * load))
                total = total + load
            first[pl.ds(pl.multiple_of(4 * R + k * step + i * 16, 16), 16), :] = total
            return carry

        lax.fori_loop(0, step // 16, chunk, 0, unroll=True)
    for k in range(STEPS):
        copies[k][2].wait()
    is_odd = (slab[0] & 1) == 1
    o, i = jnp.where(is_odd, 0, L - 1), jnp.where(is_odd, 1, L - 2)
    first[0:R, :] = h[o]
    first[R : 2 * R, :] = p[o]
    first[2 * R : 3 * R, :] = h[i]
    first[3 * R : 4 * R, :] = p[i]
    o = jnp.where(is_odd, L - 1, 0)
    zero = jnp.zeros((GR, 128), F32)
    lo, hi = packed(lambda arr, z, g, cols: (h, p)[arr][o, GR * g : GR * g + GR, cols], (-1,), zero, zero)
    second[0:GR, 0:128] = lo
    second[0:GR, 128:256] = hi
    for k, (ref, row) in enumerate(((h, 0), (p, 0), (h, R - 1), (p, R - 1))):
        second[GR + k : GR + k + 1, :] = ref[o, row : row + 1, :]
    second[GR + 4 : GR + 8, :] = jnp.zeros((4, C), F32)


def pack_own_kernel(slab, h, p, mine, first, planes, both, lo, hi):
    is_odd = (slab[0] & 1) == 1
    zero = jnp.zeros((GR, 128), F32)
    own = packed(lambda arr, z, g, cols: (h, p)[arr][z, GR * g : GR * g + GR, cols], range(L), zero, zero)
    near = packed(
        lambda arr, z, g, cols: first[R * arr + GR * g : R * arr + GR * g + GR, cols], (-1,), zero, zero
    )
    for ref, a, b in zip((lo, hi), own, near):
        ref[...] = a + jnp.where(is_odd, b, roll(b, 4 * (L + 1), 1))
    total = mine[4 * R : 5 * R, :] + first[4 * R : 5 * R, :]
    o, i = jnp.where(is_odd, L - 1, 0), jnp.where(is_odd, L - 2, 1)
    planes[0:R, :] = h[o]
    planes[R : 2 * R, :] = p[o]
    planes[2 * R : 3 * R, :] = h[i]
    planes[3 * R : 4 * R, :] = p[i]
    planes[4 * R : 5 * R, :] = total
    both[...] = total


def pack_y_kernel(slab, edges, own_lo, own_hi, lo, hi):
    is_odd = (slab[0] & 1) == 1
    for ref, own, cols in ((lo, own_lo, slice(0, 128)), (hi, own_hi, slice(128, 256))):
        b = edges[0:GR, cols]
        ref[...] = own[...] + jnp.where(is_odd, roll(b, 4 * (L + 1), 1), b)


def pack_x_kernel(slab, h, p, first, edges, ylo, yhi, lo, hi):
    is_odd = (slab[0] & 1) == 1
    for s, (ref, o, i, yrow) in enumerate(((lo, 0, 1, 0), (hi, R - 1, R - 2, GR - 1))):
        for arr, own in ((0, h), (1, p)):
            at = R * arr + o
            k = GR + 2 * s + arr
            a, b = first[at : at + 1, :], edges[k : k + 1, :]
            top = 10 * arr
            ref[top : top + 1, :] = jnp.where(is_odd, a, b)
            for z in range(L):
                ref[top + 1 + z : top + 2 + z, :] = own[z, o : o + 1, :]
                ref[20 + L * arr + z : 21 + L * arr + z, :] = own[z, i : i + 1, :]
            ref[top + 9 : top + 10, :] = jnp.where(is_odd, b, a)
        ref[36:37, 0:128] = ylo[yrow : yrow + 1, :]
        ref[36:37, 128:256] = yhi[yrow : yrow + 1, :]
        ref[37:40, :] = jnp.zeros((3, C), F32)


def sums(h, p, beside):
    total, flow = None, None
    for hn, pn in beside:
        t = recip(h + hn)
        total = 1.0 + t if total is None else total + t
        flow = t * (pn - p) if flow is None else flow + t * (pn - p)
    return total, flow


def beside_y(msgs, owns):
    lane = iota((GR, 128), 1)
    sub = iota((GR, 128), 0)
    result = []
    for msg, own, o, i, w in ((msgs[0], owns[0], 1, 0, 0), (msgs[1], owns[1], 0, 1, 1)):
        m, v = msg[...], own[...]
        ho, po = present(roll(m, -o, 1)), roll(m, -o - 2, 1)
        hi_, pi_ = present(roll(m, -i, 1)), roll(m, -i - 2, 1)
        hw, pw = present(roll(v, -w, 1)), roll(v, -w - 2, 1)

        def along_x(f):
            u = roll(f, 1, 0)
            u = jnp.where(sub == 0, roll(u, 40, 1), u)
            d = roll(f, -1, 0)
            d = jnp.where(sub == GR - 1, roll(d, -40, 1), d)
            return u, d

        hu, hd = along_x(ho)
        pu, pd = along_x(po)
        hu = jnp.where((sub == 0) & (lane < 40), ABSENT, hu)
        hd = jnp.where((sub == GR - 1) & (lane >= 80), ABSENT, hd)
        total, flow = sums(ho, po, (
            (hi_, pi_), (hw, pw), (hu, pu), (hd, pd),
            (roll(ho, 4, 1), roll(po, 4, 1)), (roll(ho, -4, 1), roll(po, -4, 1)),
        ))
        result.append((ho, po, total, flow))
    return result


def beside_y_corners(msgs, yst):
    lane = iota((GR, 128), 1)
    sub = iota((GR, 128), 0)
    at_low = (sub == 0) & (lane < 40)
    at_high = (sub == GR - 1) & (lane >= 80)
    result = []
    for s, o, cols in ((0, 1, slice(0, 128)), (1, 0, slice(128, 256))):
        ho, po, total, flow = (yst[s, k] for k in range(4))

        def corner(k):
            low = jnp.broadcast_to(msgs[0][36:37, cols], (GR, 128))
            high = jnp.broadcast_to(msgs[1][36:37, cols], (GR, 128))
            return jnp.where(sub == 0, roll(low, -80 - k, 1), roll(high, 80 - k, 1))

        t = jnp.where(at_low | at_high, recip(ho + present(corner(o))), 0.0)
        result.append(po + (flow + t * (corner(o + 2) - po)) * recip(total + t))
    return result


def beside_x(msgs, owns, xh, xp, xq):
    lane = iota((16, C), 1)
    lane_x = iota((16, 128), 1)
    sub_x = iota((16, 128), 0)
    for s, row_lane in ((0, 80), (1, 0)):
        msg, own = msgs[s], owns[s]

        def rows10(ref, at):
            return jnp.concatenate([ref[at : at + 10, :], jnp.zeros((6, C), F32)], axis=0)

        def rows8(ref, at):
            return jnp.concatenate([jnp.zeros((1, C), F32), ref[at : at + 8, :], jnp.zeros((7, C), F32)], axis=0)

        ho, po = present(rows10(msg, 0)), rows10(msg, 10)
        hi_, pi_ = present(rows8(msg, 20)), rows8(msg, 28)
        hw, pw = present(rows10(own, 0)), rows10(own, 10)

        def corner(cols, k):
            row = jnp.broadcast_to(msg[36:37, cols], (16, 128))
            return jnp.sum(jnp.where(lane_x == row_lane + 4 * sub_x + k, row, 0.0), axis=1, keepdims=True)

        left, right = slice(0, 128), slice(128, 256)
        hl = jnp.where(lane == 0, present(corner(left, 1)), roll(ho, 1, 1))
        pl_ = jnp.where(lane == 0, corner(left, 3), roll(po, 1, 1))
        hr = jnp.where(lane == C - 1, present(corner(right, 0)), roll(ho, -1, 1))
        pr = jnp.where(lane == C - 1, corner(right, 2), roll(po, -1, 1))
        xh[s] = ho
        xp[s] = po
        total, flow = sums(ho, po, (
            (hi_, pi_), (hw, pw), (hl, pl_), (hr, pr),
            (roll(ho, 1, 0), roll(po, 1, 0)), (roll(ho, -1, 0), roll(po, -1, 0)),
        ))
        xq[s] = po + flow * recip(total)


def both_edges(lo, hi):
    lane = iota((GR, 128), 1)
    return jnp.where((lane & 3) == 0, lo, roll(hi, -1, 1))


def edge_columns(both, z, g):
    return roll(both, -40 * g - 4 * (z + 1), 1)


def around_x(before, here, after):
    sub = iota((8, C), 0)
    return roll(jnp.where(sub == 7, before, here), 1, 0), roll(jnp.where(sub == 0, after, here), -1, 0)


def around_y(here, edge):
    lane = iota((8, 128), 1)
    a, b = here[:, :128], here[:, 128:]
    ra, rb = roll(a, 1, 1), roll(b, 1, 1)
    left = jnp.concatenate([jnp.where(lane == 0, edge, ra), jnp.where(lane == 0, ra, rb)], axis=1)
    ra, rb = roll(a, -1, 1), roll(b, -1, 1)
    right = jnp.concatenate([jnp.where(lane == 127, rb, ra), jnp.where(lane == 127, edge, rb)], axis=1)
    return left, right


def second_chunk(qval, qedge, weight, pval, base, over, lith, shade, put):
    low = qval(-1)[1]
    qc = qval(0)
    flow = weight(0, 4) * (qc[1] - low)
    for z in range(L):
        qn = qval(z + 1)
        flow2 = weight(z + 1, 4) * (qn[1] - qc[1])
        q = qc[1]
        change = flow2 - flow
        for k, qb in enumerate(around_x(*qc) + around_y(q, qedge(z))):
            change = change + weight(z, k) * (qb - q)
        d0 = q - pval(z)
        pn = q + RHO_SECOND * RHO_FIRST * d0 + (2.0 * RHO_SECOND / SPECTRUM_HALF) * (change - d0) * weight(z, 5)
        stress = jnp.maximum(base + over(z) - pn, 0.0)
        odd, upper = classes(lith(z))
        new = pick(odd, upper, PHI_SURFACE) * jnp.exp(-pick(odd, upper, ATHY_RATE) * stress)
        put(z, pn, new, jnp.broadcast_to(shade[z : z + 1, :], (8, C)) * recip(1.0 - new))
        qc, flow = qn, flow2


def above_rows(slab, first, planes, both, rows):
    base = jnp.where((slab[0] & 1) == 1, first[rows(4 * R), :], 0.0)
    base = base + jnp.where(slab[0] == 2, planes[rows(4 * R), :], 0.0)
    return base + jnp.where(slab[0] == 3, both[rows(0), :], 0.0)


def at8(i):
    return pl.ds(pl.multiple_of(8 * i, 8), 8)


LAST = R // 8 - 1


def triples(h, p, hz, pz, i):
    here = (at8(jnp.maximum(i - 1, 0)), at8(i), at8(jnp.minimum(i + 1, LAST)))

    def at(z):
        return (h, p, z) if 0 <= z < L else (hz, pz, {-1: 0, L: 1, -2: 2, L + 1: 3}[z])

    def hval(z):
        ref, _, k = at(z)
        a, b, c = (ref[k, rows, :] for rows in here)
        return jnp.where(i == 0, ABSENT, a), b, jnp.where(i == LAST, ABSENT, c)

    def pval(z):
        _, ref, k = at(z)
        return tuple(ref[k, rows, :] for rows in here)

    return hval, pval


def pre_kernel(h, p, wlo, w):
    def chunk(i, carry):
        rows = at8(i)
        hval, pval = triples(h, p, None, None, i)
        hc, pc = hval(0), pval(0)
        t, flow = None, None
        later = Later(4)
        for z in range(L):
            stores = []
            total, change = 1.0, 0.0
            if z > 0:
                total, change = total + t, change - flow
            if z < L - 1:
                hn, pn = hval(z + 1), pval(z + 1)
                t = recip(hc[1] + hn[1])
                flow = t * (pn[1] - pc[1])
                stores.append((w, (2, z + 1, rows), t))
                total, change = total + t, change + flow
            for k, (hb, pb) in enumerate(zip(around_x(*hc), around_x(*pc))):
                u = recip(hc[1] + hb)
                stores.append((w, (k, z, rows), u))
                total = total + u
                change = change + u * (pb - pc[1])
            later.put(*stores, (w, (3, z, rows), total), (w, (4, z, rows), change))
            hc, pc = hn, pn
        later.flush()
        return carry

    lax.fori_loop(0, R // 8, chunk, 0, unroll=True)


def weight_of(w, wy, wz, z, k, rows):
    if k == 4 and z in (0, L):
        return wz[z // L, rows, :]
    return (w, w, wy, wy, w)[k][(0, 1, 0, 1, 2)[k], z, rows, :]


def inner_kernel(
    slab, shade, h, p, over, lith, first, planes, both, w, ylo, yhi, wlo, whi,
    yst, wy, wz, p1, iv, hz, pz, out0, out1, out2,
    eh, ep, eq, o0, o1, o2, sems,
):
    is_odd = (slab[0] & 1) == 1
    for k in range(2):
        for ref, at, fix in ((hz, 2 * k * R, present), (pz, (2 * k + 1) * R, lambda t: t)):
            a, b = first[at : at + R, :], planes[at : at + R, :]
            ref[2 * k] = fix(jnp.where(is_odd, a, b))
            ref[2 * k + 1] = fix(jnp.where(is_odd, b, a))
    lo, hi = beside_y((ylo, yhi), (wlo, whi))
    for s, values in enumerate((lo, hi)):
        for k in range(4):
            yst[s, k] = values[k]
    qlo, qhi = (v[1] + v[3] * recip(v[2]) for v in (lo, hi))
    hb, pb, qb = both_edges(lo[0], hi[0]), both_edges(lo[1], hi[1]), both_edges(qlo, qhi)
    for z in range(-1, L + 1):
        for g in range(3):
            rows = slice(GR * g, GR * g + GR)
            eh[z + 1, rows, :] = edge_columns(hb, z, g)
            ep[z + 1, rows, :] = edge_columns(pb, z, g)
            if 0 <= z < L:
                eq[z, rows, :] = edge_columns(qb, z, g)

    def chunk1(i, carry):
        rows = at8(i)
        hval, pval = triples(h, p, hz, pz, i)

        later = Later(4)

        def finish(z, hc, pc, total, change):
            stores = []
            for k, (hb, pb) in enumerate(zip(around_y(hc, eh[z + 1, rows, :]), around_y(pc, ep[z + 1, rows, :]))):
                u = recip(hc + hb)
                if 0 <= z < L:
                    stores.append((wy, (k, z, rows), u))
                total = total + u
                change = change + u * (pb - pc)
            inv = recip(total)
            later.put(*stores, (iv, (z + 1, rows), inv), (p1, (z + 1, rows), pc + change * inv))

        for z, out, own in ((-1, -2, 0), (L, L + 1, L - 1)):
            hc, pc = hval(z), pval(z)
            beside = [(hval(out)[1], pval(out)[1]), (hval(own)[1], pval(own)[1])]
            beside += list(zip(around_x(*hc), around_x(*pc)))
            finish(z, hc[1], pc[1], *sums(hc[1], pc[1], beside))
        for z in range(L):
            hc, pc, total, change = h[z, rows, :], p[z, rows, :], w[3, z, rows, :], w[4, z, rows, :]
            for k in ((0,) if z == 0 else (1,) if z == L - 1 else ()):
                t = recip(hc + hz[k, rows, :])
                later.kept.append((wz, (k, rows), t))
                total = total + t
                change = change + t * (pz[k, rows, :] - pc)
            finish(z, hc, pc, total, change)
        later.flush()
        return carry

    lax.fori_loop(0, R // 8, chunk1, 0, unroll=True)

    def moved(i):
        return [
            pltpu.make_async_copy(src.at[:, at8(i), :], dst.at[:, at8(i), :], sems.at[k, i])
            for k, (src, dst) in enumerate(((o0, out0), (o1, out1), (o2, out2)))
        ]

    def chunk2(i, carry):
        rows = at8(i)
        here = (at8(i - 1), rows, at8(i + 1))

        later = Later(4)

        def put(z, a, b, c):
            later.put((o0, (z, rows), a), (o1, (z, rows), b), (o2, (z, rows), c))

        second_chunk(
            lambda z: tuple(p1[z + 1, r, :] for r in here),
            lambda z: eq[z, rows, :],
            lambda z, k: iv[z + 1, rows, :] if k == 5 else weight_of(w, wy, wz, z, k, rows),
            lambda z: p[z, rows, :],
            above_rows(slab, first, planes, both, lambda top: pl.ds(pl.multiple_of(top + 8 * i, 8), 8)),
            lambda z: over[z, rows, :],
            lambda z: lith[z, rows, :],
            shade, put,
        )
        later.flush()
        for copy in moved(i):
            copy.start()
        return carry

    lax.fori_loop(1, LAST, chunk2, 0, unroll=True)

    def arrive(i, carry):
        for copy in moved(i):
            copy.wait()
        return carry

    lax.fori_loop(1, LAST, arrive, 0)


def outer_kernel(
    slab, shade, h, p, over, lith, first, planes, both, xlo, xhi, vlo, vhi,
    w, yst, wy, wz, p1, iv, hz, pz, in0, in1, in2,
    out0, out1, out2,
    xh, xp, xq, q1, wt, o0, o1, o2, sems,
):
    beside_x((xlo, xhi), (vlo, vhi), xh, xp, xq)
    columns = both_edges(*beside_y_corners((xlo, xhi), yst))
    sub = iota((8, C), 0)
    copies = []
    for s, top, g, part in ((0, 0, 0, slice(0, 8)), (1, R - 8, 2, slice(GR - 8, GR))):
        rows = slice(top, top + 8)
        near = slice(8, 16) if s == 0 else slice(R - 16, R - 8)
        edge = sub == (0 if s == 0 else 7)

        def strip(ref, z, s=s):
            return jnp.broadcast_to(ref[s, z + 1 : z + 2, :], (8, C))

        later = Later(5)
        for z in range(-1, L + 1):
            if 0 <= z < L:
                hc, pc = h[z, rows, :], p[z, rows, :]
            else:
                k = 0 if z < 0 else 1
                hc, pc = hz[k, rows, :], pz[k, rows, :]
            total = recip(iv[z + 1, rows, :])
            change = (p1[z + 1, rows, :] - pc) * total
            t = jnp.where(edge, recip(hc + strip(xh, z)), 0.0)
            inv = recip(total + t)
            stores = [(q1, (s, z + 1), pc + (change + t * (strip(xp, z) - pc)) * inv)]
            if 0 <= z < L:
                stores += [(wt, (s, 0, z), w[s, z, rows, :] + t), (wt, (s, 1, z), inv)]
            later.put(*stores)
        later.flush()

        def q_triple(z, s=s, near=near):
            here = q1[s, z + 1]
            if z < 0 or z >= L:
                return here, here, here
            inside = p1[z + 1, near, :]
            return (strip(xq, z), here, inside) if s == 0 else (inside, here, strip(xq, z))

        def weight(z, k, s=s, rows=rows):
            if k == s:
                return wt[s, 0, z]
            if k == 5:
                return wt[s, 1, z]
            return weight_of(w, wy, wz, z, k, rows)

        later = Later(4)

        def put(z, a, b, c, s=s, later=later):
            later.put((o0, (s, z), a), (o1, (s, z), b), (o2, (s, z), c))

        second_chunk(
            q_triple,
            lambda z: edge_columns(columns[part], z, g),
            weight,
            lambda z: p[z, rows, :],
            above_rows(slab, first, planes, both, lambda t: slice(t + top, t + top + 8)),
            lambda z: over[z, rows, :],
            lambda z: lith[z, rows, :],
            shade, put,
        )
        for k, (src, dst) in enumerate(((o0, out0), (o1, out1), (o2, out2))):
            copy = pltpu.make_async_copy(src.at[s], dst.at[:, rows, :], sems.at[s, k])
            copy.start()
            copies.append(copy)
    for copy in copies:
        copy.wait()


SMEM, VMEM, HBM = pltpu.SMEM, pltpu.VMEM, pltpu.HBM


def call(kernel, name, ins, outs, scratch=(), aliases=None):
    return pl.pallas_call(
        kernel,
        out_shape=[jax.ShapeDtypeStruct(s, t) for s, t, _ in outs],
        in_specs=[pl.BlockSpec(memory_space=m) for m in ins],
        out_specs=[pl.BlockSpec(memory_space=m) for _, _, m in outs],
        scratch_shapes=list(scratch),
        input_output_aliases=aliases or {},
        compiler_params=pltpu.CompilerParams(vmem_limit_bytes=VMEM_LIMIT),
        name=name,
    )


def pair(axis, lo, hi):
    n = lax.axis_size(axis)
    up = [(i, i + 1) for i in range(n - 1)]
    down = [(j, i) for i, j in up]
    return lax.ppermute(hi, axis, up), lax.ppermute(lo, axis, down)


def vm(*shape):
    return (shape, F32, VMEM)


def body(p_in, poro, lith_in, solid):
    p_in, poro, lith_in, solid = (
        pltpu.with_memory_space_constraint(a, HBM) for a in (p_in, poro, lith_in, solid)
    )
    slab = lax.axis_index("slab").astype(jnp.int32).reshape(1)
    block = (L, R, C)
    dma = pltpu.SemaphoreType.DMA
    p, lith, h, over, first, edges, shade = call(
        start_kernel, "start", [SMEM] + [HBM] * 4,
        [vm(*block), (block, jnp.int32, VMEM), vm(*block), vm(*block), vm(5 * R, C), vm(GR + 8, C), vm(L, C)],
        [VMEM(block, F32), SMEM((L,), F32), dma((3, STEPS)), dma(())],
    )(slab, p_in, poro, lith_in, solid)
    edges_in = lax.ppermute(edges, "slab", [(1, 2), (2, 1)])
    first_in = lax.ppermute(first, "slab", [(0, 1), (1, 0), (2, 3), (3, 2)])
    planes, both, *own_y = call(
        pack_own_kernel, "pack_own", [SMEM] + [VMEM] * 4,
        [vm(5 * R, C), vm(R, C), vm(GR, 128), vm(GR, 128)],
    )(slab, h, p, first, first_in)
    planes, both, edges_in = lax.optimization_barrier((planes, both, edges_in))
    planes_in = lax.ppermute(planes, "slab", [(1, 2), (2, 1)])
    both_in = lax.ppermute(both, "slab", [(0, 3)])
    wlo, whi = call(pack_y_kernel, "pack_y", [SMEM] + [VMEM] * 3, [vm(GR, 128)] * 2)(slab, edges_in, *own_y)
    ylo, yhi = pair("mapy", wlo, whi)
    (w,) = call(pre_kernel, "pre", [VMEM] * 3, [vm(5, L + 1, R, C)])(h, p, wlo)
    ylo, yhi, w = lax.optimization_barrier((ylo, yhi, w))
    vlo, vhi = call(pack_x_kernel, "pack_x", [SMEM] + [VMEM] * 6, [vm(40, C)] * 2)(
        slab, h, p, first_in, edges_in, ylo, yhi
    )
    xlo, xhi = pair("mapx", vlo, vhi)
    hbm = (block, F32, HBM)
    columns = VMEM((L + 2, R, 128), F32)
    yst, wy, wz, p1, iv, hz, pz, *outs = call(
        inner_kernel, "inner", [SMEM] + [VMEM] * 13,
        [vm(2, 4, GR, 128), vm(2, L, R, C), vm(2, R, C)] + [vm(L + 2, R, C)] * 2 + [vm(4, R, C)] * 2 + [hbm] * 3,
        [columns, columns, VMEM((L, R, 128), F32)] + [VMEM(block, F32)] * 3 + [dma((3, R // 8))],
    )(slab, shade, h, p, over, lith, first_in, planes_in, both_in, w, ylo, yhi, wlo, whi)
    return tuple(
        call(
            outer_kernel, "outer", [SMEM] + [VMEM] * 20 + [HBM] * 3, [hbm] * 3,
            [VMEM((2, 16, C), F32)] * 3
            + [VMEM((2, L + 2, 8, C), F32), VMEM((2, 2, L, 8, C), F32)]
            + [VMEM((2, L, 8, C), F32)] * 3 + [dma((2, 3))],
            {21: 0, 22: 1, 23: 2},
        )(
            slab, shade, h, p, over, lith, first_in, planes_in, both_in, xlo, xhi, vlo, vhi,
            w, yst, wy, wz, p1, iv, hz, pz, *outs,
        )
    )


def solution(mesh):
    spec = P("slab", "mapx", "mapy")
    return jax.shard_map(
        body, mesh=mesh, in_specs=(spec, spec, spec, P("slab")), out_specs=(spec,) * 3, check_vma=False
    )
```

```python
import math

import jax
import jax.numpy as jnp
from jax import lax
from jax.experimental import pallas as pl
from jax.experimental.pallas import tpu as pltpu
from jax.sharding import PartitionSpec as P

PHI_SURFACE = (0.45, 0.55, 0.65, 0.4)
ATHY_RATE = (0.25, 0.45, 0.8, 0.35)
MOB_BASE = (1.0, 0.0, -1.5, -0.5)
MOB_SLOPE = (6.0, 5.0, 8.0, 4.0)
GRAIN_DENSITY = (2.65, 2.68, 2.72, 2.71)
WATER_DENSITY = 1.03
SPECTRUM_MID = 1.0
SPECTRUM_HALF = 0.95
SIGMA_RATIO = SPECTRUM_MID / SPECTRUM_HALF
RHO_FIRST = 1.0 / SIGMA_RATIO
RHO_SECOND = 1.0 / (2.0 * SIGMA_RATIO - RHO_FIRST)

H_BASE = tuple(math.log(0.5) - b + 0.35 * s for b, s in zip(MOB_BASE, MOB_SLOPE))
H_SLOPE = tuple(-s for s in MOB_SLOPE)
ABSENT = 1e38

F32 = jnp.float32
L, R, C = 8, 96, 256
GR = 32
STEPS = 3
VMEM_LIMIT = 40 * 1024 * 1024


def recip(x):
    r = pl.reciprocal(x, approx=True)
    return r * (2.0 - x * r)


def present(h):
    return jnp.where(h == 0.0, ABSENT, h)


def classes(lith):
    return (lith & 1) == 1, lith >= 2


def pick(odd, upper, t):
    return jnp.where(upper, jnp.where(odd, t[3], t[2]), jnp.where(odd, t[1], t[0]))


def iota(shape, dim):
    return lax.broadcasted_iota(jnp.int32, shape, dim)


def roll(x, shift, axis):
    return pltpu.roll(x, shift % x.shape[axis], axis)


class Later:
    def __init__(self, every):
        self.every, self.count, self.kept = every, 0, []

    def put(self, *stores):
        self.kept.extend(stores)
        self.count += 1
        if self.count % self.every == 0:
            self.flush()

    def flush(self):
        for ref, at, value in self.kept:
            ref[at] = value
        self.kept = []


def packed(plane, layers, acc_lo, acc_hi):
    lane = iota((GR, 128), 1)
    for g in range(3):
        for z in layers:
            for arr in range(2):
                base = 40 * g + 4 * (z + 1) + 2 * arr
                here = (lane >= base) & (lane < base + 2)
                acc_lo = jnp.where(here, roll(plane(arr, z, g, slice(0, 128)), base, 1), acc_lo)
                acc_hi = jnp.where(here, roll(plane(arr, z, g, slice(C - 128, C)), base + 2, 1), acc_hi)
    return acc_lo, acc_hi


def start_kernel(slab, p_in, poro_in, lith_in, solid_in, p, lith, h, over, first, second, shade, poro, solid, sems, solid_sem):
    step = R // STEPS
    copies = []
    solid_copy = pltpu.make_async_copy(solid_in, solid, solid_sem)
    solid_copy.start()
    for k in range(STEPS):
        rows = slice(k * step, (k + 1) * step)
        group = [
            pltpu.make_async_copy(src.at[:, rows, :], dst.at[:, rows, :], sems.at[j, k])
            for j, (src, dst) in enumerate(((poro_in, poro), (lith_in, lith), (p_in, p)))
        ]
        for copy in group:
            copy.start()
        copies.append(group)
    solid_copy.wait()
    for z in range(L):
        shade[z : z + 1, :] = jnp.full((1, C), solid[z], F32)
    for k in range(STEPS):
        copies[k][0].wait()
        copies[k][1].wait()

        def chunk(i, carry, k=k):
            rows = pl.ds(pl.multiple_of(k * step + i * 16, 16), 16)
            total = jnp.zeros((16, C), F32)
            later = Later(4)
            for z in range(L):
                odd, upper = classes(lith[z, rows, :])
                phi = poro[z, rows, :]
                hz = jnp.exp(pick(odd, upper, H_BASE) + pick(odd, upper, H_SLOPE) * phi)
                load = (pick(odd, upper, GRAIN_DENSITY) + WATER_DENSITY * phi * recip(1.0 - phi)) * solid[z]
                later.put((h, (z, rows), hz), (over, (z, rows), total + 0.5 * load))
                total = total + load
            first[pl.ds(pl.multiple_of(4 * R + k * step + i * 16, 16), 16), :] = total
            return carry

        lax.fori_loop(0, step // 16, chunk, 0, unroll=True)
    for k in range(STEPS):
        copies[k][2].wait()
    is_odd = (slab[0] & 1) == 1
    o, i = jnp.where(is_odd, 0, L - 1), jnp.where(is_odd, 1, L - 2)
    first[0:R, :] = h[o]
    first[R : 2 * R, :] = p[o]
    first[2 * R : 3 * R, :] = h[i]
    first[3 * R : 4 * R, :] = p[i]
    o = jnp.where(is_odd, L - 1, 0)
    zero = jnp.zeros((GR, 128), F32)
    lo, hi = packed(lambda arr, z, g, cols: (h, p)[arr][o, GR * g : GR * g + GR, cols], (-1,), zero, zero)
    second[0:GR, 0:128] = lo
    second[0:GR, 128:256] = hi
    for k, (ref, row) in enumerate(((h, 0), (p, 0), (h, R - 1), (p, R - 1))):
        second[GR + k : GR + k + 1, :] = ref[o, row : row + 1, :]
    second[GR + 4 : GR + 8, :] = jnp.zeros((4, C), F32)


def pack_own_kernel(slab, h, p, mine, first, planes, both, lo, hi):
    is_odd = (slab[0] & 1) == 1
    zero = jnp.zeros((GR, 128), F32)
    own = packed(lambda arr, z, g, cols: (h, p)[arr][z, GR * g : GR * g + GR, cols], range(L), zero, zero)
    near = packed(
        lambda arr, z, g, cols: first[R * arr + GR * g : R * arr + GR * g + GR, cols], (-1,), zero, zero
    )
    for ref, a, b in zip((lo, hi), own, near):
        ref[...] = a + jnp.where(is_odd, b, roll(b, 4 * (L + 1), 1))
    total = mine[4 * R : 5 * R, :] + first[4 * R : 5 * R, :]
    o, i = jnp.where(is_odd, L - 1, 0), jnp.where(is_odd, L - 2, 1)
    planes[0:R, :] = h[o]
    planes[R : 2 * R, :] = p[o]
    planes[2 * R : 3 * R, :] = h[i]
    planes[3 * R : 4 * R, :] = p[i]
    planes[4 * R : 5 * R, :] = total
    both[...] = total


def pack_y_kernel(slab, edges, own_lo, own_hi, lo, hi):
    is_odd = (slab[0] & 1) == 1
    for ref, own, cols in ((lo, own_lo, slice(0, 128)), (hi, own_hi, slice(128, 256))):
        b = edges[0:GR, cols]
        ref[...] = own[...] + jnp.where(is_odd, roll(b, 4 * (L + 1), 1), b)


def pack_x_kernel(slab, h, p, first, edges, ylo, yhi, lo, hi):
    is_odd = (slab[0] & 1) == 1
    for s, (ref, o, i, yrow) in enumerate(((lo, 0, 1, 0), (hi, R - 1, R - 2, GR - 1))):
        for arr, own in ((0, h), (1, p)):
            at = R * arr + o
            k = GR + 2 * s + arr
            a, b = first[at : at + 1, :], edges[k : k + 1, :]
            top = 10 * arr
            ref[top : top + 1, :] = jnp.where(is_odd, a, b)
            for z in range(L):
                ref[top + 1 + z : top + 2 + z, :] = own[z, o : o + 1, :]
                ref[20 + L * arr + z : 21 + L * arr + z, :] = own[z, i : i + 1, :]
            ref[top + 9 : top + 10, :] = jnp.where(is_odd, b, a)
        ref[36:37, 0:128] = ylo[yrow : yrow + 1, :]
        ref[36:37, 128:256] = yhi[yrow : yrow + 1, :]
        ref[37:40, :] = jnp.zeros((3, C), F32)


def sums(h, p, beside):
    total, flow = None, None
    for hn, pn in beside:
        t = recip(h + hn)
        total = 1.0 + t if total is None else total + t
        flow = t * (pn - p) if flow is None else flow + t * (pn - p)
    return total, flow


def beside_y(msgs, owns):
    lane = iota((GR, 128), 1)
    sub = iota((GR, 128), 0)
    result = []
    for msg, own, o, i, w in ((msgs[0], owns[0], 1, 0, 0), (msgs[1], owns[1], 0, 1, 1)):
        m, v = msg[...], own[...]
        ho, po = present(roll(m, -o, 1)), roll(m, -o - 2, 1)
        hi_, pi_ = present(roll(m, -i, 1)), roll(m, -i - 2, 1)
        hw, pw = present(roll(v, -w, 1)), roll(v, -w - 2, 1)

        def along_x(f):
            u = roll(f, 1, 0)
            u = jnp.where(sub == 0, roll(u, 40, 1), u)
            d = roll(f, -1, 0)
            d = jnp.where(sub == GR - 1, roll(d, -40, 1), d)
            return u, d

        hu, hd = along_x(ho)
        pu, pd = along_x(po)
        hu = jnp.where((sub == 0) & (lane < 40), ABSENT, hu)
        hd = jnp.where((sub == GR - 1) & (lane >= 80), ABSENT, hd)
        total, flow = sums(ho, po, (
            (hi_, pi_), (hw, pw), (hu, pu), (hd, pd),
            (roll(ho, 4, 1), roll(po, 4, 1)), (roll(ho, -4, 1), roll(po, -4, 1)),
        ))
        result.append((ho, po, total, flow))
    return result


def beside_y_corners(msgs, yst):
    lane = iota((GR, 128), 1)
    sub = iota((GR, 128), 0)
    at_low = (sub == 0) & (lane < 40)
    at_high = (sub == GR - 1) & (lane >= 80)
    result = []
    for s, o, cols in ((0, 1, slice(0, 128)), (1, 0, slice(128, 256))):
        ho, po, total, flow = (yst[s, k] for k in range(4))

        def corner(k):
            low = jnp.broadcast_to(msgs[0][36:37, cols], (GR, 128))
            high = jnp.broadcast_to(msgs[1][36:37, cols], (GR, 128))
            return jnp.where(sub == 0, roll(low, -80 - k, 1), roll(high, 80 - k, 1))

        t = jnp.where(at_low | at_high, recip(ho + present(corner(o))), 0.0)
        result.append(po + (flow + t * (corner(o + 2) - po)) * recip(total + t))
    return result


def beside_x(msgs, owns, xh, xp, xq):
    lane = iota((16, C), 1)
    lane_x = iota((16, 128), 1)
    sub_x = iota((16, 128), 0)
    for s, row_lane in ((0, 80), (1, 0)):
        msg, own = msgs[s], owns[s]

        def rows10(ref, at):
            return jnp.concatenate([ref[at : at + 10, :], jnp.zeros((6, C), F32)], axis=0)

        def rows8(ref, at):
            return jnp.concatenate([jnp.zeros((1, C), F32), ref[at : at + 8, :], jnp.zeros((7, C), F32)], axis=0)

        ho, po = present(rows10(msg, 0)), rows10(msg, 10)
        hi_, pi_ = present(rows8(msg, 20)), rows8(msg, 28)
        hw, pw = present(rows10(own, 0)), rows10(own, 10)

        def corner(cols, k):
            row = jnp.broadcast_to(msg[36:37, cols], (16, 128))
            return jnp.sum(jnp.where(lane_x == row_lane + 4 * sub_x + k, row, 0.0), axis=1, keepdims=True)

        left, right = slice(0, 128), slice(128, 256)
        hl = jnp.where(lane == 0, present(corner(left, 1)), roll(ho, 1, 1))
        pl_ = jnp.where(lane == 0, corner(left, 3), roll(po, 1, 1))
        hr = jnp.where(lane == C - 1, present(corner(right, 0)), roll(ho, -1, 1))
        pr = jnp.where(lane == C - 1, corner(right, 2), roll(po, -1, 1))
        xh[s] = ho
        xp[s] = po
        total, flow = sums(ho, po, (
            (hi_, pi_), (hw, pw), (hl, pl_), (hr, pr),
            (roll(ho, 1, 0), roll(po, 1, 0)), (roll(ho, -1, 0), roll(po, -1, 0)),
        ))
        xq[s] = po + flow * recip(total)


def both_edges(lo, hi):
    lane = iota((GR, 128), 1)
    return jnp.where((lane & 3) == 0, lo, roll(hi, -1, 1))


def edge_columns(both, z, g):
    return roll(both, -40 * g - 4 * (z + 1), 1)


def around_x(before, here, after):
    sub = iota((8, C), 0)
    return roll(jnp.where(sub == 7, before, here), 1, 0), roll(jnp.where(sub == 0, after, here), -1, 0)


def around_y(here, edge):
    lane = iota((8, 128), 1)
    a, b = here[:, :128], here[:, 128:]
    ra, rb = roll(a, 1, 1), roll(b, 1, 1)
    left = jnp.concatenate([jnp.where(lane == 0, edge, ra), jnp.where(lane == 0, ra, rb)], axis=1)
    ra, rb = roll(a, -1, 1), roll(b, -1, 1)
    right = jnp.concatenate([jnp.where(lane == 127, rb, ra), jnp.where(lane == 127, edge, rb)], axis=1)
    return left, right


def second_chunk(qval, qedge, weight, pval, base, over, lith, shade, put):
    low = qval(-1)[1]
    qc = qval(0)
    flow = weight(0, 4) * (qc[1] - low)
    for z in range(L):
        qn = qval(z + 1)
        flow2 = weight(z + 1, 4) * (qn[1] - qc[1])
        q = qc[1]
        change = flow2 - flow
        for k, qb in enumerate(around_x(*qc) + around_y(q, qedge(z))):
            change = change + weight(z, k) * (qb - q)
        d0 = q - pval(z)
        pn = q + RHO_SECOND * RHO_FIRST * d0 + (2.0 * RHO_SECOND / SPECTRUM_HALF) * (change - d0) * weight(z, 5)
        stress = jnp.maximum(base + over(z) - pn, 0.0)
        odd, upper = classes(lith(z))
        new = pick(odd, upper, PHI_SURFACE) * jnp.exp(-pick(odd, upper, ATHY_RATE) * stress)
        put(z, pn, new, jnp.broadcast_to(shade[z : z + 1, :], (8, C)) * recip(1.0 - new))
        qc, flow = qn, flow2


def above_rows(slab, first, planes, both, rows):
    base = jnp.where((slab[0] & 1) == 1, first[rows(4 * R), :], 0.0)
    base = base + jnp.where(slab[0] == 2, planes[rows(4 * R), :], 0.0)
    return base + jnp.where(slab[0] == 3, both[rows(0), :], 0.0)


def at8(i):
    return pl.ds(pl.multiple_of(8 * i, 8), 8)


LAST = R // 8 - 1


def triples(h, p, hz, pz, i):
    here = (at8(jnp.maximum(i - 1, 0)), at8(i), at8(jnp.minimum(i + 1, LAST)))

    def at(z):
        return (h, p, z) if 0 <= z < L else (hz, pz, {-1: 0, L: 1, -2: 2, L + 1: 3}[z])

    def hval(z):
        ref, _, k = at(z)
        a, b, c = (ref[k, rows, :] for rows in here)
        return jnp.where(i == 0, ABSENT, a), b, jnp.where(i == LAST, ABSENT, c)

    def pval(z):
        _, ref, k = at(z)
        return tuple(ref[k, rows, :] for rows in here)

    return hval, pval


def pre_kernel(h, p, wlo, w):
    def chunk(i, carry):
        rows = at8(i)
        hval, pval = triples(h, p, None, None, i)
        hc, pc = hval(0), pval(0)
        t, flow = None, None
        later = Later(4)
        for z in range(L):
            stores = []
            total, change = 1.0, 0.0
            if z > 0:
                total, change = total + t, change - flow
            if z < L - 1:
                hn, pn = hval(z + 1), pval(z + 1)
                t = recip(hc[1] + hn[1])
                flow = t * (pn[1] - pc[1])
                stores.append((w, (2, z + 1, rows), t))
                total, change = total + t, change + flow
            for k, (hb, pb) in enumerate(zip(around_x(*hc), around_x(*pc))):
                u = recip(hc[1] + hb)
                stores.append((w, (k, z, rows), u))
                total = total + u
                change = change + u * (pb - pc[1])
            later.put(*stores, (w, (3, z, rows), total), (w, (4, z, rows), change))
            hc, pc = hn, pn
        later.flush()
        return carry

    lax.fori_loop(0, R // 8, chunk, 0, unroll=True)


def weight_of(w, wy, wz, z, k, rows):
    if k == 4 and z in (0, L):
        return wz[z // L, rows, :]
    return (w, w, wy, wy, w)[k][(0, 1, 0, 1, 2)[k], z, rows, :]


def inner_kernel(
    slab, shade, h, p, over, lith, first, planes, both, w, ylo, yhi, wlo, whi,
    yst, wy, wz, p1, iv, hz, pz, out0, out1, out2,
    eh, ep, eq, o0, o1, o2, sems,
):
    is_odd = (slab[0] & 1) == 1
    for k in range(2):
        for ref, at, fix in ((hz, 2 * k * R, present), (pz, (2 * k + 1) * R, lambda t: t)):
            a, b = first[at : at + R, :], planes[at : at + R, :]
            ref[2 * k] = fix(jnp.where(is_odd, a, b))
            ref[2 * k + 1] = fix(jnp.where(is_odd, b, a))
    lo, hi = beside_y((ylo, yhi), (wlo, whi))
    for s, values in enumerate((lo, hi)):
        for k in range(4):
            yst[s, k] = values[k]
    qlo, qhi = (v[1] + v[3] * recip(v[2]) for v in (lo, hi))
    hb, pb, qb = both_edges(lo[0], hi[0]), both_edges(lo[1], hi[1]), both_edges(qlo, qhi)
    for z in range(-1, L + 1):
        for g in range(3):
            rows = slice(GR * g, GR * g + GR)
            eh[z + 1, rows, :] = edge_columns(hb, z, g)
            ep[z + 1, rows, :] = edge_columns(pb, z, g)
            if 0 <= z < L:
                eq[z, rows, :] = edge_columns(qb, z, g)

    def chunk1(i, carry):
        rows = at8(i)
        hval, pval = triples(h, p, hz, pz, i)

        later = Later(4)

        def finish(z, hc, pc, total, change):
            stores = []
            for k, (hb, pb) in enumerate(zip(around_y(hc, eh[z + 1, rows, :]), around_y(pc, ep[z + 1, rows, :]))):
                u = recip(hc + hb)
                if 0 <= z < L:
                    stores.append((wy, (k, z, rows), u))
                total = total + u
                change = change + u * (pb - pc)
            inv = recip(total)
            later.put(*stores, (iv, (z + 1, rows), inv), (p1, (z + 1, rows), pc + change * inv))

        for z, out, own in ((-1, -2, 0), (L, L + 1, L - 1)):
            hc, pc = hval(z), pval(z)
            beside = [(hval(out)[1], pval(out)[1]), (hval(own)[1], pval(own)[1])]
            beside += list(zip(around_x(*hc), around_x(*pc)))
            finish(z, hc[1], pc[1], *sums(hc[1], pc[1], beside))
        for z in range(L):
            hc, pc, total, change = h[z, rows, :], p[z, rows, :], w[3, z, rows, :], w[4, z, rows, :]
            for k in ((0,) if z == 0 else (1,) if z == L - 1 else ()):
                t = recip(hc + hz[k, rows, :])
                later.kept.append((wz, (k, rows), t))
                total = total + t
                change = change + t * (pz[k, rows, :] - pc)
            finish(z, hc, pc, total, change)
        later.flush()
        return carry

    lax.fori_loop(0, R // 8, chunk1, 0, unroll=True)

    def moved(i):
        return [
            pltpu.make_async_copy(src.at[:, at8(i), :], dst.at[:, at8(i), :], sems.at[k, i])
            for k, (src, dst) in enumerate(((o0, out0), (o1, out1), (o2, out2)))
        ]

    def chunk2(i, carry):
        rows = at8(i)
        here = (at8(i - 1), rows, at8(i + 1))

        later = Later(4)

        def put(z, a, b, c):
            later.put((o0, (z, rows), a), (o1, (z, rows), b), (o2, (z, rows), c))

        second_chunk(
            lambda z: tuple(p1[z + 1, r, :] for r in here),
            lambda z: eq[z, rows, :],
            lambda z, k: iv[z + 1, rows, :] if k == 5 else weight_of(w, wy, wz, z, k, rows),
            lambda z: p[z, rows, :],
            above_rows(slab, first, planes, both, lambda top: pl.ds(pl.multiple_of(top + 8 * i, 8), 8)),
            lambda z: over[z, rows, :],
            lambda z: lith[z, rows, :],
            shade, put,
        )
        later.flush()
        for copy in moved(i):
            copy.start()
        return carry

    lax.fori_loop(1, LAST, chunk2, 0, unroll=True)

    def arrive(i, carry):
        for copy in moved(i):
            copy.wait()
        return carry

    lax.fori_loop(1, LAST, arrive, 0)


def outer_kernel(
    slab, shade, h, p, over, lith, first, planes, both, xlo, xhi, vlo, vhi,
    w, yst, wy, wz, p1, iv, hz, pz, in0, in1, in2,
    out0, out1, out2,
    xh, xp, xq, q1, wt, o0, o1, o2, sems,
):
    beside_x((xlo, xhi), (vlo, vhi), xh, xp, xq)
    columns = both_edges(*beside_y_corners((xlo, xhi), yst))
    sub = iota((8, C), 0)
    copies = []
    for s, top, g, part in ((0, 0, 0, slice(0, 8)), (1, R - 8, 2, slice(GR - 8, GR))):
        rows = slice(top, top + 8)
        near = slice(8, 16) if s == 0 else slice(R - 16, R - 8)
        edge = sub == (0 if s == 0 else 7)

        def strip(ref, z, s=s):
            return jnp.broadcast_to(ref[s, z + 1 : z + 2, :], (8, C))

        later = Later(5)
        for z in range(-1, L + 1):
            if 0 <= z < L:
                hc, pc = h[z, rows, :], p[z, rows, :]
            else:
                k = 0 if z < 0 else 1
                hc, pc = hz[k, rows, :], pz[k, rows, :]
            total = recip(iv[z + 1, rows, :])
            change = (p1[z + 1, rows, :] - pc) * total
            t = jnp.where(edge, recip(hc + strip(xh, z)), 0.0)
            inv = recip(total + t)
            stores = [(q1, (s, z + 1), pc + (change + t * (strip(xp, z) - pc)) * inv)]
            if 0 <= z < L:
                stores += [(wt, (s, 0, z), w[s, z, rows, :] + t), (wt, (s, 1, z), inv)]
            later.put(*stores)
        later.flush()

        def q_triple(z, s=s, near=near):
            here = q1[s, z + 1]
            if z < 0 or z >= L:
                return here, here, here
            inside = p1[z + 1, near, :]
            return (strip(xq, z), here, inside) if s == 0 else (inside, here, strip(xq, z))

        def weight(z, k, s=s, rows=rows):
            if k == s:
                return wt[s, 0, z]
            if k == 5:
                return wt[s, 1, z]
            return weight_of(w, wy, wz, z, k, rows)

        later = Later(4)

        def put(z, a, b, c, s=s, later=later):
            later.put((o0, (s, z), a), (o1, (s, z), b), (o2, (s, z), c))

        second_chunk(
            q_triple,
            lambda z: edge_columns(columns[part], z, g),
            weight,
            lambda z: p[z, rows, :],
            above_rows(slab, first, planes, both, lambda t: slice(t + top, t + top + 8)),
            lambda z: over[z, rows, :],
            lambda z: lith[z, rows, :],
            shade, put,
        )
        for k, (src, dst) in enumerate(((o0, out0), (o1, out1), (o2, out2))):
            copy = pltpu.make_async_copy(src.at[s], dst.at[:, rows, :], sems.at[s, k])
            copy.start()
            copies.append(copy)
    for copy in copies:
        copy.wait()


SMEM, VMEM, HBM = pltpu.SMEM, pltpu.VMEM, pltpu.HBM


COSTS = {
    "pre": pl.CostEstimate(flops=10**8, transcendentals=0, bytes_accessed=10**8),
    "pack_x": pl.CostEstimate(flops=10**10, transcendentals=0, bytes_accessed=10**10),
    "inner": pl.CostEstimate(flops=10**10, transcendentals=0, bytes_accessed=10**10),
}


def call(kernel, name, ins, outs, scratch=(), aliases=None):
    return pl.pallas_call(
        kernel,
        out_shape=[jax.ShapeDtypeStruct(s, t) for s, t, _ in outs],
        in_specs=[pl.BlockSpec(memory_space=m) for m in ins],
        out_specs=[pl.BlockSpec(memory_space=m) for _, _, m in outs],
        scratch_shapes=list(scratch),
        input_output_aliases=aliases or {},
        compiler_params=pltpu.CompilerParams(vmem_limit_bytes=VMEM_LIMIT),
        name=name,
        cost_estimate=COSTS.get(name),
    )


def pair(axis, lo, hi):
    n = lax.axis_size(axis)
    up = [(i, i + 1) for i in range(n - 1)]
    down = [(j, i) for i, j in up]
    return lax.ppermute(hi, axis, up), lax.ppermute(lo, axis, down)


def vm(*shape):
    return (shape, F32, VMEM)


def body(p_in, poro, lith_in, solid):
    p_in, poro, lith_in, solid = (
        pltpu.with_memory_space_constraint(a, HBM) for a in (p_in, poro, lith_in, solid)
    )
    slab = lax.axis_index("slab").astype(jnp.int32).reshape(1)
    block = (L, R, C)
    dma = pltpu.SemaphoreType.DMA
    p, lith, h, over, first, edges, shade = call(
        start_kernel, "start", [SMEM] + [HBM] * 4,
        [vm(*block), (block, jnp.int32, VMEM), vm(*block), vm(*block), vm(5 * R, C), vm(GR + 8, C), vm(L, C)],
        [VMEM(block, F32), SMEM((L,), F32), dma((3, STEPS)), dma(())],
    )(slab, p_in, poro, lith_in, solid)
    edges_in = lax.ppermute(edges, "slab", [(1, 2), (2, 1)])
    first_in = lax.ppermute(first, "slab", [(0, 1), (1, 0), (2, 3), (3, 2)])
    planes, both, *own_y = call(
        pack_own_kernel, "pack_own", [SMEM] + [VMEM] * 4,
        [vm(5 * R, C), vm(R, C), vm(GR, 128), vm(GR, 128)],
    )(slab, h, p, first, first_in)
    planes, both, edges_in = lax.optimization_barrier((planes, both, edges_in))
    planes_in = lax.ppermute(planes, "slab", [(1, 2), (2, 1)])
    both_in = lax.ppermute(both, "slab", [(0, 3)])
    wlo, whi = call(pack_y_kernel, "pack_y", [SMEM] + [VMEM] * 3, [vm(GR, 128)] * 2)(slab, edges_in, *own_y)
    ylo, yhi = pair("mapy", wlo, whi)
    (w,) = call(pre_kernel, "pre", [VMEM] * 3, [vm(5, L + 1, R, C)])(h, p, wlo)
    ylo, yhi, w = lax.optimization_barrier((ylo, yhi, w))
    vlo, vhi = call(pack_x_kernel, "pack_x", [SMEM] + [VMEM] * 6, [vm(40, C)] * 2)(
        slab, h, p, first_in, edges_in, ylo, yhi
    )
    xlo, xhi = pair("mapx", vlo, vhi)
    hbm = (block, F32, HBM)
    columns = VMEM((L + 2, R, 128), F32)
    yst, wy, wz, p1, iv, hz, pz, *outs = call(
        inner_kernel, "inner", [SMEM] + [VMEM] * 13,
        [vm(2, 4, GR, 128), vm(2, L, R, C), vm(2, R, C)] + [vm(L + 2, R, C)] * 2 + [vm(4, R, C)] * 2 + [hbm] * 3,
        [columns, columns, VMEM((L, R, 128), F32)] + [VMEM(block, F32)] * 3 + [dma((3, R // 8))],
    )(slab, shade, h, p, over, lith, first_in, planes_in, both_in, w, ylo, yhi, wlo, whi)
    return tuple(
        call(
            outer_kernel, "outer", [SMEM] + [VMEM] * 20 + [HBM] * 3, [hbm] * 3,
            [VMEM((2, 16, C), F32)] * 3
            + [VMEM((2, L + 2, 8, C), F32), VMEM((2, 2, L, 8, C), F32)]
            + [VMEM((2, L, 8, C), F32)] * 3 + [dma((2, 3))],
            {21: 0, 22: 1, 23: 2},
        )(
            slab, shade, h, p, over, lith, first_in, planes_in, both_in, xlo, xhi, vlo, vhi,
            w, yst, wy, wz, p1, iv, hz, pz, *outs,
        )
    )


def solution(mesh):
    spec = P("slab", "mapx", "mapy")
    return jax.shard_map(
        body, mesh=mesh, in_specs=(spec, spec, spec, P("slab")), out_specs=(spec,) * 3, check_vma=False
    )
```

```python
import math

import jax
import jax.numpy as jnp
from jax import lax
from jax.experimental import pallas as pl
from jax.experimental.pallas import tpu as pltpu
from jax.sharding import PartitionSpec as P

PHI_SURFACE = (0.45, 0.55, 0.65, 0.4)
ATHY_RATE = (0.25, 0.45, 0.8, 0.35)
MOB_BASE = (1.0, 0.0, -1.5, -0.5)
MOB_SLOPE = (6.0, 5.0, 8.0, 4.0)
GRAIN_DENSITY = (2.65, 2.68, 2.72, 2.71)
WATER_DENSITY = 1.03
SPECTRUM_MID = 1.0
SPECTRUM_HALF = 0.95
SIGMA_RATIO = SPECTRUM_MID / SPECTRUM_HALF
RHO_FIRST = 1.0 / SIGMA_RATIO
RHO_SECOND = 1.0 / (2.0 * SIGMA_RATIO - RHO_FIRST)

H_BASE = tuple(math.log(0.5) - b + 0.35 * s for b, s in zip(MOB_BASE, MOB_SLOPE))
H_SLOPE = tuple(-s for s in MOB_SLOPE)
ABSENT = 1e38

F32 = jnp.float32
L, R, C = 8, 96, 256
GR = 32
STEPS = 3
VMEM_LIMIT = 40 * 1024 * 1024


def recip(x):
    r = pl.reciprocal(x, approx=True)
    return r * (2.0 - x * r)


def present(h):
    return jnp.where(h == 0.0, ABSENT, h)


def classes(lith):
    return (lith & 1) == 1, lith >= 2


def pick(odd, upper, t):
    return jnp.where(upper, jnp.where(odd, t[3], t[2]), jnp.where(odd, t[1], t[0]))


def iota(shape, dim):
    return lax.broadcasted_iota(jnp.int32, shape, dim)


def roll(x, shift, axis):
    return pltpu.roll(x, shift % x.shape[axis], axis)


class Later:
    def __init__(self, every):
        self.every, self.count, self.kept = every, 0, []

    def put(self, *stores):
        self.kept.extend(stores)
        self.count += 1
        if self.count % self.every == 0:
            self.flush()

    def flush(self):
        for ref, at, value in self.kept:
            ref[at] = value
        self.kept = []


def packed(plane, layers, acc_lo, acc_hi):
    lane = iota((GR, 128), 1)
    for g in range(3):
        for z in layers:
            for arr in range(2):
                base = 40 * g + 4 * (z + 1) + 2 * arr
                here = (lane >= base) & (lane < base + 2)
                acc_lo = jnp.where(here, roll(plane(arr, z, g, slice(0, 128)), base, 1), acc_lo)
                acc_hi = jnp.where(here, roll(plane(arr, z, g, slice(C - 128, C)), base + 2, 1), acc_hi)
    return acc_lo, acc_hi


def start_kernel(slab, p_in, poro_in, lith_in, solid_in, p, lith, h, over, first, second, shade, poro, solid, sems, solid_sem):
    step = R // STEPS
    copies = []
    solid_copy = pltpu.make_async_copy(solid_in, solid, solid_sem)
    solid_copy.start()
    for k in range(STEPS):
        rows = slice(k * step, (k + 1) * step)
        group = [
            pltpu.make_async_copy(src.at[:, rows, :], dst.at[:, rows, :], sems.at[j, k])
            for j, (src, dst) in enumerate(((poro_in, poro), (lith_in, lith), (p_in, p)))
        ]
        for copy in group:
            copy.start()
        copies.append(group)
    solid_copy.wait()
    for z in range(L):
        shade[z : z + 1, :] = jnp.full((1, C), solid[z], F32)
    for k in range(STEPS):
        copies[k][0].wait()
        copies[k][1].wait()

        def chunk(i, carry, k=k):
            rows = pl.ds(pl.multiple_of(k * step + i * 16, 16), 16)
            total = jnp.zeros((16, C), F32)
            later = Later(4)
            for z in range(L):
                odd, upper = classes(lith[z, rows, :])
                phi = poro[z, rows, :]
                hz = jnp.exp(pick(odd, upper, H_BASE) + pick(odd, upper, H_SLOPE) * phi)
                load = (pick(odd, upper, GRAIN_DENSITY) + WATER_DENSITY * phi * recip(1.0 - phi)) * solid[z]
                later.put((h, (z, rows), hz), (over, (z, rows), total + 0.5 * load))
                total = total + load
            first[pl.ds(pl.multiple_of(4 * R + k * step + i * 16, 16), 16), :] = total
            return carry

        lax.fori_loop(0, step // 16, chunk, 0, unroll=True)
    for k in range(STEPS):
        copies[k][2].wait()
    is_odd = (slab[0] & 1) == 1
    o, i = jnp.where(is_odd, 0, L - 1), jnp.where(is_odd, 1, L - 2)
    first[0:R, :] = h[o]
    first[R : 2 * R, :] = p[o]
    first[2 * R : 3 * R, :] = h[i]
    first[3 * R : 4 * R, :] = p[i]
    o = jnp.where(is_odd, L - 1, 0)
    zero = jnp.zeros((GR, 128), F32)
    lo, hi = packed(lambda arr, z, g, cols: (h, p)[arr][o, GR * g : GR * g + GR, cols], (-1,), zero, zero)
    second[0:GR, 0:128] = lo
    second[0:GR, 128:256] = hi
    for k, (ref, row) in enumerate(((h, 0), (p, 0), (h, R - 1), (p, R - 1))):
        second[GR + k : GR + k + 1, :] = ref[o, row : row + 1, :]
    second[GR + 4 : GR + 8, :] = jnp.zeros((4, C), F32)


def pack_own_kernel(slab, h, p, mine, first, planes, both, lo, hi):
    is_odd = (slab[0] & 1) == 1
    zero = jnp.zeros((GR, 128), F32)
    own = packed(lambda arr, z, g, cols: (h, p)[arr][z, GR * g : GR * g + GR, cols], range(L), zero, zero)
    near = packed(
        lambda arr, z, g, cols: first[R * arr + GR * g : R * arr + GR * g + GR, cols], (-1,), zero, zero
    )
    for ref, a, b in zip((lo, hi), own, near):
        ref[...] = a + jnp.where(is_odd, b, roll(b, 4 * (L + 1), 1))
    total = mine[4 * R : 5 * R, :] + first[4 * R : 5 * R, :]
    o, i = jnp.where(is_odd, L - 1, 0), jnp.where(is_odd, L - 2, 1)
    planes[0:R, :] = h[o]
    planes[R : 2 * R, :] = p[o]
    planes[2 * R : 3 * R, :] = h[i]
    planes[3 * R : 4 * R, :] = p[i]
    planes[4 * R : 5 * R, :] = total
    both[...] = total


def pack_y_kernel(slab, edges, own_lo, own_hi, lo, hi):
    is_odd = (slab[0] & 1) == 1
    for ref, own, cols in ((lo, own_lo, slice(0, 128)), (hi, own_hi, slice(128, 256))):
        b = edges[0:GR, cols]
        ref[...] = own[...] + jnp.where(is_odd, roll(b, 4 * (L + 1), 1), b)


def pack_x_kernel(slab, h, p, first, edges, ylo, yhi, lo, hi):
    is_odd = (slab[0] & 1) == 1
    for s, (ref, o, i, yrow) in enumerate(((lo, 0, 1, 0), (hi, R - 1, R - 2, GR - 1))):
        for arr, own in ((0, h), (1, p)):
            at = R * arr + o
            k = GR + 2 * s + arr
            a, b = first[at : at + 1, :], edges[k : k + 1, :]
            top = 10 * arr
            ref[top : top + 1, :] = jnp.where(is_odd, a, b)
            for z in range(L):
                ref[top + 1 + z : top + 2 + z, :] = own[z, o : o + 1, :]
                ref[20 + L * arr + z : 21 + L * arr + z, :] = own[z, i : i + 1, :]
            ref[top + 9 : top + 10, :] = jnp.where(is_odd, b, a)
        ref[36:37, 0:128] = ylo[yrow : yrow + 1, :]
        ref[36:37, 128:256] = yhi[yrow : yrow + 1, :]
        ref[37:40, :] = jnp.zeros((3, C), F32)


def sums(h, p, beside):
    total, flow = None, None
    for hn, pn in beside:
        t = recip(h + hn)
        total = 1.0 + t if total is None else total + t
        flow = t * (pn - p) if flow is None else flow + t * (pn - p)
    return total, flow


def beside_y(msgs, owns):
    lane = iota((GR, 128), 1)
    sub = iota((GR, 128), 0)
    result = []
    for msg, own, o, i, w in ((msgs[0], owns[0], 1, 0, 0), (msgs[1], owns[1], 0, 1, 1)):
        m, v = msg[...], own[...]
        ho, po = present(roll(m, -o, 1)), roll(m, -o - 2, 1)
        hi_, pi_ = present(roll(m, -i, 1)), roll(m, -i - 2, 1)
        hw, pw = present(roll(v, -w, 1)), roll(v, -w - 2, 1)

        def along_x(f):
            u = roll(f, 1, 0)
            u = jnp.where(sub == 0, roll(u, 40, 1), u)
            d = roll(f, -1, 0)
            d = jnp.where(sub == GR - 1, roll(d, -40, 1), d)
            return u, d

        hu, hd = along_x(ho)
        pu, pd = along_x(po)
        hu = jnp.where((sub == 0) & (lane < 40), ABSENT, hu)
        hd = jnp.where((sub == GR - 1) & (lane >= 80), ABSENT, hd)
        total, flow = sums(ho, po, (
            (hi_, pi_), (hw, pw), (hu, pu), (hd, pd),
            (roll(ho, 4, 1), roll(po, 4, 1)), (roll(ho, -4, 1), roll(po, -4, 1)),
        ))
        result.append((ho, po, total, flow))
    return result


def beside_y_corners(msgs, yst):
    lane = iota((GR, 128), 1)
    sub = iota((GR, 128), 0)
    at_low = (sub == 0) & (lane < 40)
    at_high = (sub == GR - 1) & (lane >= 80)
    result = []
    for s, o, cols in ((0, 1, slice(0, 128)), (1, 0, slice(128, 256))):
        ho, po, total, flow = (yst[s, k] for k in range(4))

        def corner(k):
            low = jnp.broadcast_to(msgs[0][36:37, cols], (GR, 128))
            high = jnp.broadcast_to(msgs[1][36:37, cols], (GR, 128))
            return jnp.where(sub == 0, roll(low, -80 - k, 1), roll(high, 80 - k, 1))

        t = jnp.where(at_low | at_high, recip(ho + present(corner(o))), 0.0)
        result.append(po + (flow + t * (corner(o + 2) - po)) * recip(total + t))
    return result


def beside_x(msgs, owns, xh, xp, xq):
    lane = iota((16, C), 1)
    lane_x = iota((16, 128), 1)
    sub_x = iota((16, 128), 0)
    for s, row_lane in ((0, 80), (1, 0)):
        msg, own = msgs[s], owns[s]

        def rows10(ref, at):
            return jnp.concatenate([ref[at : at + 10, :], jnp.zeros((6, C), F32)], axis=0)

        def rows8(ref, at):
            return jnp.concatenate([jnp.zeros((1, C), F32), ref[at : at + 8, :], jnp.zeros((7, C), F32)], axis=0)

        ho, po = present(rows10(msg, 0)), rows10(msg, 10)
        hi_, pi_ = present(rows8(msg, 20)), rows8(msg, 28)
        hw, pw = present(rows10(own, 0)), rows10(own, 10)

        def corner(cols, k):
            row = jnp.broadcast_to(msg[36:37, cols], (16, 128))
            return jnp.sum(jnp.where(lane_x == row_lane + 4 * sub_x + k, row, 0.0), axis=1, keepdims=True)

        left, right = slice(0, 128), slice(128, 256)
        hl = jnp.where(lane == 0, present(corner(left, 1)), roll(ho, 1, 1))
        pl_ = jnp.where(lane == 0, corner(left, 3), roll(po, 1, 1))
        hr = jnp.where(lane == C - 1, present(corner(right, 0)), roll(ho, -1, 1))
        pr = jnp.where(lane == C - 1, corner(right, 2), roll(po, -1, 1))
        xh[s] = ho
        xp[s] = po
        total, flow = sums(ho, po, (
            (hi_, pi_), (hw, pw), (hl, pl_), (hr, pr),
            (roll(ho, 1, 0), roll(po, 1, 0)), (roll(ho, -1, 0), roll(po, -1, 0)),
        ))
        xq[s] = po + flow * recip(total)


def both_edges(lo, hi):
    lane = iota((GR, 128), 1)
    return jnp.where((lane & 3) == 0, lo, roll(hi, -1, 1))


def edge_columns(both, z, g):
    return roll(both, -40 * g - 4 * (z + 1), 1)


def around_x(before, here, after):
    sub = iota((8, C), 0)
    return roll(jnp.where(sub == 7, before, here), 1, 0), roll(jnp.where(sub == 0, after, here), -1, 0)


def around_y(here, edge):
    lane = iota((8, 128), 1)
    a, b = here[:, :128], here[:, 128:]
    ra, rb = roll(a, 1, 1), roll(b, 1, 1)
    left = jnp.concatenate([jnp.where(lane == 0, edge, ra), jnp.where(lane == 0, ra, rb)], axis=1)
    ra, rb = roll(a, -1, 1), roll(b, -1, 1)
    right = jnp.concatenate([jnp.where(lane == 127, rb, ra), jnp.where(lane == 127, edge, rb)], axis=1)
    return left, right


def second_chunk(qval, qedge, weight, pval, base, over, lith, shade, put):
    low = qval(-1)[1]
    qc = qval(0)
    flow = weight(0, 4) * (qc[1] - low)
    for z in range(L):
        qn = qval(z + 1)
        flow2 = weight(z + 1, 4) * (qn[1] - qc[1])
        q = qc[1]
        change = flow2 - flow
        for k, qb in enumerate(around_x(*qc) + around_y(q, qedge(z))):
            change = change + weight(z, k) * (qb - q)
        d0 = q - pval(z)
        pn = q + RHO_SECOND * RHO_FIRST * d0 + (2.0 * RHO_SECOND / SPECTRUM_HALF) * (change - d0) * weight(z, 5)
        stress = jnp.maximum(base + over(z) - pn, 0.0)
        odd, upper = classes(lith(z))
        new = pick(odd, upper, PHI_SURFACE) * jnp.exp(-pick(odd, upper, ATHY_RATE) * stress)
        put(z, pn, new, jnp.broadcast_to(shade[z : z + 1, :], (8, C)) * recip(1.0 - new))
        qc, flow = qn, flow2


def above_rows(slab, first, planes, both, rows):
    base = jnp.where((slab[0] & 1) == 1, first[rows(4 * R), :], 0.0)
    base = base + jnp.where(slab[0] == 2, planes[rows(4 * R), :], 0.0)
    return base + jnp.where(slab[0] == 3, both[rows(0), :], 0.0)


def at8(i):
    return pl.ds(pl.multiple_of(8 * i, 8), 8)


LAST = R // 8 - 1


def triples(h, p, hz, pz, i):
    here = (at8(jnp.maximum(i - 1, 0)), at8(i), at8(jnp.minimum(i + 1, LAST)))

    def at(z):
        return (h, p, z) if 0 <= z < L else (hz, pz, {-1: 0, L: 1, -2: 2, L + 1: 3}[z])

    def hval(z):
        ref, _, k = at(z)
        a, b, c = (ref[k, rows, :] for rows in here)
        return jnp.where(i == 0, ABSENT, a), b, jnp.where(i == LAST, ABSENT, c)

    def pval(z):
        _, ref, k = at(z)
        return tuple(ref[k, rows, :] for rows in here)

    return hval, pval


def pre_kernel(h, p, w):
    def chunk(i, carry):
        rows = at8(i)
        hval, pval = triples(h, p, None, None, i)
        hc, pc = hval(0), pval(0)
        t, flow = None, None
        later = Later(4)
        for z in range(L):
            stores = []
            total, change = 1.0, 0.0
            if z > 0:
                total, change = total + t, change - flow
            if z < L - 1:
                hn, pn = hval(z + 1), pval(z + 1)
                t = recip(hc[1] + hn[1])
                flow = t * (pn[1] - pc[1])
                stores.append((w, (2, z + 1, rows), t))
                total, change = total + t, change + flow
            for k, (hb, pb) in enumerate(zip(around_x(*hc), around_x(*pc))):
                u = recip(hc[1] + hb)
                stores.append((w, (k, z, rows), u))
                total = total + u
                change = change + u * (pb - pc[1])
            later.put(*stores, (w, (3, z, rows), total), (w, (4, z, rows), change))
            hc, pc = hn, pn
        later.flush()
        return carry

    lax.fori_loop(0, R // 8, chunk, 0, unroll=True)


def weight_of(w, wy, wz, z, k, rows):
    if k == 4 and z in (0, L):
        return wz[z // L, rows, :]
    return (w, w, wy, wy, w)[k][(0, 1, 0, 1, 2)[k], z, rows, :]


def inner_kernel(
    slab, shade, h, p, over, lith, first, planes, both, w, ylo, yhi, wlo, whi,
    yst, wy, wz, p1, iv, hz, pz, out0, out1, out2,
    eh, ep, eq, o0, o1, o2, sems,
):
    is_odd = (slab[0] & 1) == 1
    for k in range(2):
        for ref, at, fix in ((hz, 2 * k * R, present), (pz, (2 * k + 1) * R, lambda t: t)):
            a, b = first[at : at + R, :], planes[at : at + R, :]
            ref[2 * k] = fix(jnp.where(is_odd, a, b))
            ref[2 * k + 1] = fix(jnp.where(is_odd, b, a))
    lo, hi = beside_y((ylo, yhi), (wlo, whi))
    for s, values in enumerate((lo, hi)):
        for k in range(4):
            yst[s, k] = values[k]
    qlo, qhi = (v[1] + v[3] * recip(v[2]) for v in (lo, hi))
    hb, pb, qb = both_edges(lo[0], hi[0]), both_edges(lo[1], hi[1]), both_edges(qlo, qhi)
    for z in range(-1, L + 1):
        for g in range(3):
            rows = slice(GR * g, GR * g + GR)
            eh[z + 1, rows, :] = edge_columns(hb, z, g)
            ep[z + 1, rows, :] = edge_columns(pb, z, g)
            if 0 <= z < L:
                eq[z, rows, :] = edge_columns(qb, z, g)

    def chunk1(i, carry):
        rows = at8(i)
        hval, pval = triples(h, p, hz, pz, i)

        later = Later(4)

        def finish(z, hc, pc, total, change):
            stores = []
            for k, (hb, pb) in enumerate(zip(around_y(hc, eh[z + 1, rows, :]), around_y(pc, ep[z + 1, rows, :]))):
                u = recip(hc + hb)
                if 0 <= z < L:
                    stores.append((wy, (k, z, rows), u))
                total = total + u
                change = change + u * (pb - pc)
            inv = recip(total)
            later.put(*stores, (iv, (z + 1, rows), inv), (p1, (z + 1, rows), pc + change * inv))

        for z, out, own in ((-1, -2, 0), (L, L + 1, L - 1)):
            hc, pc = hval(z), pval(z)
            beside = [(hval(out)[1], pval(out)[1]), (hval(own)[1], pval(own)[1])]
            beside += list(zip(around_x(*hc), around_x(*pc)))
            finish(z, hc[1], pc[1], *sums(hc[1], pc[1], beside))
        for z in range(L):
            hc, pc, total, change = h[z, rows, :], p[z, rows, :], w[3, z, rows, :], w[4, z, rows, :]
            for k in ((0,) if z == 0 else (1,) if z == L - 1 else ()):
                t = recip(hc + hz[k, rows, :])
                later.kept.append((wz, (k, rows), t))
                total = total + t
                change = change + t * (pz[k, rows, :] - pc)
            finish(z, hc, pc, total, change)
        later.flush()
        return carry

    lax.fori_loop(0, R // 8, chunk1, 0, unroll=True)

    def moved(i):
        return [
            pltpu.make_async_copy(src.at[:, at8(i), :], dst.at[:, at8(i), :], sems.at[k, i])
            for k, (src, dst) in enumerate(((o0, out0), (o1, out1), (o2, out2)))
        ]

    def chunk2(i, carry):
        rows = at8(i)
        here = (at8(i - 1), rows, at8(i + 1))

        later = Later(4)

        def put(z, a, b, c):
            later.put((o0, (z, rows), a), (o1, (z, rows), b), (o2, (z, rows), c))

        second_chunk(
            lambda z: tuple(p1[z + 1, r, :] for r in here),
            lambda z: eq[z, rows, :],
            lambda z, k: iv[z + 1, rows, :] if k == 5 else weight_of(w, wy, wz, z, k, rows),
            lambda z: p[z, rows, :],
            above_rows(slab, first, planes, both, lambda top: pl.ds(pl.multiple_of(top + 8 * i, 8), 8)),
            lambda z: over[z, rows, :],
            lambda z: lith[z, rows, :],
            shade, put,
        )
        later.flush()
        for copy in moved(i):
            copy.start()
        return carry

    lax.fori_loop(1, LAST, chunk2, 0, unroll=True)

    def arrive(i, carry):
        for copy in moved(i):
            copy.wait()
        return carry

    lax.fori_loop(1, LAST, arrive, 0)


def outer_kernel(
    slab, shade, h, p, over, lith, first, planes, both, xlo, xhi, vlo, vhi,
    w, yst, wy, wz, p1, iv, hz, pz, in0, in1, in2,
    out0, out1, out2,
    xh, xp, xq, q1, wt, o0, o1, o2, sems,
):
    beside_x((xlo, xhi), (vlo, vhi), xh, xp, xq)
    columns = both_edges(*beside_y_corners((xlo, xhi), yst))
    sub = iota((8, C), 0)
    copies = []
    for s, top, g, part in ((0, 0, 0, slice(0, 8)), (1, R - 8, 2, slice(GR - 8, GR))):
        rows = slice(top, top + 8)
        near = slice(8, 16) if s == 0 else slice(R - 16, R - 8)
        edge = sub == (0 if s == 0 else 7)

        def strip(ref, z, s=s):
            return jnp.broadcast_to(ref[s, z + 1 : z + 2, :], (8, C))

        later = Later(5)
        for z in range(-1, L + 1):
            if 0 <= z < L:
                hc, pc = h[z, rows, :], p[z, rows, :]
            else:
                k = 0 if z < 0 else 1
                hc, pc = hz[k, rows, :], pz[k, rows, :]
            total = recip(iv[z + 1, rows, :])
            change = (p1[z + 1, rows, :] - pc) * total
            t = jnp.where(edge, recip(hc + strip(xh, z)), 0.0)
            inv = recip(total + t)
            stores = [(q1, (s, z + 1), pc + (change + t * (strip(xp, z) - pc)) * inv)]
            if 0 <= z < L:
                stores += [(wt, (s, 0, z), w[s, z, rows, :] + t), (wt, (s, 1, z), inv)]
            later.put(*stores)
        later.flush()

        def q_triple(z, s=s, near=near):
            here = q1[s, z + 1]
            if z < 0 or z >= L:
                return here, here, here
            inside = p1[z + 1, near, :]
            return (strip(xq, z), here, inside) if s == 0 else (inside, here, strip(xq, z))

        def weight(z, k, s=s, rows=rows):
            if k == s:
                return wt[s, 0, z]
            if k == 5:
                return wt[s, 1, z]
            return weight_of(w, wy, wz, z, k, rows)

        later = Later(4)

        def put(z, a, b, c, s=s, later=later):
            later.put((o0, (s, z), a), (o1, (s, z), b), (o2, (s, z), c))

        second_chunk(
            q_triple,
            lambda z: edge_columns(columns[part], z, g),
            weight,
            lambda z: p[z, rows, :],
            above_rows(slab, first, planes, both, lambda t: slice(t + top, t + top + 8)),
            lambda z: over[z, rows, :],
            lambda z: lith[z, rows, :],
            shade, put,
        )
        for k, (src, dst) in enumerate(((o0, out0), (o1, out1), (o2, out2))):
            copy = pltpu.make_async_copy(src.at[s], dst.at[:, rows, :], sems.at[s, k])
            copy.start()
            copies.append(copy)
    for copy in copies:
        copy.wait()


SMEM, VMEM, HBM = pltpu.SMEM, pltpu.VMEM, pltpu.HBM


COSTS = {
    "pre": pl.CostEstimate(flops=10**8, transcendentals=0, bytes_accessed=10**8),
    "pack_x": pl.CostEstimate(flops=10**10, transcendentals=0, bytes_accessed=10**10),
    "inner": pl.CostEstimate(flops=10**10, transcendentals=0, bytes_accessed=10**10),
}


def call(kernel, name, ins, outs, scratch=(), aliases=None):
    return pl.pallas_call(
        kernel,
        out_shape=[jax.ShapeDtypeStruct(s, t) for s, t, _ in outs],
        in_specs=[pl.BlockSpec(memory_space=m) for m in ins],
        out_specs=[pl.BlockSpec(memory_space=m) for _, _, m in outs],
        scratch_shapes=list(scratch),
        input_output_aliases=aliases or {},
        compiler_params=pltpu.CompilerParams(vmem_limit_bytes=VMEM_LIMIT),
        name=name,
        cost_estimate=COSTS.get(name),
    )


def pair(axis, lo, hi):
    n = lax.axis_size(axis)
    up = [(i, i + 1) for i in range(n - 1)]
    down = [(j, i) for i, j in up]
    return lax.ppermute(hi, axis, up), lax.ppermute(lo, axis, down)


def vm(*shape):
    return (shape, F32, VMEM)


def body(p_in, poro, lith_in, solid):
    p_in, poro, lith_in, solid = (
        pltpu.with_memory_space_constraint(a, HBM) for a in (p_in, poro, lith_in, solid)
    )
    slab = lax.axis_index("slab").astype(jnp.int32).reshape(1)
    block = (L, R, C)
    dma = pltpu.SemaphoreType.DMA
    p, lith, h, over, first, edges, shade = call(
        start_kernel, "start", [SMEM] + [HBM] * 4,
        [vm(*block), (block, jnp.int32, VMEM), vm(*block), vm(*block), vm(5 * R, C), vm(GR + 8, C), vm(L, C)],
        [VMEM(block, F32), SMEM((L,), F32), dma((3, STEPS)), dma(())],
    )(slab, p_in, poro, lith_in, solid)
    edges_in = lax.ppermute(edges, "slab", [(1, 2), (2, 1)])
    first_in = lax.ppermute(first, "slab", [(0, 1), (1, 0), (2, 3), (3, 2)])
    planes, both, *own_y = call(
        pack_own_kernel, "pack_own", [SMEM] + [VMEM] * 4,
        [vm(5 * R, C), vm(R, C), vm(GR, 128), vm(GR, 128)],
    )(slab, h, p, first, first_in)
    planes, both, edges_in = lax.optimization_barrier((planes, both, edges_in))
    planes_in = lax.ppermute(planes, "slab", [(1, 2), (2, 1)])
    both_in = lax.ppermute(both, "slab", [(0, 3)])
    (w,) = call(pre_kernel, "pre", [VMEM] * 2, [vm(5, L + 1, R, C)])(h, p)
    edges_in, w = lax.optimization_barrier((edges_in, w))
    wlo, whi = call(pack_y_kernel, "pack_y", [SMEM] + [VMEM] * 3, [vm(GR, 128)] * 2)(slab, edges_in, *own_y)
    ylo, yhi = pair("mapy", wlo, whi)
    vlo, vhi = call(pack_x_kernel, "pack_x", [SMEM] + [VMEM] * 6, [vm(40, C)] * 2)(
        slab, h, p, first_in, edges_in, ylo, yhi
    )
    xlo, xhi = pair("mapx", vlo, vhi)
    hbm = (block, F32, HBM)
    columns = VMEM((L + 2, R, 128), F32)
    yst, wy, wz, p1, iv, hz, pz, *outs = call(
        inner_kernel, "inner", [SMEM] + [VMEM] * 13,
        [vm(2, 4, GR, 128), vm(2, L, R, C), vm(2, R, C)] + [vm(L + 2, R, C)] * 2 + [vm(4, R, C)] * 2 + [hbm] * 3,
        [columns, columns, VMEM((L, R, 128), F32)] + [VMEM(block, F32)] * 3 + [dma((3, R // 8))],
    )(slab, shade, h, p, over, lith, first_in, planes_in, both_in, w, ylo, yhi, wlo, whi)
    return tuple(
        call(
            outer_kernel, "outer", [SMEM] + [VMEM] * 20 + [HBM] * 3, [hbm] * 3,
            [VMEM((2, 16, C), F32)] * 3
            + [VMEM((2, L + 2, 8, C), F32), VMEM((2, 2, L, 8, C), F32)]
            + [VMEM((2, L, 8, C), F32)] * 3 + [dma((2, 3))],
            {21: 0, 22: 1, 23: 2},
        )(
            slab, shade, h, p, over, lith, first_in, planes_in, both_in, xlo, xhi, vlo, vhi,
            w, yst, wy, wz, p1, iv, hz, pz, *outs,
        )
    )


def solution(mesh):
    spec = P("slab", "mapx", "mapy")
    return jax.shard_map(
        body, mesh=mesh, in_specs=(spec, spec, spec, P("slab")), out_specs=(spec,) * 3, check_vma=False
    )
```

```python
import math

import jax
import jax.numpy as jnp
from jax import lax
from jax.experimental import pallas as pl
from jax.experimental.pallas import tpu as pltpu
from jax.sharding import PartitionSpec as P

PHI_SURFACE = (0.45, 0.55, 0.65, 0.4)
ATHY_RATE = (0.25, 0.45, 0.8, 0.35)
MOB_BASE = (1.0, 0.0, -1.5, -0.5)
MOB_SLOPE = (6.0, 5.0, 8.0, 4.0)
GRAIN_DENSITY = (2.65, 2.68, 2.72, 2.71)
WATER_DENSITY = 1.03
SPECTRUM_MID = 1.0
SPECTRUM_HALF = 0.95
SIGMA_RATIO = SPECTRUM_MID / SPECTRUM_HALF
RHO_FIRST = 1.0 / SIGMA_RATIO
RHO_SECOND = 1.0 / (2.0 * SIGMA_RATIO - RHO_FIRST)

H_BASE = tuple(math.log(0.5) - b + 0.35 * s for b, s in zip(MOB_BASE, MOB_SLOPE))
H_SLOPE = tuple(-s for s in MOB_SLOPE)
ABSENT = 1e38

F32 = jnp.float32
L, R, C = 8, 96, 256
GR = 32
STEPS = 3
VMEM_LIMIT = 40 * 1024 * 1024


def recip(x):
    r = pl.reciprocal(x, approx=True)
    return r * (2.0 - x * r)


def present(h):
    return jnp.where(h == 0.0, ABSENT, h)


def classes(lith):
    return (lith & 1) == 1, lith >= 2


def pick(odd, upper, t):
    return jnp.where(upper, jnp.where(odd, t[3], t[2]), jnp.where(odd, t[1], t[0]))


def iota(shape, dim):
    return lax.broadcasted_iota(jnp.int32, shape, dim)


def roll(x, shift, axis):
    return pltpu.roll(x, shift % x.shape[axis], axis)


class Later:
    def __init__(self, every):
        self.every, self.count, self.kept = every, 0, []

    def put(self, *stores):
        self.kept.extend(stores)
        self.count += 1
        if self.count % self.every == 0:
            self.flush()

    def flush(self):
        for ref, at, value in self.kept:
            ref[at] = value
        self.kept = []


def packed(plane, layers, acc_lo, acc_hi):
    lane = iota((GR, 128), 1)
    for g in range(3):
        for z in layers:
            for arr in range(2):
                base = 40 * g + 4 * (z + 1) + 2 * arr
                here = (lane >= base) & (lane < base + 2)
                acc_lo = jnp.where(here, roll(plane(arr, z, g, slice(0, 128)), base, 1), acc_lo)
                acc_hi = jnp.where(here, roll(plane(arr, z, g, slice(C - 128, C)), base + 2, 1), acc_hi)
    return acc_lo, acc_hi


def start_kernel(slab, p_in, poro_in, lith_in, solid_in, p, lith, h, over, first, second, shade, poro, solid, sems, solid_sem):
    step = R // STEPS
    copies = []
    solid_copy = pltpu.make_async_copy(solid_in, solid, solid_sem)
    solid_copy.start()
    for k in range(STEPS):
        rows = slice(k * step, (k + 1) * step)
        group = [
            pltpu.make_async_copy(src.at[:, rows, :], dst.at[:, rows, :], sems.at[j, k])
            for j, (src, dst) in enumerate(((poro_in, poro), (lith_in, lith), (p_in, p)))
        ]
        for copy in group:
            copy.start()
        copies.append(group)
    solid_copy.wait()
    for z in range(L):
        shade[z : z + 1, :] = jnp.full((1, C), solid[z], F32)
    for k in range(STEPS):
        copies[k][0].wait()
        copies[k][1].wait()

        def chunk(i, carry, k=k):
            rows = pl.ds(pl.multiple_of(k * step + i * 16, 16), 16)
            total = jnp.zeros((16, C), F32)
            later = Later(4)
            for z in range(L):
                odd, upper = classes(lith[z, rows, :])
                phi = poro[z, rows, :]
                hz = jnp.exp(pick(odd, upper, H_BASE) + pick(odd, upper, H_SLOPE) * phi)
                load = (pick(odd, upper, GRAIN_DENSITY) + WATER_DENSITY * phi * recip(1.0 - phi)) * solid[z]
                later.put((h, (z, rows), hz), (over, (z, rows), total + 0.5 * load))
                total = total + load
            first[pl.ds(pl.multiple_of(4 * R + k * step + i * 16, 16), 16), :] = total
            return carry

        lax.fori_loop(0, step // 16, chunk, 0, unroll=True)
    for k in range(STEPS):
        copies[k][2].wait()
    is_odd = (slab[0] & 1) == 1
    o, i = jnp.where(is_odd, 0, L - 1), jnp.where(is_odd, 1, L - 2)
    first[0:R, :] = h[o]
    first[R : 2 * R, :] = p[o]
    first[2 * R : 3 * R, :] = h[i]
    first[3 * R : 4 * R, :] = p[i]
    o = jnp.where(is_odd, L - 1, 0)
    zero = jnp.zeros((GR, 128), F32)
    lo, hi = packed(lambda arr, z, g, cols: (h, p)[arr][o, GR * g : GR * g + GR, cols], (-1,), zero, zero)
    second[0:GR, 0:128] = lo
    second[0:GR, 128:256] = hi
    for k, (ref, row) in enumerate(((h, 0), (p, 0), (h, R - 1), (p, R - 1))):
        second[GR + k : GR + k + 1, :] = ref[o, row : row + 1, :]
    second[GR + 4 : GR + 8, :] = jnp.zeros((4, C), F32)


def pack_own_kernel(slab, h, p, mine, first, planes, both, lo, hi):
    is_odd = (slab[0] & 1) == 1
    zero = jnp.zeros((GR, 128), F32)
    own = packed(lambda arr, z, g, cols: (h, p)[arr][z, GR * g : GR * g + GR, cols], range(L), zero, zero)
    near = packed(
        lambda arr, z, g, cols: first[R * arr + GR * g : R * arr + GR * g + GR, cols], (-1,), zero, zero
    )
    for ref, a, b in zip((lo, hi), own, near):
        ref[...] = a + jnp.where(is_odd, b, roll(b, 4 * (L + 1), 1))
    total = mine[4 * R : 5 * R, :] + first[4 * R : 5 * R, :]
    o, i = jnp.where(is_odd, L - 1, 0), jnp.where(is_odd, L - 2, 1)
    planes[0:R, :] = h[o]
    planes[R : 2 * R, :] = p[o]
    planes[2 * R : 3 * R, :] = h[i]
    planes[3 * R : 4 * R, :] = p[i]
    both[...] = total


def pack_y_kernel(slab, edges, own_lo, own_hi, lo, hi):
    is_odd = (slab[0] & 1) == 1
    for ref, own, cols in ((lo, own_lo, slice(0, 128)), (hi, own_hi, slice(128, 256))):
        b = edges[0:GR, cols]
        ref[...] = own[...] + jnp.where(is_odd, roll(b, 4 * (L + 1), 1), b)


def pack_x_kernel(slab, h, p, first, edges, ylo, yhi, lo, hi):
    is_odd = (slab[0] & 1) == 1
    for s, (ref, o, i, yrow) in enumerate(((lo, 0, 1, 0), (hi, R - 1, R - 2, GR - 1))):
        for arr, own in ((0, h), (1, p)):
            at = R * arr + o
            k = GR + 2 * s + arr
            a, b = first[at : at + 1, :], edges[k : k + 1, :]
            top = 10 * arr
            ref[top : top + 1, :] = jnp.where(is_odd, a, b)
            for z in range(L):
                ref[top + 1 + z : top + 2 + z, :] = own[z, o : o + 1, :]
                ref[20 + L * arr + z : 21 + L * arr + z, :] = own[z, i : i + 1, :]
            ref[top + 9 : top + 10, :] = jnp.where(is_odd, b, a)
        ref[36:37, 0:128] = ylo[yrow : yrow + 1, :]
        ref[36:37, 128:256] = yhi[yrow : yrow + 1, :]
        ref[37:40, :] = jnp.zeros((3, C), F32)


def sums(h, p, beside):
    total, flow = None, None
    for hn, pn in beside:
        t = recip(h + hn)
        total = 1.0 + t if total is None else total + t
        flow = t * (pn - p) if flow is None else flow + t * (pn - p)
    return total, flow


def beside_y(msgs, owns):
    lane = iota((GR, 128), 1)
    sub = iota((GR, 128), 0)
    result = []
    for msg, own, o, i, w in ((msgs[0], owns[0], 1, 0, 0), (msgs[1], owns[1], 0, 1, 1)):
        m, v = msg[...], own[...]
        ho, po = present(roll(m, -o, 1)), roll(m, -o - 2, 1)
        hi_, pi_ = present(roll(m, -i, 1)), roll(m, -i - 2, 1)
        hw, pw = present(roll(v, -w, 1)), roll(v, -w - 2, 1)

        def along_x(f):
            u = roll(f, 1, 0)
            u = jnp.where(sub == 0, roll(u, 40, 1), u)
            d = roll(f, -1, 0)
            d = jnp.where(sub == GR - 1, roll(d, -40, 1), d)
            return u, d

        hu, hd = along_x(ho)
        pu, pd = along_x(po)
        hu = jnp.where((sub == 0) & (lane < 40), ABSENT, hu)
        hd = jnp.where((sub == GR - 1) & (lane >= 80), ABSENT, hd)
        total, flow = sums(ho, po, (
            (hi_, pi_), (hw, pw), (hu, pu), (hd, pd),
            (roll(ho, 4, 1), roll(po, 4, 1)), (roll(ho, -4, 1), roll(po, -4, 1)),
        ))
        result.append((ho, po, total, flow))
    return result


def beside_y_corners(msgs, yst):
    lane = iota((GR, 128), 1)
    sub = iota((GR, 128), 0)
    at_low = (sub == 0) & (lane < 40)
    at_high = (sub == GR - 1) & (lane >= 80)
    result = []
    for s, o, cols in ((0, 1, slice(0, 128)), (1, 0, slice(128, 256))):
        ho, po, total, flow = (yst[s, k] for k in range(4))

        def corner(k):
            low = jnp.broadcast_to(msgs[0][36:37, cols], (GR, 128))
            high = jnp.broadcast_to(msgs[1][36:37, cols], (GR, 128))
            return jnp.where(sub == 0, roll(low, -80 - k, 1), roll(high, 80 - k, 1))

        t = jnp.where(at_low | at_high, recip(ho + present(corner(o))), 0.0)
        result.append(po + (flow + t * (corner(o + 2) - po)) * recip(total + t))
    return result


def beside_x(msgs, owns, xh, xp, xq):
    lane = iota((16, C), 1)
    lane_x = iota((16, 128), 1)
    sub_x = iota((16, 128), 0)
    for s, row_lane in ((0, 80), (1, 0)):
        msg, own = msgs[s], owns[s]

        def rows10(ref, at):
            return jnp.concatenate([ref[at : at + 10, :], jnp.zeros((6, C), F32)], axis=0)

        def rows8(ref, at):
            return jnp.concatenate([jnp.zeros((1, C), F32), ref[at : at + 8, :], jnp.zeros((7, C), F32)], axis=0)

        ho, po = present(rows10(msg, 0)), rows10(msg, 10)
        hi_, pi_ = present(rows8(msg, 20)), rows8(msg, 28)
        hw, pw = present(rows10(own, 0)), rows10(own, 10)

        def corner(cols, k):
            row = jnp.broadcast_to(msg[36:37, cols], (16, 128))
            return jnp.sum(jnp.where(lane_x == row_lane + 4 * sub_x + k, row, 0.0), axis=1, keepdims=True)

        left, right = slice(0, 128), slice(128, 256)
        hl = jnp.where(lane == 0, present(corner(left, 1)), roll(ho, 1, 1))
        pl_ = jnp.where(lane == 0, corner(left, 3), roll(po, 1, 1))
        hr = jnp.where(lane == C - 1, present(corner(right, 0)), roll(ho, -1, 1))
        pr = jnp.where(lane == C - 1, corner(right, 2), roll(po, -1, 1))
        xh[s] = ho
        xp[s] = po
        total, flow = sums(ho, po, (
            (hi_, pi_), (hw, pw), (hl, pl_), (hr, pr),
            (roll(ho, 1, 0), roll(po, 1, 0)), (roll(ho, -1, 0), roll(po, -1, 0)),
        ))
        xq[s] = po + flow * recip(total)


def both_edges(lo, hi):
    lane = iota((GR, 128), 1)
    return jnp.where((lane & 3) == 0, lo, roll(hi, -1, 1))


def edge_columns(both, z, g):
    return roll(both, -40 * g - 4 * (z + 1), 1)


def around_x(before, here, after):
    sub = iota((8, C), 0)
    return roll(jnp.where(sub == 7, before, here), 1, 0), roll(jnp.where(sub == 0, after, here), -1, 0)


def around_y(here, edge):
    lane = iota((8, 128), 1)
    a, b = here[:, :128], here[:, 128:]
    ra, rb = roll(a, 1, 1), roll(b, 1, 1)
    left = jnp.concatenate([jnp.where(lane == 0, edge, ra), jnp.where(lane == 0, ra, rb)], axis=1)
    ra, rb = roll(a, -1, 1), roll(b, -1, 1)
    right = jnp.concatenate([jnp.where(lane == 127, rb, ra), jnp.where(lane == 127, edge, rb)], axis=1)
    return left, right


def second_chunk(qval, qedge, weight, pval, base, over, lith, shade, put):
    low = qval(-1)[1]
    qc = qval(0)
    flow = weight(0, 4) * (qc[1] - low)
    for z in range(L):
        qn = qval(z + 1)
        flow2 = weight(z + 1, 4) * (qn[1] - qc[1])
        q = qc[1]
        change = flow2 - flow
        for k, qb in enumerate(around_x(*qc) + around_y(q, qedge(z))):
            change = change + weight(z, k) * (qb - q)
        d0 = q - pval(z)
        pn = q + RHO_SECOND * RHO_FIRST * d0 + (2.0 * RHO_SECOND / SPECTRUM_HALF) * (change - d0) * weight(z, 5)
        stress = jnp.maximum(base + over(z) - pn, 0.0)
        odd, upper = classes(lith(z))
        new = pick(odd, upper, PHI_SURFACE) * jnp.exp(-pick(odd, upper, ATHY_RATE) * stress)
        put(z, pn, new, jnp.broadcast_to(shade[z : z + 1, :], (8, C)) * recip(1.0 - new))
        qc, flow = qn, flow2


def above_rows(slab, first, both, rows):
    base = jnp.where((slab[0] & 1) == 1, first[rows(4 * R), :], 0.0)
    return base + jnp.where(slab[0] >= 2, both[rows(0), :], 0.0)


def at8(i):
    return pl.ds(pl.multiple_of(8 * i, 8), 8)


LAST = R // 8 - 1


def triples(h, p, hz, pz, i):
    here = (at8(jnp.maximum(i - 1, 0)), at8(i), at8(jnp.minimum(i + 1, LAST)))

    def at(z):
        return (h, p, z) if 0 <= z < L else (hz, pz, {-1: 0, L: 1, -2: 2, L + 1: 3}[z])

    def hval(z):
        ref, _, k = at(z)
        a, b, c = (ref[k, rows, :] for rows in here)
        return jnp.where(i == 0, ABSENT, a), b, jnp.where(i == LAST, ABSENT, c)

    def pval(z):
        _, ref, k = at(z)
        return tuple(ref[k, rows, :] for rows in here)

    return hval, pval


def pre_kernel(h, p, wlo, w):
    def chunk(i, carry):
        rows = at8(i)
        hval, pval = triples(h, p, None, None, i)
        hc, pc = hval(0), pval(0)
        t, flow = None, None
        later = Later(4)
        for z in range(L):
            stores = []
            total, change = 1.0, 0.0
            if z > 0:
                total, change = total + t, change - flow
            if z < L - 1:
                hn, pn = hval(z + 1), pval(z + 1)
                t = recip(hc[1] + hn[1])
                flow = t * (pn[1] - pc[1])
                stores.append((w, (2, z + 1, rows), t))
                total, change = total + t, change + flow
            for k, (hb, pb) in enumerate(zip(around_x(*hc), around_x(*pc))):
                u = recip(hc[1] + hb)
                stores.append((w, (k, z, rows), u))
                total = total + u
                change = change + u * (pb - pc[1])
            later.put(*stores, (w, (3, z, rows), total), (w, (4, z, rows), change))
            hc, pc = hn, pn
        later.flush()
        return carry

    lax.fori_loop(0, R // 8, chunk, 0, unroll=True)


def weight_of(w, wy, wz, z, k, rows):
    if k == 4 and z in (0, L):
        return wz[z // L, rows, :]
    return (w, w, wy, wy, w)[k][(0, 1, 0, 1, 2)[k], z, rows, :]


def inner_kernel(
    slab, shade, h, p, over, lith, first, planes, both, w, ylo, yhi, wlo, whi,
    yst, wy, wz, p1, iv, hz, pz, out0, out1, out2,
    eh, ep, eq, o0, o1, o2, sems,
):
    is_odd = (slab[0] & 1) == 1
    for k in range(2):
        for ref, at, fix in ((hz, 2 * k * R, present), (pz, (2 * k + 1) * R, lambda t: t)):
            a, b = first[at : at + R, :], planes[at : at + R, :]
            ref[2 * k] = fix(jnp.where(is_odd, a, b))
            ref[2 * k + 1] = fix(jnp.where(is_odd, b, a))
    lo, hi = beside_y((ylo, yhi), (wlo, whi))
    for s, values in enumerate((lo, hi)):
        for k in range(4):
            yst[s, k] = values[k]
    qlo, qhi = (v[1] + v[3] * recip(v[2]) for v in (lo, hi))
    hb, pb, qb = both_edges(lo[0], hi[0]), both_edges(lo[1], hi[1]), both_edges(qlo, qhi)
    for z in range(-1, L + 1):
        for g in range(3):
            rows = slice(GR * g, GR * g + GR)
            eh[z + 1, rows, :] = edge_columns(hb, z, g)
            ep[z + 1, rows, :] = edge_columns(pb, z, g)
            if 0 <= z < L:
                eq[z, rows, :] = edge_columns(qb, z, g)

    def chunk1(i, carry):
        rows = at8(i)
        hval, pval = triples(h, p, hz, pz, i)

        later = Later(4)

        def finish(z, hc, pc, total, change):
            stores = []
            for k, (hb, pb) in enumerate(zip(around_y(hc, eh[z + 1, rows, :]), around_y(pc, ep[z + 1, rows, :]))):
                u = recip(hc + hb)
                if 0 <= z < L:
                    stores.append((wy, (k, z, rows), u))
                total = total + u
                change = change + u * (pb - pc)
            inv = recip(total)
            later.put(*stores, (iv, (z + 1, rows), inv), (p1, (z + 1, rows), pc + change * inv))

        for z, out, own in ((-1, -2, 0), (L, L + 1, L - 1)):
            hc, pc = hval(z), pval(z)
            beside = [(hval(out)[1], pval(out)[1]), (hval(own)[1], pval(own)[1])]
            beside += list(zip(around_x(*hc), around_x(*pc)))
            finish(z, hc[1], pc[1], *sums(hc[1], pc[1], beside))
        for z in range(L):
            hc, pc, total, change = h[z, rows, :], p[z, rows, :], w[3, z, rows, :], w[4, z, rows, :]
            for k in ((0,) if z == 0 else (1,) if z == L - 1 else ()):
                t = recip(hc + hz[k, rows, :])
                later.kept.append((wz, (k, rows), t))
                total = total + t
                change = change + t * (pz[k, rows, :] - pc)
            finish(z, hc, pc, total, change)
        later.flush()
        return carry

    lax.fori_loop(0, R // 8, chunk1, 0, unroll=True)

    def moved(i):
        return [
            pltpu.make_async_copy(src.at[:, at8(i), :], dst.at[:, at8(i), :], sems.at[k, i])
            for k, (src, dst) in enumerate(((o0, out0), (o1, out1), (o2, out2)))
        ]

    def chunk2(i, carry):
        rows = at8(i)
        here = (at8(i - 1), rows, at8(i + 1))

        later = Later(4)

        def put(z, a, b, c):
            later.put((o0, (z, rows), a), (o1, (z, rows), b), (o2, (z, rows), c))

        second_chunk(
            lambda z: tuple(p1[z + 1, r, :] for r in here),
            lambda z: eq[z, rows, :],
            lambda z, k: iv[z + 1, rows, :] if k == 5 else weight_of(w, wy, wz, z, k, rows),
            lambda z: p[z, rows, :],
            above_rows(slab, first, both, lambda top: pl.ds(pl.multiple_of(top + 8 * i, 8), 8)),
            lambda z: over[z, rows, :],
            lambda z: lith[z, rows, :],
            shade, put,
        )
        later.flush()
        for copy in moved(i):
            copy.start()
        return carry

    lax.fori_loop(1, LAST, chunk2, 0, unroll=True)

    def arrive(i, carry):
        for copy in moved(i):
            copy.wait()
        return carry

    lax.fori_loop(1, LAST, arrive, 0)


def outer_kernel(
    slab, shade, h, p, over, lith, first, planes, both, xlo, xhi, vlo, vhi,
    w, yst, wy, wz, p1, iv, hz, pz, in0, in1, in2,
    out0, out1, out2,
    xh, xp, xq, q1, wt, o0, o1, o2, sems,
):
    beside_x((xlo, xhi), (vlo, vhi), xh, xp, xq)
    columns = both_edges(*beside_y_corners((xlo, xhi), yst))
    sub = iota((8, C), 0)
    copies = []
    for s, top, g, part in ((0, 0, 0, slice(0, 8)), (1, R - 8, 2, slice(GR - 8, GR))):
        rows = slice(top, top + 8)
        near = slice(8, 16) if s == 0 else slice(R - 16, R - 8)
        edge = sub == (0 if s == 0 else 7)

        def strip(ref, z, s=s):
            return jnp.broadcast_to(ref[s, z + 1 : z + 2, :], (8, C))

        later = Later(5)
        for z in range(-1, L + 1):
            if 0 <= z < L:
                hc, pc = h[z, rows, :], p[z, rows, :]
            else:
                k = 0 if z < 0 else 1
                hc, pc = hz[k, rows, :], pz[k, rows, :]
            total = recip(iv[z + 1, rows, :])
            change = (p1[z + 1, rows, :] - pc) * total
            t = jnp.where(edge, recip(hc + strip(xh, z)), 0.0)
            inv = recip(total + t)
            stores = [(q1, (s, z + 1), pc + (change + t * (strip(xp, z) - pc)) * inv)]
            if 0 <= z < L:
                stores += [(wt, (s, 0, z), w[s, z, rows, :] + t), (wt, (s, 1, z), inv)]
            later.put(*stores)
        later.flush()

        def q_triple(z, s=s, near=near):
            here = q1[s, z + 1]
            if z < 0 or z >= L:
                return here, here, here
            inside = p1[z + 1, near, :]
            return (strip(xq, z), here, inside) if s == 0 else (inside, here, strip(xq, z))

        def weight(z, k, s=s, rows=rows):
            if k == s:
                return wt[s, 0, z]
            if k == 5:
                return wt[s, 1, z]
            return weight_of(w, wy, wz, z, k, rows)

        later = Later(4)

        def put(z, a, b, c, s=s, later=later):
            later.put((o0, (s, z), a), (o1, (s, z), b), (o2, (s, z), c))

        second_chunk(
            q_triple,
            lambda z: edge_columns(columns[part], z, g),
            weight,
            lambda z: p[z, rows, :],
            above_rows(slab, first, both, lambda t: slice(t + top, t + top + 8)),
            lambda z: over[z, rows, :],
            lambda z: lith[z, rows, :],
            shade, put,
        )
        for k, (src, dst) in enumerate(((o0, out0), (o1, out1), (o2, out2))):
            copy = pltpu.make_async_copy(src.at[s], dst.at[:, rows, :], sems.at[s, k])
            copy.start()
            copies.append(copy)
    for copy in copies:
        copy.wait()


SMEM, VMEM, HBM = pltpu.SMEM, pltpu.VMEM, pltpu.HBM


COSTS = {
    "pre": pl.CostEstimate(flops=10**8, transcendentals=0, bytes_accessed=10**8),
    "pack_x": pl.CostEstimate(flops=10**10, transcendentals=0, bytes_accessed=10**10),
    "inner": pl.CostEstimate(flops=10**10, transcendentals=0, bytes_accessed=10**10),
}


def call(kernel, name, ins, outs, scratch=(), aliases=None):
    return pl.pallas_call(
        kernel,
        out_shape=[jax.ShapeDtypeStruct(s, t) for s, t, _ in outs],
        in_specs=[pl.BlockSpec(memory_space=m) for m in ins],
        out_specs=[pl.BlockSpec(memory_space=m) for _, _, m in outs],
        scratch_shapes=list(scratch),
        input_output_aliases=aliases or {},
        compiler_params=pltpu.CompilerParams(vmem_limit_bytes=VMEM_LIMIT),
        name=name,
        cost_estimate=COSTS.get(name),
    )


def pair(axis, lo, hi):
    n = lax.axis_size(axis)
    up = [(i, i + 1) for i in range(n - 1)]
    down = [(j, i) for i, j in up]
    return lax.ppermute(hi, axis, up), lax.ppermute(lo, axis, down)


def vm(*shape):
    return (shape, F32, VMEM)


def body(p_in, poro, lith_in, solid):
    p_in, poro, lith_in, solid = (
        pltpu.with_memory_space_constraint(a, HBM) for a in (p_in, poro, lith_in, solid)
    )
    slab = lax.axis_index("slab").astype(jnp.int32).reshape(1)
    block = (L, R, C)
    dma = pltpu.SemaphoreType.DMA
    p, lith, h, over, first, edges, shade = call(
        start_kernel, "start", [SMEM] + [HBM] * 4,
        [vm(*block), (block, jnp.int32, VMEM), vm(*block), vm(*block), vm(5 * R, C), vm(GR + 8, C), vm(L, C)],
        [VMEM(block, F32), SMEM((L,), F32), dma((3, STEPS)), dma(())],
    )(slab, p_in, poro, lith_in, solid)
    edges_in = lax.ppermute(edges, "slab", [(1, 2), (2, 1)])
    first_in = lax.ppermute(first, "slab", [(0, 1), (1, 0), (2, 3), (3, 2)])
    planes, both, *own_y = call(
        pack_own_kernel, "pack_own", [SMEM] + [VMEM] * 4,
        [vm(4 * R, C), vm(R, C), vm(GR, 128), vm(GR, 128)],
    )(slab, h, p, first, first_in)
    planes, both, edges_in = lax.optimization_barrier((planes, both, edges_in))
    planes_in = lax.ppermute(planes, "slab", [(1, 2), (2, 1)])
    both_in = lax.ppermute(both, "slab", [(1, 2), (0, 3)])
    wlo, whi = call(pack_y_kernel, "pack_y", [SMEM] + [VMEM] * 3, [vm(GR, 128)] * 2)(slab, edges_in, *own_y)
    ylo, yhi = pair("mapy", wlo, whi)
    (w,) = call(pre_kernel, "pre", [VMEM] * 3, [vm(5, L + 1, R, C)])(h, p, wlo)
    ylo, yhi, w = lax.optimization_barrier((ylo, yhi, w))
    vlo, vhi = call(pack_x_kernel, "pack_x", [SMEM] + [VMEM] * 6, [vm(40, C)] * 2)(
        slab, h, p, first_in, edges_in, ylo, yhi
    )
    xlo, xhi = pair("mapx", vlo, vhi)
    hbm = (block, F32, HBM)
    columns = VMEM((L + 2, R, 128), F32)
    yst, wy, wz, p1, iv, hz, pz, *outs = call(
        inner_kernel, "inner", [SMEM] + [VMEM] * 13,
        [vm(2, 4, GR, 128), vm(2, L, R, C), vm(2, R, C)] + [vm(L + 2, R, C)] * 2 + [vm(4, R, C)] * 2 + [hbm] * 3,
        [columns, columns, VMEM((L, R, 128), F32)] + [VMEM(block, F32)] * 3 + [dma((3, R // 8))],
    )(slab, shade, h, p, over, lith, first_in, planes_in, both_in, w, ylo, yhi, wlo, whi)
    return tuple(
        call(
            outer_kernel, "outer", [SMEM] + [VMEM] * 20 + [HBM] * 3, [hbm] * 3,
            [VMEM((2, 16, C), F32)] * 3
            + [VMEM((2, L + 2, 8, C), F32), VMEM((2, 2, L, 8, C), F32)]
            + [VMEM((2, L, 8, C), F32)] * 3 + [dma((2, 3))],
            {21: 0, 22: 1, 23: 2},
        )(
            slab, shade, h, p, over, lith, first_in, planes_in, both_in, xlo, xhi, vlo, vhi,
            w, yst, wy, wz, p1, iv, hz, pz, *outs,
        )
    )


def solution(mesh):
    spec = P("slab", "mapx", "mapy")
    return jax.shard_map(
        body, mesh=mesh, in_specs=(spec, spec, spec, P("slab")), out_specs=(spec,) * 3, check_vma=False
    )
```
